32 devices in a mesh: seq: 2 (over x), fsdp: 16 (over z, y, core).
Axes of the slice: x: 2, y: 2, z: 4, core: 2. Of those that a mesh axis runs over, the one named last changes fastest.
Arguments:
- tokens: bfloat16 [16, 384, 2048], P('fsdp', 'seq'), may hold values from -6 to 6
- cotangent: bfloat16 [16, 384, 2048], P('fsdp', 'seq'), may hold values from -6 to 6
- mixer_gain: bfloat16 [2048], P('fsdp'), may hold values from 0.099609375 to 1.8984375
- query_weight: bfloat16 [2048, 1024], P('fsdp'), may hold values from -0.125 to 0.125
- key_weight: bfloat16 [2048, 256], P('fsdp'), may hold values from -0.125 to 0.125
- value_weight: bfloat16 [2048, 256], P('fsdp'), may hold values from -0.125 to 0.125
- attn_out_weight: bfloat16 [1024, 2048], P('fsdp'), may hold values from -0.75 to 0.75
- mamba_in_weight: bfloat16 [2048, 6704], P('fsdp'), may hold values from -0.125 to 0.125
- conv_weight: bfloat16 [4, 3584], P(None, 'fsdp'), may hold values from -3 to 3
- conv_bias: bfloat16 [3584], P('fsdp'), may hold values from -3 to 3
- decay_log: bfloat16 [48], replicated, may hold values from -4.59375 to -0.69921875
- step_bias: bfloat16 [48], replicated, may hold values from -4 to -1
- skip_gain: bfloat16 [48], replicated, may hold values from 0.5 to 1.5
- mamba_gain: bfloat16 [3072], P('fsdp'), may hold values from 0.099609375 to 1.8984375
- mamba_out_weight: bfloat16 [3072, 2048], P('fsdp'), may hold values from -0.109375 to 0.109375
- ffn_gain: bfloat16 [2048], P('fsdp'), may hold values from 0.099609375 to 1.8984375
- gate_weight: bfloat16 [2048, 4096], P('fsdp'), may hold values from -0.125 to 0.125
- up_weight: bfloat16 [2048, 4096], P('fsdp'), may hold values from -0.125 to 0.125
- down_weight: bfloat16 [4096, 2048], P('fsdp'), may hold values from -0.09375 to 0.09375
Outputs:
- output: bfloat16 [16, 384, 2048], P('fsdp', 'seq')
- tokens_grad: float32 [16, 384, 2048], P('fsdp', 'seq')
- mixer_gain_grad: float32 [2048], P('fsdp')
- query_grad: float32 [2048, 1024], P('fsdp')
- key_grad: float32 [2048, 256], P('fsdp')
- value_grad: float32 [2048, 256], P('fsdp')
- attn_out_grad: float32 [1024, 2048], P('fsdp')
- mamba_in_grad: float32 [2048, 6704], P('fsdp')
- conv_weight_grad: float32 [4, 3584], P(None, 'fsdp')
- conv_bias_grad: float32 [3584], P('fsdp')
- decay_log_grad: float32 [48], replicated
- step_bias_grad: float32 [48], replicated
- skip_gain_grad: float32 [48], replicated
- mamba_gain_grad: float32 [3072], P('fsdp')
- mamba_out_grad: float32 [3072, 2048], P('fsdp')
- ffn_gain_grad: float32 [2048], P('fsdp')
- gate_grad: float32 [2048, 4096], P('fsdp')
- up_grad: float32 [2048, 4096], P('fsdp')
- down_grad: float32 [4096, 2048], P('fsdp')
The draws below stay inside these ranges and needn't reach their ends.
All inputs are finite; a program needn't handle non-finite values.
Results may differ from the reference program's by a relative error of at most 0.018.
Values may be sent and summed in bfloat16 or wider, within the bound.
A program may use at most 448 MiB of HBM per device.

```python
import math
import jax
import jax.numpy as jnp
from jax import lax

D = 2048
HQ = 8
KVH = 2
HD = 128
MH = 48
MP = 64
NST = 256
KCONV = 4
FF = 4096
SPAN = 128
LENGTH = 384
SEQS = 16
PROJ = 6704
CONVDIM = 3584


def shard_levels(stream_key, shape, shards, smallest, high):
    loudness, own = 1.0, jax.random.fold_in(stream_key, 6)
    for dim, shards_of in shards:
        steps = jnp.exp(jax.random.uniform(jax.random.fold_in(own, dim), (shards_of,), jnp.float32, smallest / len(shards), high / len(shards)))
        loudness = loudness * jnp.repeat(steps, shape[dim] // shards_of).reshape([-1 if axis == dim else 1 for axis in range(len(shape))])
    return loudness


def bell_draw(rng, dims, width, reach, cuts=(), kind=jnp.bfloat16):
    drawn = jax.random.normal(rng, dims, jnp.float32) * width
    if len(cuts) > 0:
        drawn = shard_levels(rng, dims, cuts, -0.22, 0.18) * drawn
    return jnp.clip(drawn, min=-reach, max=reach).astype(kind)


def setup_inputs(seed: int = 0) -> dict:
    key_of = jax.random.split(jax.random.key(seed), 20)
    tokens = bell_draw(key_of[0], (SEQS, LENGTH, D), 1.0, 6.0, ((0, 16), (1, 2)))
    cotangent = bell_draw(key_of[1], (SEQS, LENGTH, D), 1.0, 6.0, ((0, 16), (1, 2)))
    mixer_gain = jnp.clip(1.0 + 0.18 * jax.random.normal(key_of[2], (D,), jnp.float32), 0.099609375, 1.8984375).astype(jnp.bfloat16)
    query_weight = bell_draw(key_of[3], (D, HQ * HD), D ** -0.5, 0.125, ((0, 16),))
    key_weight = bell_draw(key_of[4], (D, KVH * HD), D ** -0.5, 0.125, ((0, 16),))
    value_weight = bell_draw(key_of[5], (D, KVH * HD), D ** -0.5, 0.125, ((0, 16),))
    attn_out_weight = bell_draw(key_of[6], (HQ * HD, D), (HQ * HD // 16) ** -0.5, 0.75, ((0, 16),))
    mamba_in_weight = bell_draw(key_of[7], (D, PROJ), D ** -0.5, 0.125, ((0, 16),))
    conv_weight = bell_draw(key_of[8], (KCONV, CONVDIM), KCONV ** -0.5, 3.0, ((1, 16),))
    conv_bias = bell_draw(key_of[9], (CONVDIM,), 0.5, 3.0, ((0, 16),))
    decay_log = jnp.clip(jax.random.uniform(key_of[10], (MH,), jnp.float32, -4.59375, -0.69921875), -4.59375, -0.69921875).astype(jnp.bfloat16)
    step_bias = jnp.clip(jax.random.uniform(key_of[11], (MH,), jnp.float32, -4.0, -1.0), -4.0, -1.0).astype(jnp.bfloat16)
    skip_gain = jnp.clip(jax.random.uniform(key_of[12], (MH,), jnp.float32, 0.5, 1.5), 0.5, 1.5).astype(jnp.bfloat16)
    mamba_gain = jnp.clip(1.0 + 0.18 * jax.random.normal(key_of[13], (MH * MP,), jnp.float32), 0.099609375, 1.8984375).astype(jnp.bfloat16)
    mamba_out_weight = bell_draw(key_of[14], (MH * MP, D), (MH * MP) ** -0.5, 0.109375, ((0, 16),))
    ffn_gain = jnp.clip(1.0 + 0.18 * jax.random.normal(key_of[15], (D,), jnp.float32), 0.099609375, 1.8984375).astype(jnp.bfloat16)
    gate_weight = bell_draw(key_of[16], (D, FF), D ** -0.5, 0.125, ((0, 16),))
    up_weight = bell_draw(key_of[17], (D, FF), D ** -0.5, 0.125, ((0, 16),))
    down_weight = bell_draw(key_of[18], (FF, D), FF ** -0.5, 0.09375, ((0, 16),))
    return {"tokens": tokens, "cotangent": cotangent, "mixer_gain": mixer_gain, "query_weight": query_weight, "key_weight": key_weight, "value_weight": value_weight, "attn_out_weight": attn_out_weight, "mamba_in_weight": mamba_in_weight, "conv_weight": conv_weight, "conv_bias": conv_bias, "decay_log": decay_log, "step_bias": step_bias, "skip_gain": skip_gain, "mamba_gain": mamba_gain, "mamba_out_weight": mamba_out_weight, "ffn_gain": ffn_gain, "gate_weight": gate_weight, "up_weight": up_weight, "down_weight": down_weight}


EPSILON = 1e-05
ROPE_BASE = 100000000000.0
MASKED = -1e+30
PRECISE = lax.Precision.HIGHEST

@jax.custom_vjp
def low(v):
    return lax.optimization_barrier(v.astype(jnp.bfloat16)).astype(jnp.float32)

@jax.custom_vjp
def low_back(v):
    return v

def low_keep(v):
    return (low(v), None)

def low_pass(kept, grad):
    return (grad,)

def back_keep(v):
    return (v, None)

def back_low(kept, grad):
    return (low(grad),)
low.defvjp(low_keep, low_pass)
low_back.defvjp(back_keep, back_low)

def rms_norm(values, scaling):
    factor = lax.rsqrt(lax.optimization_barrier(jnp.mean(values * values, axis=-1, keepdims=True)) + EPSILON)
    return values * factor * scaling

def project(left, right):
    return jnp.einsum('...i,ij->...j', left, right, precision=PRECISE)

def causal_conv(signal, kernel):
    length = signal.shape[0]
    tap_count = kernel.shape[0]
    padded = jnp.pad(signal, ((tap_count - 1, 0), (0, 0)))
    summed = padded[0:length] * kernel[0]
    for offset in range(1, tap_count):
        summed = summed + padded[offset:offset + length] * kernel[offset]
    return summed

def rope_tables(length, head_size):
    half_size = head_size // 2
    frequency = jnp.exp(jnp.arange(half_size, dtype=jnp.float32) * (-2.0 * math.log(ROPE_BASE) / head_size))
    angles = jnp.arange(length, dtype=jnp.float32)[:, None] * frequency[None, :]
    return (jnp.cos(angles)[:, None, :], jnp.sin(angles)[:, None, :])

def rotate(values, cosine, sine_table):
    half_size = values.shape[-1] // 2
    front_half = values[..., :half_size]
    back_half = values[..., half_size:]
    return jnp.concatenate([front_half * cosine - back_half * sine_table, back_half * cosine + front_half * sine_table], axis=-1)

def scan_states(inputs, step_sizes, decay_rates, input_map, output_map):
    length, head_count, head_width = inputs.shape
    state_size = input_map.shape[1]
    number = length // SPAN
    blocks = (inputs.reshape(number, SPAN, head_count, head_width), step_sizes.reshape(number, SPAN, head_count), input_map.reshape(number, SPAN, state_size), output_map.reshape(number, SPAN, state_size))
    causal = jnp.arange(SPAN)[:, None] >= jnp.arange(SPAN)[None, :]

    def advance(state_now, pieces):
        block_x, block_dt, block_b, block_c = pieces
        cumulated = jnp.cumsum(block_dt * decay_rates, axis=0)
        log_gaps = jnp.where(causal[:, :, None], cumulated[:, None, :] - cumulated[None, :, :], MASKED)
        coupling = jnp.dot(block_c, block_b.T, precision=PRECISE)
        weights = coupling[:, :, None] * jnp.exp(log_gaps) * block_dt[None, :, :]
        within = jnp.einsum('tsh,shp->thp', weights, block_x, precision=PRECISE)
        carried = jnp.einsum('tn,hpn->thp', block_c, state_now, precision=PRECISE) * jnp.exp(cumulated)[:, :, None]
        ending = cumulated[-1]
        fading = jnp.exp(ending[None, :] - cumulated) * block_dt
        state_now = state_now * jnp.exp(ending)[:, None, None] + jnp.einsum('sh,shp,sn->hpn', fading, block_x, block_b, precision=PRECISE)
        return (state_now, within + carried)
    initial = jnp.zeros((head_count, head_width, state_size), jnp.float32)
    ignored, outputs = lax.scan(jax.checkpoint(advance), initial, blocks)
    return outputs.reshape(length, head_count, head_width)

def mamba_core(seq_inputs, step_raw, map_inputs, x_kernel, x_bias, map_kernel, map_bias, decay_log, step_bias, skip_gain):
    length = seq_inputs.shape[0]
    head_count = step_raw.shape[1]
    head_width = seq_inputs.shape[1] // head_count
    state_size = map_inputs.shape[1] // 2
    convolved = jax.nn.silu(causal_conv(seq_inputs, x_kernel) + x_bias).reshape(length, head_count, head_width)
    map_values = jax.nn.silu(causal_conv(map_inputs, map_kernel) + map_bias)
    step_sizes = jax.nn.softplus(step_raw + step_bias)
    decay_rates = -jnp.exp(decay_log)
    outputs = scan_states(convolved, step_sizes, decay_rates, map_values[:, :state_size], map_values[:, state_size:])
    outputs = outputs + skip_gain[:, None] * convolved
    return outputs.reshape(length, head_count * head_width)

def attention_seq(queries, key_proj, value_proj):
    length = queries.shape[0]
    cosine, sine_table = rope_tables(length, HD)
    rotated_query = low(rotate(queries.reshape(length, HQ, HD), cosine, sine_table))
    rotated_keys = low(rotate(key_proj.reshape(length, KVH, HD), cosine, sine_table))
    shared_values = value_proj.reshape(length, KVH, HD)
    repeat_count = HQ // KVH
    full_keys = jnp.repeat(rotated_keys, repeat_count, axis=1)
    full_values = jnp.repeat(shared_values, repeat_count, axis=1)
    scores = low_back(jnp.einsum('qhd,khd->hqk', rotated_query, full_keys, precision=PRECISE) * HD ** (-0.5))
    causal = jnp.arange(length)[:, None] >= jnp.arange(length)[None, :]
    scores = jnp.where(causal[None], scores, MASKED)
    highest = lax.optimization_barrier(jnp.max(scores, axis=-1, keepdims=True))
    weights = jnp.exp(scores - highest)
    normalized = weights / lax.optimization_barrier(jnp.sum(weights, axis=-1, keepdims=True))
    attended = jnp.einsum('hqk,khd->qhd', low(normalized), full_values, precision=PRECISE)
    return attended.reshape(length, HQ * HD)

def block_layer(tokens, mixer_gain, query_weight, key_weight, value_weight, attn_out_weight, mamba_in_weight, conv_weight, conv_bias, decay_log, step_bias, skip_gain, mamba_gain, mamba_out_weight, ffn_gain, gate_weight, up_weight, down_weight):
    inner_width = MH * MP
    hidden = low(rms_norm(tokens, mixer_gain))
    queries = low_back(low(project(hidden, query_weight)))
    key_proj = low_back(low(project(hidden, key_weight)))
    value_proj = low_back(low(project(hidden, value_weight)))
    projected = low_back(project(hidden, mamba_in_weight))
    gate_branch = projected[..., :inner_width]
    seq_inputs = low_back(low(projected[..., inner_width:2 * inner_width]))
    map_inputs = low(projected[..., 2 * inner_width:2 * inner_width + 2 * NST])
    step_raw = low_back(low(projected[..., 2 * inner_width + 2 * NST:]))
    attended = low_back(low(jax.vmap(attention_seq)(queries, key_proj, value_proj)))
    scanned = jax.vmap(mamba_core, in_axes=(0, 0, 0, None, None, None, None, None, None, None))(seq_inputs, step_raw, map_inputs, conv_weight[:, :inner_width], conv_bias[:inner_width], conv_weight[:, inner_width:], conv_bias[inner_width:], decay_log, step_bias, skip_gain)
    scanned = low_back(low(scanned))
    gated_values = scanned * jax.nn.silu(gate_branch)
    normed = low(rms_norm(gated_values, mamba_gain))
    mixer_sum = low_back(project(attended, attn_out_weight) + project(normed, mamba_out_weight))
    middle = tokens + mixer_sum
    second = low(rms_norm(middle, ffn_gain))
    gate = low_back(project(second, gate_weight))
    upward = low_back(project(second, up_weight))
    active = low(jax.nn.silu(gate) * upward)
    return middle + low_back(project(active, down_weight))

def reference(tokens, cotangent, mixer_gain, query_weight, key_weight, value_weight, attn_out_weight, mamba_in_weight, conv_weight, conv_bias, decay_log, step_bias, skip_gain, mamba_gain, mamba_out_weight, ffn_gain, gate_weight, up_weight, down_weight):
    parameters = tuple((parameter.astype(jnp.float32) for parameter in (mixer_gain, query_weight, key_weight, value_weight, attn_out_weight, mamba_in_weight, conv_weight, conv_bias, decay_log, step_bias, skip_gain, mamba_gain, mamba_out_weight, ffn_gain, gate_weight, up_weight, down_weight)))
    group_size = 4 if SEQS % 4 == 0 else 1
    batches = SEQS // group_size
    token_groups = tokens.reshape(batches, group_size, LENGTH, D).astype(jnp.float32)
    cotangent_groups = cotangent.reshape(batches, group_size, LENGTH, D).astype(jnp.float32)

    def one_group(totals, pieces):
        group_tokens, group_cotangent = pieces
        result, pullback = jax.vjp(block_layer, group_tokens, *parameters)
        gradients = pullback(group_cotangent)
        totals = tuple((running + addend for running, addend in zip(totals, gradients[1:])))
        return (totals, (result.astype(jnp.bfloat16), gradients[0]))
    initial = tuple((jnp.zeros(parameter.shape, jnp.float32) for parameter in parameters))
    totals, (outputs, token_grads) = lax.scan(one_group, initial, (token_groups, cotangent_groups))
    return (outputs.reshape(SEQS, LENGTH, D), token_grads.reshape(SEQS, LENGTH, D), totals[0], totals[1], totals[2], totals[3], totals[4], totals[5], totals[6], totals[7], totals[8], totals[9], totals[10], totals[11], totals[12], totals[13], totals[14], totals[15], totals[16])
```

```python
import math

import jax
import jax.numpy as jnp
from jax import lax
from jax.sharding import Mesh
from jax.sharding import PartitionSpec as P

HQ = 8
KVH = 2
HD = 128
MH = 48
MP = 64
NST = 256
EPSILON = 1e-05
ROPE_BASE = 100000000000.0
MASKED = -1e30
BF = jnp.bfloat16
F32 = jnp.float32
MESH_AXES = ("x", "z", "y", "c")
FSDP = ("z", "y", "c")
PARTS = 8


def mm(left, right):
    return jnp.dot(left, right, preferred_element_type=F32)


def outer_product(left, right):
    return lax.dot_general(left, right, (((0,), (0,)), ((), ())), preferred_element_type=F32)


def across(left, right):
    return lax.dot_general(left, right, (((1,), (1,)), ((), ())), preferred_element_type=F32)


def norm_factor(values, width=None):
    return lax.rsqrt(jnp.mean(values * values, axis=-1, keepdims=True) + EPSILON)


def norm_back(values, scaling, incoming):
    factor = norm_factor(values)
    normal = values * factor
    scaled = incoming * scaling
    grad_values = factor * (scaled - normal * jnp.mean(scaled * normal, axis=-1, keepdims=True))
    return (grad_values, jnp.sum(incoming * normal, axis=0))


def rope_tables(length, head_size):
    half_size = head_size // 2
    frequency = jnp.exp(
        jnp.arange(half_size, dtype=F32) * (-2.0 * math.log(ROPE_BASE) / head_size)
    )
    angles = jnp.arange(length, dtype=F32)[:, None] * frequency[None, :]
    return (jnp.cos(angles), jnp.sin(angles))


def rotate(values, cosine, sine):
    half = values.shape[-1] // 2
    front, back = values[..., :half], values[..., half:]
    return jnp.concatenate([front * cosine - back * sine, back * cosine + front * sine], axis=-1)


def conv(signal, kernel):
    taps, length = kernel.shape[0], signal.shape[1]
    padded = jnp.pad(signal, ((0, 0), (taps - 1, 0), (0, 0)))
    return sum(padded[:, j : j + length] * kernel[j] for j in range(taps))


def conv_back(signal, kernel, grad):
    taps, length = kernel.shape[0], signal.shape[1]
    padded = jnp.pad(signal, ((0, 0), (taps - 1, 0), (0, 0)))
    later = jnp.pad(grad, ((0, 0), (0, taps - 1), (0, 0)))
    grad_signal = sum(
        later[:, taps - 1 - j : taps - 1 - j + length] * kernel[j] for j in range(taps)
    )
    grad_kernel = jnp.stack(
        [jnp.sum(padded[:, j : j + length] * grad, axis=(0, 1)) for j in range(taps)]
    )
    return grad_signal, grad_kernel, jnp.sum(grad, axis=(0, 1))


def silu_back(values, grad):
    sig = jax.nn.sigmoid(values)
    return grad * sig * (1.0 + values * (1.0 - sig))


def core_parts(xin, step, maps, params):
    xk, xb, mk, mb, decay_log, step_bias, skip = params
    seqs, length, width = xin.shape
    heads = step.shape[-1]
    ux = conv(xin.astype(F32), xk) + xb
    um = conv(maps.astype(F32), mk) + mb
    xs = (ux * jax.nn.sigmoid(ux)).reshape(seqs, length, heads, MP)
    mv = (um * jax.nn.sigmoid(um)).astype(BF)
    bees, cees = mv[..., :NST], mv[..., NST:]
    dt = jax.nn.softplus(step.astype(F32) + step_bias)
    rate = -jnp.exp(decay_log)
    cum = jnp.cumsum(dt * rate, axis=1)
    causal = jnp.arange(length)[:, None] >= jnp.arange(length)[None, :]
    cumt = jnp.swapaxes(cum, 1, 2)
    decay = jnp.exp(jnp.where(causal, cumt[..., :, None] - cumt[..., None, :], MASKED))
    coupling = jnp.einsum("btn,bsn->bts", cees, bees, preferred_element_type=F32)
    mixing = (coupling[:, None] * decay).astype(BF)
    xr = (dt[..., None] * xs).astype(BF)
    y = jnp.einsum("bhts,bshp->bthp", mixing, xr, preferred_element_type=F32)
    return ux, um, xs, bees, cees, dt, rate, decay, mixing, xr, y


def core_forward(xin, step, maps, params):
    parts = core_parts(xin, step, maps, params)
    return (parts[-1] + params[-1][:, None] * parts[2]).reshape(xin.shape)


def core_backward(xin, step, maps, params, grad):
    xk, xb, mk, mb, decay_log, step_bias, skip = params
    ux, um, xs, bees, cees, dt, rate, decay, mixing, xr, y = core_parts(xin, step, maps, params)
    gy = grad.reshape(xs.shape)
    gyf = gy.astype(F32)
    gxr = jnp.einsum("bhts,bthp->bshp", mixing, gy, preferred_element_type=F32)
    gm = jnp.einsum("bthp,bshp->bhts", gy, xr, preferred_element_type=F32)
    gcoup = jnp.sum(gm * decay, axis=1).astype(BF)
    gc = jnp.einsum("bts,bsn->btn", gcoup, bees, preferred_element_type=F32)
    gb = jnp.einsum("bts,btn->bsn", gcoup, cees, preferred_element_type=F32)
    gcum = jnp.sum(gyf * y, axis=-1) - jnp.sum(xr.astype(F32) * gxr, axis=-1)
    ga = jnp.flip(jnp.cumsum(jnp.flip(gcum, 1), axis=1), 1)
    gdt = ga * rate + jnp.sum(gxr * xs, axis=-1)
    gdecay = jnp.sum(ga * dt, axis=(0, 1)) * rate
    gxs = gxr * dt[..., None] + skip[:, None] * gyf
    gskip = jnp.sum(gyf * xs, axis=(0, 1, 3))
    gstep = gdt * jax.nn.sigmoid(step.astype(F32) + step_bias)
    gsb = jnp.sum(gstep, axis=(0, 1))
    gux = silu_back(ux, gxs.reshape(ux.shape))
    gum = silu_back(um, jnp.concatenate([gb, gc], axis=-1))
    gxin, gxk, gxb = conv_back(xin.astype(F32), xk, gux)
    gmaps, gmk, gmb = conv_back(maps.astype(F32), mk, gum)
    return gxin, gstep, gmaps, gxk, gxb, gmk, gmb, gdecay, gsb, gskip


def score_rows(rq, rk):
    length = rq.shape[1]
    causal = jnp.arange(length)[:, None] >= jnp.arange(length)[None, :]
    scores = jnp.einsum("bqd,bkd->bqk", rq, rk, preferred_element_type=F32) * HD ** (-0.5)
    return jnp.where(causal, scores, MASKED)


def attend(rq, rk, v):
    scores = score_rows(rq, rk)
    highest = jnp.max(scores, axis=-1, keepdims=True)
    weights = jnp.exp(scores - highest)
    total = jnp.sum(weights, axis=-1, keepdims=True)
    probs = (weights / total).astype(BF)
    att = jnp.einsum("bqk,bkd->bqd", probs, v, preferred_element_type=F32).astype(BF)
    return att, highest + jnp.log(total)


def attend_back(rq, rk, v, lse, grad):
    p = jnp.exp(score_rows(rq, rk) - lse)
    gv = jnp.einsum("bqk,bqd->bkd", p.astype(BF), grad, preferred_element_type=F32)
    gp = jnp.einsum("bqd,bkd->bqk", grad, v, preferred_element_type=F32)
    gs = (p * (gp - jnp.sum(p * gp, axis=-1, keepdims=True))).astype(BF)
    scale = HD ** (-0.5)
    gq = jnp.einsum("bqk,bkd->bqd", gs, rk, preferred_element_type=F32) * scale
    gk = jnp.einsum("bqk,bqd->bkd", gs, rq, preferred_element_type=F32) * scale
    return gq, gk, gv


def flip(value, *axes):
    count = 2 ** len(axes)
    pairs = [(i, count - 1 - i) for i in range(count)]
    axes = tuple(sorted(axes, key=MESH_AXES.index))
    return lax.ppermute(value, axes, pairs)


def ordered(own, other, axis):
    second = lax.axis_index(axis) == 1
    return jnp.where(second, other, own), jnp.where(second, own, other)


def plane_gather(block):
    half = block.shape[0] // 2
    by_x, by_y = flip(block, "x"), flip(block, "y")
    diagonal = jnp.concatenate([flip(by_x[:half], "y"), flip(by_y[half:], "x")])
    here = [block, by_x, by_y, diagonal]
    there = [flip(v, "c") for v in here]
    out = []
    for own, other in ((0, 1), (2, 3)):
        out += ordered(here[own], here[other], "x")
    for own, other in ((0, 1), (2, 3)):
        out += ordered(there[own], there[other], "x")
    return jnp.concatenate(out)


def plane_scatter(partial):
    rows = partial(1).shape[0]
    far = partial(1).astype(BF)
    near = partial(0)
    width = near.shape[1]
    count = rows // 4
    x = lax.axis_index("x")
    outs = []
    for at, first in ((0, "y"), (1, "x")):
        cols = slice(at * (width // 2), (at + 1) * (width // 2))
        chip = near[:, cols] + flip(far[:, cols], "c").astype(F32)
        chip = chip.reshape(2, 2, count, width // 2)
        if first == "y":
            got = flip(chip[1].astype(BF), "y")
            line = chip[0] + got.astype(F32)
            away = lax.dynamic_index_in_dim(line, 1 - x, 0, keepdims=False)
            kept = lax.dynamic_index_in_dim(line, x, 0, keepdims=False)
            got = flip(away.astype(BF), "x")
        else:
            away = lax.dynamic_index_in_dim(chip, 1 - x, 1, keepdims=False)
            kept = lax.dynamic_index_in_dim(chip, x, 1, keepdims=False)
            line = kept + flip(away.astype(BF), "x").astype(F32)
            kept, got = line[0], flip(line[1].astype(BF), "y")
        outs.append(kept + got.astype(F32))
    return jnp.concatenate(outs, axis=1)


def flip_rows(value, axis):
    got = flip(value, axis)
    if axis == "x":
        return got
    parts = got.reshape((2, 2, -1) + value.shape[1:])
    return jnp.flip(parts, 0 if axis == "c" else 1).reshape(value.shape)


def plane_sum(value):
    for axis in ("c", "y", "x"):
        value = value + flip_rows(value, axis)
    return value


def column_sum(value, axes):
    for axis in axes:
        half = value.shape[1] // 2
        at = lax.axis_index(axis)
        away = lax.dynamic_slice_in_dim(value, (1 - at) * half, half, 1)
        kept = lax.dynamic_slice_in_dim(value, at * half, half, 1)
        value = kept.astype(F32) + flip_rows(away.astype(BF), axis).astype(F32)
    return value


def row_half(value, index):
    half = value.shape[0] // 2
    return value[index * half : (index + 1) * half]


def part_index():
    return 4 * lax.axis_index("x") + 2 * lax.axis_index("c") + lax.axis_index("y")


def half_columns(weight):
    half = weight.shape[1] // 2
    return lax.dynamic_slice_in_dim(weight, lax.axis_index("x") * half, half, 1)


def exchange(blocks, high, low):
    h, l = lax.axis_index(high), lax.axis_index(low)

    def block(dh, dl):
        return lax.dynamic_index_in_dim(blocks, 2 * (h ^ dh) + (l ^ dl), 0, keepdims=False)

    own, by_low = block(0, 0), flip(block(0, 1), low)
    by_high, by_both = flip(block(1, 0), high), flip(block(1, 1), high, low)
    near, far = ordered(own, by_low, low), ordered(by_high, by_both, low)
    first, second = ordered(near[0], far[0], high), ordered(near[1], far[1], high)
    return [[first[0], second[0]], [first[1], second[1]]]


def gather_inner(block):
    by_c = flip(block, "c")
    by_y, by_both = flip(block, "y"), flip(by_c, "y")
    near, far = ordered(block, by_c, "c"), ordered(by_y, by_both, "c")
    first, second = ordered(near[0], far[0], "y"), ordered(near[1], far[1], "y")
    whole = jnp.stack([first[0], second[0], first[1], second[1]], axis=1)
    return whole.reshape(-1, block.shape[-1])


def fetch_columns(weights):
    rows = weights[0].shape[0]
    block = jnp.concatenate(
        [half_columns(w).reshape(rows, 4, w.shape[1] // PARTS) for w in weights], axis=2
    )
    got = exchange(block.transpose(1, 0, 2), "c", "y")
    moved = jnp.concatenate([got[0][0], got[1][0], got[0][1], got[1][1]])
    return lax.all_gather(moved, "z", axis=0, tiled=True)


def return_columns(grad, widths):
    part = lax.psum_scatter(grad.astype(BF), "z", scatter_dimension=0, tiled=True)
    rows, width = part.shape[0] // 4, part.shape[1]
    part = part.reshape(2, 2, rows, width).transpose(1, 0, 2, 3).reshape(4, rows, width)
    got = exchange(part, "c", "y")
    moved = jnp.stack([got[0][0], got[0][1], got[1][0], got[1][1]], axis=1)
    whole = jnp.stack(ordered(moved, flip(moved, "x"), "x"), axis=1)
    outs, at = [], 0
    for w in widths:
        outs.append(whole[..., at : at + w].astype(F32))
        at += w
    return outs


def fetch_rows(weight):
    if lax.axis_size("z") != 4:
        whole = lax.all_gather(weight, FSDP, axis=0, tiled=True)
        rows = whole.shape[0] // PARTS
        return lax.dynamic_slice_in_dim(whole, part_index() * rows, rows, 0)
    block = lax.all_gather(half_columns(weight), "z", axis=0, tiled=False)
    got = exchange(block, "x", "c")
    return jnp.concatenate(
        [jnp.concatenate([got[0][c], got[1][c]], axis=1) for c in (0, 1)], axis=0
    )


def return_rows(grad):
    rows, cols = grad.shape
    if lax.axis_size("z") != 4:
        whole = jnp.zeros((rows * PARTS, cols), BF)
        whole = lax.dynamic_update_slice_in_dim(whole, grad.astype(BF), part_index() * rows, 0)
        whole = lax.psum_scatter(whole, FSDP, scatter_dimension=0, tiled=True)
        return lax.psum(whole, "x").astype(F32)
    block = grad.astype(BF).reshape(2, rows // 2, 2, cols // 2).transpose(2, 0, 1, 3)
    got = exchange(block.reshape(4, rows // 2, cols // 2), "x", "c")
    moved = jnp.stack([got[0][0], got[0][1], got[1][0], got[1][1]])
    part = lax.psum_scatter(moved, "z", scatter_dimension=0, tiled=False)
    return jnp.concatenate(ordered(part, flip(part, "x"), "x"), axis=1).astype(F32)


def pack(arrays, multiple):
    flat = jnp.concatenate([a.reshape(-1) for a in arrays])
    return jnp.pad(flat, (0, -flat.shape[0] % multiple))


def shards(
    tokens,
    cotangent,
    mixer_gain,
    query_weight,
    key_weight,
    value_weight,
    attn_out_weight,
    mamba_in_weight,
    conv_weight,
    conv_bias,
    decay_log,
    step_bias,
    skip_gain,
    mamba_gain,
    mamba_out_weight,
    ffn_gain,
    gate_weight,
    up_weight,
    down_weight,
):
    token_count, model_dim = tokens.shape[1], tokens.shape[2]
    length = 2 * token_count
    inner = MH * MP
    channels = inner + 2 * NST
    part = part_index()
    wide, heads = inner // PARTS, MH // PARTS
    rows = token_count * PARTS
    seqs = rows // length
    fsdp = lax.axis_size("z") * 4

    smalls = [mixer_gain, ffn_gain, mamba_gain, conv_bias, conv_weight]
    gathered = lax.all_gather(pack(smalls, 128), FSDP, axis=0, tiled=False)
    got, at = [], 0
    for s in smalls:
        got.append(gathered[:, at : at + s.size].reshape((fsdp,) + s.shape))
        at += s.size
    gain_in = got[0].reshape(-1).astype(F32)
    gain_ffn = got[1].reshape(-1).astype(F32)
    gain_mamba = got[2].reshape(-1).astype(F32)
    bias_full = got[3].reshape(-1).astype(F32)
    conv_full = got[4].transpose(1, 0, 2).reshape(4, channels).astype(F32)
    gain_mamba = lax.dynamic_slice_in_dim(gain_mamba, part * wide, wide, 0)

    def own_heads(v):
        return lax.dynamic_slice_in_dim(v.astype(F32), part * heads, heads, 0)

    core_params = (
        lax.dynamic_slice_in_dim(conv_full, part * wide, wide, 1),
        lax.dynamic_slice_in_dim(bias_full, part * wide, wide, 0),
        conv_full[:, inner:],
        bias_full[inner:],
        own_heads(decay_log),
        own_heads(step_bias),
        own_heads(skip_gain),
    )

    kvh = HD * lax.axis_index("x")
    shared = jnp.concatenate(
        [
            lax.dynamic_slice_in_dim(key_weight, kvh, HD, 1),
            lax.dynamic_slice_in_dim(value_weight, kvh, HD, 1),
            mamba_in_weight[:, 2 * inner :],
        ],
        axis=1,
    )
    shared = gather_inner(lax.all_gather(shared, "z", axis=0, tiled=False))
    w_in = fetch_columns(
        [query_weight, mamba_in_weight[:, :inner], mamba_in_weight[:, inner : 2 * inner]]
    )
    w_attn_out = fetch_rows(attn_out_weight)
    w_mamba_out = fetch_rows(mamba_out_weight)
    w_gateup = fetch_columns([gate_weight, up_weight])
    w_down = fetch_rows(down_weight)
    ff = w_down.shape[0]

    token_rows = tokens.reshape(token_count, model_dim).astype(F32)
    hidden = (token_rows * norm_factor(token_rows) * gain_in).astype(BF)
    hidden = plane_gather(hidden)
    incoming = plane_gather(cotangent.reshape(token_count, model_dim))

    projected = mm(hidden, w_in)
    query = projected[:, :HD].astype(BF)
    gate_branch = projected[:, HD : HD + wide]
    xin = projected[:, HD + wide :].astype(BF).reshape(seqs, length, wide)
    common = mm(hidden, shared).astype(BF)
    key, value = common[:, :HD], common[:, HD : 2 * HD]
    maps = common[:, 2 * HD : 2 * HD + 2 * NST].reshape(seqs, length, 2 * NST)
    step = lax.dynamic_slice_in_dim(common, 2 * HD + 2 * NST + part * heads, heads, 1)
    step = step.reshape(seqs, length, heads)

    cosine, sine = rope_tables(length, HD)
    rq = rotate(query.reshape(seqs, length, HD).astype(F32), cosine, sine).astype(BF)
    rk = rotate(key.reshape(seqs, length, HD).astype(F32), cosine, sine).astype(BF)
    value = value.reshape(seqs, length, HD)
    attended, lse = attend(rq, rk, value)
    attended = attended.reshape(rows, HD)
    scanned = core_forward(xin, step, maps, core_params).reshape(rows, wide)
    scanned = scanned.astype(BF).astype(F32)

    sig_z = jax.nn.sigmoid(gate_branch)
    silu_z = gate_branch * sig_z
    gated = scanned * silu_z
    squares = plane_sum(jnp.sum(gated * gated, axis=-1))
    factor = lax.rsqrt(squares / inner + EPSILON)[:, None]
    normal = gated * factor
    normed = (normal * gain_mamba).astype(BF)
    mixed = jnp.concatenate([attended, normed], axis=1)
    w_out = jnp.concatenate([w_attn_out, w_mamba_out], axis=0)
    mixer_sum = plane_scatter(lambda i: mm(row_half(mixed, i), w_out))
    middle = token_rows + mixer_sum
    second = (middle * norm_factor(middle) * gain_ffn).astype(BF)
    second = plane_gather(second)
    gate_up = mm(second, w_gateup)
    gate_act, up_act = gate_up[:, :ff], gate_up[:, ff:]
    sig_g = jax.nn.sigmoid(gate_act)
    active = (gate_act * sig_g * up_act).astype(BF)
    result = middle + plane_scatter(lambda i: mm(row_half(active, i), w_down))
    output = result.astype(BF).reshape(1, token_count, model_dim)

    grad_down = outer_product(active, incoming)
    grad_active = across(incoming, w_down)
    grad_gate = grad_active * up_act * sig_g * (1.0 + gate_act * (1.0 - sig_g))
    grad_up = grad_active * gate_act * sig_g
    grad_gateup = jnp.concatenate([grad_gate.astype(BF), grad_up.astype(BF)], axis=1)
    grad_wgateup = outer_product(second, grad_gateup)
    grad_second = plane_scatter(lambda i: across(row_half(grad_gateup, i), w_gateup))
    grad_norm, grad_gain_ffn = norm_back(middle, gain_ffn, grad_second)
    grad_middle = cotangent.reshape(token_count, model_dim).astype(F32) + grad_norm

    grad_mixer = plane_gather(grad_middle.astype(BF))
    grad_out = outer_product(mixed, grad_mixer)
    grad_att = across(grad_mixer, w_attn_out).astype(BF).reshape(seqs, length, HD)
    grad_normed = across(grad_mixer, w_mamba_out)
    grad_gain_mamba = jnp.sum(grad_normed * normal, axis=0)
    scaled = grad_normed * gain_mamba
    dots = plane_sum(jnp.sum(scaled * normal, axis=-1))[:, None] / inner
    grad_gated = factor * (scaled - normal * dots)
    grad_scanned = (grad_gated * silu_z).astype(BF).reshape(seqs, length, wide)
    grad_gate_branch = grad_gated * scanned * sig_z * (1.0 + gate_branch * (1.0 - sig_z))

    gq, gk, gv = attend_back(rq, rk, value, lse, grad_att)
    gq = rotate(gq, cosine, -sine).astype(BF).reshape(rows, HD)
    gk = rotate(gk, cosine, -sine).reshape(rows, HD)
    gv = gv.reshape(rows, HD)
    gxin, gstep, gmaps, gxk, gxb, gmk, gmb, gdecay, gsb, gskip = core_backward(
        xin, step, maps, core_params, grad_scanned
    )
    grad_in = jnp.concatenate(
        [gq, grad_gate_branch.astype(BF), gxin.reshape(rows, wide).astype(BF)], axis=1
    )
    grad_win = outer_product(hidden, grad_in)
    gstep_all = lax.dynamic_update_slice_in_dim(
        jnp.zeros((rows, MH), BF), gstep.reshape(rows, heads).astype(BF), part * heads, 1
    )
    grad_common = jnp.concatenate(
        [gk.astype(BF), gv.astype(BF), gmaps.reshape(rows, 2 * NST).astype(BF), gstep_all], axis=1
    )
    kv_part = column_sum(grad_common[:, : 2 * HD], ("c", "y"))
    maps_part = column_sum(grad_common[:, 2 * HD : 2 * HD + 2 * NST], ("c", "y", "x"))
    grad_slices = jnp.concatenate([kv_part, maps_part, gstep.reshape(rows, heads)], axis=1)
    grad_wslices = outer_product(hidden, grad_slices.astype(BF))
    grad_hidden = plane_scatter(
        lambda i: across(row_half(grad_in, i), w_in) + across(row_half(grad_common, i), shared)
    )
    grad_norm, grad_gain_in = norm_back(token_rows, gain_in, grad_hidden)
    tokens_grad = (grad_middle + grad_norm).reshape(1, token_count, model_dim)

    shard_down = return_rows(grad_down)
    shard_gate, shard_up = return_columns(grad_wgateup, [ff, ff])
    shard_attn_out = return_rows(grad_out[:HD])
    shard_mamba_out = return_rows(grad_out[HD:])
    grad_win = jnp.concatenate([grad_win, grad_wslices], axis=1)
    shard_query, shard_gate_br, shard_xin, kv, mapped, stepped = return_columns(
        grad_win, [HD, wide, wide, HD // 2, NST // 4, heads]
    )
    count = query_weight.shape[0]
    shard_key = kv[:, :, :2].reshape(count, 2 * HD)
    shard_value = kv[:, :, 2:].reshape(count, 2 * HD)
    shard_mamba_in = jnp.concatenate(
        [
            shard_gate_br.reshape(count, inner),
            shard_xin.reshape(count, inner),
            mapped.transpose(0, 2, 1, 3).reshape(count, 2 * NST),
            stepped.reshape(count, MH),
        ],
        axis=1,
    )
    shard_query = shard_query.reshape(count, HQ * HD)
    shard_gate = shard_gate.reshape(count, PARTS * ff)
    shard_up = shard_up.reshape(count, PARTS * ff)

    conv_grad = jnp.zeros((4, channels), F32)
    conv_grad = lax.dynamic_update_slice_in_dim(conv_grad, gxk, part * wide, 1)
    conv_grad = conv_grad.at[:, inner:].set(gmk)
    bias_grad = jnp.zeros((channels,), F32)
    bias_grad = lax.dynamic_update_slice_in_dim(bias_grad, gxb, part * wide, 0)
    bias_grad = bias_grad.at[inner:].set(gmb)
    gain_grad = lax.dynamic_update_slice_in_dim(
        jnp.zeros((inner,), F32), grad_gain_mamba, part * wide, 0
    )
    head_grad = lax.dynamic_update_slice_in_dim(
        jnp.zeros((3, MH), F32), jnp.stack([gdecay, gsb, gskip]), part * heads, 1
    )
    spread = [grad_gain_in, grad_gain_ffn, gain_grad, bias_grad]
    little = [v.reshape(fsdp, -1) for v in spread]
    little.append(conv_grad.reshape(4, fsdp, -1).transpose(1, 0, 2).reshape(fsdp, -1))
    little.append(jnp.broadcast_to(head_grad.reshape(1, -1), (fsdp, 3 * MH)))
    little = jnp.concatenate(little, axis=1)
    total = lax.all_to_all(little, FSDP, split_axis=0, concat_axis=0, tiled=True).sum(axis=0)
    total = total + flip(total, "x")
    got, at = [], 0
    for like in (mixer_gain, ffn_gain, mamba_gain, conv_bias, conv_weight, head_grad):
        got.append(total[at : at + like.size].reshape(like.shape))
        at += like.size

    return (
        output,
        tokens_grad,
        got[0],
        shard_query,
        shard_key,
        shard_value,
        shard_attn_out,
        shard_mamba_in,
        got[4],
        got[3],
        got[5][0],
        got[5][1],
        got[5][2],
        got[2],
        shard_mamba_out,
        got[1],
        shard_gate,
        shard_up,
        shard_down,
    )


def solution(mesh):
    fsdp = mesh.shape["fsdp"]
    grid = Mesh(mesh.devices.reshape(2, fsdp // 4, 2, 2), ("x", "z", "y", "c"))
    rows, flat, whole = P(FSDP, None), P(FSDP), P()
    stream = P(FSDP, "x", None)
    weights = (
        flat, rows, rows, rows, rows, rows, P(None, FSDP), flat, whole, whole, whole,
        flat, rows, flat, rows, rows, rows,
    )
    return jax.shard_map(
        shards,
        mesh=grid,
        in_specs=(stream, stream) + weights,
        out_specs=(stream, stream) + weights,
        check_vma=False,
    )
```

```python
import math

import jax
import jax.numpy as jnp
from jax import lax
from jax.experimental import pallas as pl
from jax.experimental.pallas import tpu as pltpu
from jax.sharding import Mesh
from jax.sharding import PartitionSpec as P

HQ = 8
KVH = 2
HD = 128
MH = 48
MP = 64
NST = 256
EPSILON = 1e-05
ROPE_BASE = 100000000000.0
MASKED = -1e30
BF = jnp.bfloat16
F32 = jnp.float32
MESH_AXES = ("x", "z", "y", "c")
FSDP = ("z", "y", "c")
PARTS = 8
VMEM = 48 * 1024 * 1024


def mm(left, right):
    return jnp.dot(left, right, preferred_element_type=F32)


def outer_product(left, right):
    return lax.dot_general(left, right, (((0,), (0,)), ((), ())), preferred_element_type=F32)


def across(left, right):
    return lax.dot_general(left, right, (((1,), (1,)), ((), ())), preferred_element_type=F32)


def rope_tables(length, head_size):
    half_size = head_size // 2
    frequency = jnp.exp(
        jnp.arange(half_size, dtype=F32) * (-2.0 * math.log(ROPE_BASE) / head_size)
    )
    angles = jnp.arange(length, dtype=F32)[:, None] * frequency[None, :]
    cosine, sine = jnp.cos(angles), jnp.sin(angles)
    return [jnp.concatenate(v, axis=1) for v in ([cosine, cosine], [-sine, sine])]


def silu_parts(values):
    sig = 1.0 / (1.0 + jnp.exp(-values))
    return values * sig, sig


def shifted(values, count):
    if count == 0:
        return values
    rows = values.shape[0]
    at = lax.broadcasted_iota(jnp.int32, values.shape, 0)
    kept = (at >= count) if count > 0 else (at < rows + count)
    return jnp.where(kept, pltpu.roll(values, count % rows, 0), 0.0)


def conv_silu(signal, kernel, bias):
    taps = kernel.shape[0]
    total = bias + signal * kernel[taps - 1 : taps]
    for back in range(1, taps):
        total = total + shifted(signal, back) * kernel[taps - 1 - back : taps - back]
    value, sig = silu_parts(total)
    return value, sig * (1.0 + total * (1.0 - sig))


def conv_grads(signal, kernel, grad):
    taps = kernel.shape[0]
    back = grad * kernel[taps - 1 : taps]
    rows = []
    for count in range(taps - 1, 0, -1):
        rows.append(jnp.sum(shifted(signal, count) * grad, axis=0, keepdims=True))
        back = back + shifted(grad, -count) * kernel[taps - 1 - count : taps - count]
    rows.append(jnp.sum(signal * grad, axis=0, keepdims=True))
    return back, jnp.concatenate(rows, axis=0), jnp.sum(grad, axis=0, keepdims=True)


def dot(left, right, dims=((1,), (0,)), precision=None):
    return lax.dot_general(
        left, right, (dims, ((), ())), preferred_element_type=F32, precision=precision
    )


ROWS = ((0,), (0,))
LANES = ((1,), (1,))
PRECISE = lax.Precision.HIGHEST


def step_place():
    return (MH // PARTS) * (2 * lax.axis_index("c") + lax.axis_index("y"))


def scan_parts(x_ref, m_ref, s_ref, xk_ref, xb_ref, mk_ref, mb_ref, h_ref):
    length = x_ref.shape[0]
    xin, maps = x_ref[...].astype(BF).astype(F32), m_ref[...].astype(F32)
    xs, xslope = conv_silu(xin, xk_ref[...], xb_ref[...])
    mv, mslope = conv_silu(maps, mk_ref[...], mb_ref[...])
    mv = mv.astype(BF)
    bees, cees = mv[:, :NST], mv[:, NST:]
    raw = pltpu.roll(s_ref[...].astype(F32), 2 * MP - step_place(), 1) + h_ref[1:2]
    dt = jnp.maximum(raw, 0.0) + jnp.log1p(jnp.exp(-jnp.abs(raw)))
    rate = -jnp.exp(h_ref[0:1])
    t = lax.broadcasted_iota(jnp.int32, (length, length), 0)
    s = lax.broadcasted_iota(jnp.int32, (length, length), 1)
    lower = (t >= s).astype(F32)
    cum = dot(lower, dt * rate, precision=PRECISE)
    coupling = dot(cees, bees, LANES)
    return xin, maps, xs, xslope, mslope, bees, cees, raw, dt, rate, lower, cum, coupling


def lane_pair(values, first):
    lane = lax.broadcasted_iota(jnp.int32, (values.shape[0], 2 * MP), 1)
    return jnp.where(lane < MP, values[:, first : first + 1], values[:, first + 1 : first + 2])


def decay_of(cum, cumt, lower, head):
    gap = cum[:, head : head + 1] - cumt[head : head + 1, :]
    return jnp.exp(jnp.where(lower > 0.0, gap, MASKED))


def rotated(ref, cos_ref, sin_ref):
    value = ref[...].astype(BF).astype(F32)
    return (value * cos_ref[...] + pltpu.roll(value, HD // 2, 1) * sin_ref[...]).astype(BF)


def causal_scores(rq, rk):
    length = rq.shape[0]
    t = lax.broadcasted_iota(jnp.int32, (length, length), 0)
    s = lax.broadcasted_iota(jnp.int32, (length, length), 1)
    scores = jnp.where(t >= s, dot(rq, rk, LANES) * HD ** (-0.5), MASKED)
    highest = jnp.max(scores, axis=1, keepdims=True)
    weights = jnp.exp(scores - highest)
    return weights, jnp.sum(weights, axis=1, keepdims=True)


def mixer_kernel(
    x_ref, m_ref, s_ref, z_ref, q_ref, k_ref, v_ref, xk_ref, xb_ref, mk_ref, mb_ref, h_ref,
    cos_ref, sin_ref, scan_ref, gated_ref, square_ref, att_ref,
):
    xin, maps, xs, xslope, mslope, bees, cees, raw, dt, rate, lower, cum, coupling = scan_parts(
        x_ref, m_ref, s_ref, xk_ref, xb_ref, mk_ref, mb_ref, h_ref
    )
    cumt = cum.T
    lane = lax.broadcasted_iota(jnp.int32, (xs.shape[0], 2 * MP), 1)
    squares = jnp.zeros((xs.shape[0], 1), F32)
    for pair in range(xs.shape[1] // (2 * MP)):
        cols = slice(2 * MP * pair, 2 * MP * (pair + 1))
        xp = xs[:, cols]
        xr = (xp * lane_pair(dt, 2 * pair)).astype(BF)
        ys = []
        for head in (2 * pair, 2 * pair + 1):
            mixing = (coupling * decay_of(cum, cumt, lower, head)).astype(BF)
            ys.append(dot(mixing, xr))
        y = jnp.where(lane < MP, ys[0], ys[1]) + lane_pair(h_ref[2:3], 2 * pair) * xp
        y = y.astype(BF)
        scan_ref[:, cols] = y
        gated = y.astype(F32) * silu_parts(z_ref[:, cols])[0]
        gated_ref[:, cols] = gated
        squares = squares + jnp.sum(gated * gated, axis=1, keepdims=True)
    square_ref[...] = squares
    weights, total = causal_scores(
        rotated(q_ref, cos_ref, sin_ref), rotated(k_ref, cos_ref, sin_ref)
    )
    att_ref[...] = dot((weights / total).astype(BF), v_ref[...]).astype(BF)


def mixer_back_kernel(
    x_ref, m_ref, s_ref, z_ref, q_ref, k_ref, v_ref, xk_ref, xb_ref, mk_ref, mb_ref, h_ref,
    cos_ref, sin_ref, scan_ref, gn_ref, gain_ref, factor_ref, dots_ref, ga_ref,
    gin_ref, gcom_ref,
    gxk_ref, gxb_ref, gmk_ref, gmb_ref, gh_ref,
):
    xin, maps, xs, xslope, mslope, bees, cees, raw, dt, rate, lower, cum, coupling = scan_parts(
        x_ref, m_ref, s_ref, xk_ref, xb_ref, mk_ref, mb_ref, h_ref
    )
    length, width = xs.shape
    cumt = cum.T
    lane = lax.broadcasted_iota(jnp.int32, (length, 2 * MP), 1)
    factor, dots = factor_ref[...], dots_ref[...]
    gcoup = jnp.zeros((length, length), F32)
    gcum = jnp.zeros((length, 2 * MP), F32)
    gdt = jnp.zeros((length, 2 * MP), F32)
    gskip = jnp.zeros((1, 2 * MP), F32)
    gus = []
    for pair in range(width // (2 * MP)):
        cols = slice(2 * MP * pair, 2 * MP * (pair + 1))
        gate, scanned = z_ref[:, cols], scan_ref[:, cols].astype(F32)
        silu_z, sig_z = silu_parts(gate)
        normal = scanned * silu_z * factor
        ggated = factor * (gn_ref[:, cols] * gain_ref[:, cols] - normal * dots)
        gin_ref[:, cols] = (ggated * scanned * sig_z * (1.0 + gate * (1.0 - sig_z))).astype(BF)
        gy = (ggated * silu_z).astype(BF)
        gyf = gy.astype(F32)
        xp, dtp = xs[:, cols], lane_pair(dt, 2 * pair)
        xr = (xp * dtp).astype(BF)
        ys, gxrs = [], []
        for own, head in enumerate((2 * pair, 2 * pair + 1)):
            mine = (lane < MP) if own == 0 else (lane >= MP)
            decay = decay_of(cum, cumt, lower, head)
            mixing = (coupling * decay).astype(BF)
            ys.append(dot(mixing, xr))
            gxrs.append(dot(mixing, gy, ROWS))
            gcoup = gcoup + dot(jnp.where(mine, gy, jnp.zeros_like(gy)), xr, LANES) * decay
        y = jnp.where(lane < MP, ys[0], ys[1])
        gxr = jnp.where(lane < MP, gxrs[0], gxrs[1])
        flow, drive, direct = gyf * y - xr.astype(F32) * gxr, gxr * xp, gyf * xp
        for own, head in enumerate((2 * pair, 2 * pair + 1)):
            mine = (lane < MP) if own == 0 else (lane >= MP)

            def share(v):
                return jnp.sum(jnp.where(mine, v, 0.0), axis=1, keepdims=True)

            gcum = jnp.where(lane == head, share(flow), gcum)
            gdt = jnp.where(lane == head, share(drive), gdt)
            gskip = jnp.where(
                lane[:1] == head, jnp.sum(share(direct), axis=0, keepdims=True), gskip
            )
        gus.append((gxr * dtp + lane_pair(h_ref[2:3], 2 * pair) * gyf) * xslope[:, cols])
    gu = jnp.concatenate(gus, axis=1)
    gx, gxk, gxb = conv_grads(xin, xk_ref[...], gu)
    gin_ref[:, width : 2 * width] = gx.astype(BF)
    gflow = dot(lower, gcum, ROWS, precision=PRECISE)
    gdt = gdt + gflow * rate
    graw = gdt / (1.0 + jnp.exp(-raw))
    graw = jnp.where(lane < width // MP, graw, 0.0)
    gcom_ref[:, 2 * NST + 2 * HD :] = pltpu.roll(graw, step_place(), 1).astype(BF)
    gdecay = jnp.sum(gflow * dt, axis=0, keepdims=True) * rate
    gcb = gcoup.astype(BF)
    gmaps = jnp.concatenate([dot(gcb, cees, ROWS), dot(gcb, bees)], axis=1) * mslope
    gm, gmk, gmb = conv_grads(maps, mk_ref[...], gmaps)
    gcom_ref[:, : 2 * NST] = gm.astype(BF)
    gh = jnp.concatenate([gdecay, jnp.sum(graw, axis=0, keepdims=True), gskip], axis=0)

    @pl.when(pl.program_id(0) == 0)
    def _():
        for ref in (gxk_ref, gxb_ref, gmk_ref, gmb_ref, gh_ref):
            ref[...] = jnp.zeros_like(ref)

    gxk_ref[...] += gxk
    gxb_ref[...] += gxb
    gmk_ref[...] += gmk
    gmb_ref[...] += gmb
    gh_ref[0:3] += gh

    rq, rk = rotated(q_ref, cos_ref, sin_ref), rotated(k_ref, cos_ref, sin_ref)
    weights, total = causal_scores(rq, rk)
    probs = weights / total
    gatt = ga_ref[...]
    gcom_ref[:, 2 * NST + HD : 2 * NST + 2 * HD] = dot(probs.astype(BF), gatt, ROWS).astype(BF)
    gp = dot(gatt, v_ref[...], LANES)
    gsc = (probs * (gp - jnp.sum(probs * gp, axis=1, keepdims=True))).astype(BF)
    places = ((gin_ref, 2 * width), (gcom_ref, 2 * NST))
    for (ref, at), grad in zip(places, (dot(gsc, rk), dot(gsc, rq, ROWS))):
        grad = grad * HD ** (-0.5)
        back = grad * cos_ref[...] - pltpu.roll(grad, HD // 2, 1) * sin_ref[...]
        ref[:, at : at + HD] = back.astype(BF)


def column_block(length, width, at):
    return pl.BlockSpec((length, width), lambda i: (i, at // width))


def mixer_specs(length, wide):
    return [
        column_block(length, wide, wide),
        column_block(length, 2 * NST, 0),
        column_block(length, 2 * MP, 2 * NST + 2 * HD),
        column_block(length, wide, 0),
        column_block(length, HD, 2 * wide),
        column_block(length, HD, 2 * NST),
        column_block(length, HD, 2 * NST + HD),
    ]


def whole_specs(arrays):
    return [pl.BlockSpec(a.shape, lambda i: (0, 0)) for a in arrays]


def mixer_forward(seqs, length, projected, common, params, tables):
    wide = params[0].shape[1]
    outs = [(wide, BF), (wide, F32), (1, F32), (HD, BF)]
    return pl.pallas_call(
        mixer_kernel,
        grid=(seqs,),
        in_specs=mixer_specs(length, wide) + whole_specs(params + tables),
        out_specs=[column_block(length, w, 0) for w, _ in outs],
        out_shape=[jax.ShapeDtypeStruct((seqs * length, w), d) for w, d in outs],
        compiler_params=pltpu.CompilerParams(vmem_limit_bytes=VMEM),
        name="mixer",
    )(projected, common, common, projected, projected, common, common, *params, *tables)


def mixer_backward(seqs, length, projected, common, params, tables, scanned, grad_normed, gain, factor, dots, grad_att):
    wide = params[0].shape[1]
    outs = [2 * wide + HD, 2 * NST + 2 * HD + 2 * MP]
    sums = [(4, wide), (1, wide), (4, 2 * NST), (1, 2 * NST), (8, 2 * MP)]
    rows = [scanned, grad_normed]
    tail = [factor, dots, grad_att]
    return pl.pallas_call(
        mixer_back_kernel,
        grid=(seqs,),
        in_specs=mixer_specs(length, wide) + whole_specs(params + tables)
        + [column_block(length, a.shape[1], 0) for a in rows] + whole_specs([gain])
        + [column_block(length, a.shape[1], 0) for a in tail],
        out_specs=[column_block(length, w, 0) for w in outs]
        + [pl.BlockSpec(s, lambda i: (0, 0)) for s in sums],
        out_shape=[jax.ShapeDtypeStruct((seqs * length, w), BF) for w in outs]
        + [jax.ShapeDtypeStruct(s, F32) for s in sums],
        compiler_params=pltpu.CompilerParams(vmem_limit_bytes=VMEM),
        name="mixer_back",
    )(
        projected, common, common, projected, projected, common, common,
        *params, *tables, *rows, gain, *tail,
    )


def remote(src, dst, send, recv, axis):
    other = 1 - lax.axis_index(axis)
    return pltpu.make_async_remote_copy(
        src_ref=src,
        dst_ref=dst,
        send_sem=send,
        recv_sem=recv,
        device_id={axis: other},
        device_id_type=pl.DeviceIdType.MESH,
    )


def greet(axes):
    barrier = pltpu.get_barrier_semaphore()
    for axis in axes:
        other = 1 - lax.axis_index(axis)
        pl.semaphore_signal(
            barrier, inc=1, device_id={axis: other}, device_id_type=pl.DeviceIdType.MESH
        )
    pl.semaphore_wait(barrier, len(axes))


def line_item(region, sems, sources=None):
    z, n = lax.axis_index("z"), lax.axis_size("z")

    def copy(way, k, at, src):
        return pltpu.make_async_remote_copy(
            src_ref=src,
            dst_ref=region(at),
            send_sem=sems.at[0, way, k],
            recv_sem=sems.at[1, way, k],
            device_id={"z": z + 1 - 2 * way},
            device_id_type=pl.DeviceIdType.MESH,
        )

    def send(k):
        src = sources if k == 0 and sources is not None else None

        @pl.when((z + 1 < n) & (z - k >= 0))
        def _():
            copy(0, k, z - k, region(z - k) if src is None else src).start()

        @pl.when((z >= 1) & (z + k < n))
        def _():
            copy(1, k, z + k, region(z + k) if src is None else src).start()

    def arrive(k):
        @pl.when(z - 1 - k >= 0)
        def _():
            copy(0, k, z - 1 - k, region(z - 1 - k)).wait_recv()

        @pl.when(z + 1 + k < n)
        def _():
            copy(1, k, z + 1 + k, region(z + 1 + k)).wait_recv()

    def finish():
        for k in range(n - 1):
            src = sources if k == 0 and sources is not None else None

            @pl.when((z + 1 < n) & (z - k >= 0))
            def _(k=k, src=src):
                copy(0, k, z - k, region(z - k) if src is None else src).wait_send()

            @pl.when((z >= 1) & (z + k < n))
            def _(k=k, src=src):
                copy(1, k, z + k, region(z + k) if src is None else src).wait_send()

    return send, arrive, finish


def gather_regions(region, half, sems, own_ready, own=None):
    x, y, c = (lax.axis_index(a) for a in ("x", "y", "c"))
    sent = []

    def send(i, ref, axis, src=None):
        src = ref if src is None else src
        copy = remote(src, ref, sems.at[0, i], sems.at[1, i], axis)
        copy.start()
        sent.append(copy)

    def got(i, ref, axis):
        remote(ref, ref, sems.at[0, i], sems.at[1, i], axis).wait_recv()

    def begin():
        if own is None:
            own_ready()
        for i, axis in enumerate(("x", "y", "c")):
            send(i, region(x, y, c), axis, own)

    def forward():
        got(0, region(1 - x, y, c), "x")
        send(3, half(region(1 - x, y, c), 0), "y")
        send(4, region(1 - x, y, c), "c")
        got(1, region(x, 1 - y, c), "y")
        send(5, half(region(x, 1 - y, c), 1), "x")
        send(6, region(x, 1 - y, c), "c")

    def end():
        got(3, half(region(1 - x, 1 - y, c), 0), "y")
        got(5, half(region(1 - x, 1 - y, c), 1), "x")
        send(7, region(1 - x, 1 - y, c), "c")
        got(2, region(x, y, 1 - c), "c")
        got(4, region(1 - x, y, 1 - c), "c")
        got(6, region(x, 1 - y, 1 - c), "c")
        got(7, region(1 - x, 1 - y, 1 - c), "c")
        for copy in sent:
            copy.wait_send()
        if own is not None:
            own_ready()

    return begin, forward, end


def greet_all():
    barrier = pltpu.get_barrier_semaphore()
    x, z, y, c = (lax.axis_index(a) for a in ("x", "z", "y", "c"))
    n = lax.axis_size("z")

    def tell(where):
        pl.semaphore_signal(
            barrier, inc=1, device_id=where, device_id_type=pl.DeviceIdType.MESH
        )

    for where in ({"x": 1 - x}, {"y": 1 - y}, {"c": 1 - c}, {"y": 1 - y, "c": 1 - c}):
        tell(where)

    @pl.when(z >= 1)
    def _():
        tell({"z": z - 1})

    @pl.when(z + 1 < n)
    def _():
        tell({"z": z + 1})

    pl.semaphore_wait(barrier, 4 + jnp.minimum(z, 1) + jnp.minimum(n - 1 - z, 1))


def sum_scratch(count, width):
    half = width // 2
    return [
        pltpu.VMEM((2, 2, 2, count, half), BF),
        pltpu.VMEM((2, 2, count, half), BF),
        pltpu.VMEM((2, 2, count, half), BF),
        pltpu.VMEM((2, count, half), BF),
        pltpu.VMEM((2, count, half), BF),
        pltpu.SemaphoreType.DMA((2, 6)),
    ]


def reduce_plane(part, scratch):
    core, wide_in, wide_out, thin_in, thin_out, sems = scratch
    half = part.shape[4] // 2
    x, y, c = (lax.axis_index(a) for a in ("x", "y", "c"))
    firsts, seconds = ("y", "x"), ("x", "y")
    cols = [slice(0, half), slice(half, 2 * half)]

    def chip(i, yy, xx):
        return part[yy, c, xx, :, cols[i]].astype(F32) + core[i, yy, xx].astype(F32)

    def kept(i, index):
        mine = chip(i, y, index) if i == 0 else chip(i, index, x)
        return mine + wide_in[i, index].astype(F32)

    copies = [
        remote(part.at[:, 1 - c, :, :, cols[i]], core.at[i], sems.at[0, i], sems.at[1, i], "c")
        for i in (0, 1)
    ]
    wides = [
        remote(wide_out.at[i], wide_in.at[i], sems.at[0, 2 + i], sems.at[1, 2 + i], firsts[i])
        for i in (0, 1)
    ]
    thins = [
        remote(thin_out.at[i], thin_in.at[i], sems.at[0, 4 + i], sems.at[1, 4 + i], seconds[i])
        for i in (0, 1)
    ]

    def begin():
        for copy in copies:
            copy.start()

    def wide():
        for i in (0, 1):
            copies[i].wait()
            for k in (0, 1):
                wide_out[i, k] = (chip(i, 1 - y, k) if i == 0 else chip(i, k, 1 - x)).astype(BF)
            wides[i].start()

    def thin():
        for i in (0, 1):
            wides[i].wait()
            thin_out[i] = kept(i, 1 - x if i == 0 else 1 - y).astype(BF)
            thins[i].start()

    def end():
        outs = []
        for i in (0, 1):
            thins[i].wait()
            outs.append(kept(i, x if i == 0 else y) + thin_in[i].astype(F32))
        return jnp.concatenate(outs, axis=1)

    return begin, wide, thin, end


def gathered(block, out, sems, local):
    x, y, c = (lax.axis_index(a) for a in ("x", "y", "c"))
    half = block.shape[0] // 2
    own = pltpu.make_async_copy(block, out.at[y, c, x], local)
    own.start()
    steps = gather_regions(
        lambda x, y, c: out.at[y, c, x],
        lambda ref, i: ref.at[pl.ds(i * half, half)],
        sems,
        own.wait,
        block,
    )
    return steps


def factor_of(values):
    return lax.rsqrt(jnp.mean(values * values, axis=1, keepdims=True) + EPSILON)


def norm_back_parts(values, scaling, grad):
    factor = factor_of(values)
    normal = values * factor
    scaled = grad * scaling
    inner = jnp.mean(scaled * normal, axis=1, keepdims=True)
    return factor * (scaled - normal * inner), jnp.sum(grad * normal, axis=0, keepdims=True)


def middle_kernel(
    part_ref, rows_ref, gain_ref, down_ref, out_ref, middle_ref, whole_ref,
    block, sems, local, down_sems, *scratch,
):
    z, n = lax.axis_index("z"), lax.axis_size("z")
    greet_all()
    begin, wide, thin, end = reduce_plane(part_ref, scratch)
    begin()
    own = pltpu.make_async_copy(down_ref, whole_ref.at[z], local.at[1])
    own.start()
    send, arrive, finish = line_item(lambda at: whole_ref.at[at], down_sems, down_ref)
    send(0)

    def more(k):
        if k < n:
            arrive(k - 1)
        if k < n - 1:
            send(k)

    wide()
    more(1)
    thin()
    middle = rows_ref[...].astype(F32) + end()
    middle_ref[...] = middle
    block[...] = (middle * factor_of(middle) * gain_ref[...]).astype(BF)
    first, *steps = gathered(block, out_ref, sems, local.at[0])
    first()
    more(2)
    for step in steps:
        step()
    for k in range(3, n):
        more(k)
    own.wait()
    finish()


def middle_back_kernel(
    part_ref, rows_ref, gain_ref, cot_ref, out_ref, grad_ref, gain_grad_ref,
    block, sems, local, *scratch,
):
    greet(("x", "y", "c"))
    begin, wide, thin, end = reduce_plane(part_ref, scratch)
    begin()
    wide()
    thin()
    grad, gain_grad_ref[...] = norm_back_parts(rows_ref[...], gain_ref[...], end())
    grad = grad + cot_ref[...].astype(F32)
    grad_ref[...] = grad
    block[...] = grad.astype(BF)
    for step in gathered(block, out_ref, sems, local.at[0]):
        step()


def middle_calls(part, rows, gain, down=None, cot=None):
    n = lax.axis_size("z")
    count, width = rows.shape
    vmem, hbm = pl.BlockSpec(memory_space=pltpu.VMEM), pl.BlockSpec(memory_space=pl.ANY)
    dma = pltpu.SemaphoreType.DMA
    out = [jax.ShapeDtypeStruct((2, 2, 2, count, width), BF), jax.ShapeDtypeStruct((count, width), F32)]
    scratch = [pltpu.VMEM((count, width), BF), dma((2, 8)), dma((2,))]
    if cot is None:
        inputs, specs = [part, rows, gain, down], [vmem] * 3 + [hbm]
        out += [jax.ShapeDtypeStruct((n,) + down.shape, BF)]
        out_specs = [hbm, vmem, hbm]
        scratch += [dma((2, 2, n))]
    else:
        inputs, specs = [part, rows, gain, cot], [vmem] * 4
        out += [jax.ShapeDtypeStruct((1, width), F32)]
        out_specs = [hbm, vmem, vmem]
    return pl.pallas_call(
        middle_kernel if cot is None else middle_back_kernel,
        in_specs=specs,
        out_specs=out_specs,
        out_shape=out,
        scratch_shapes=scratch + sum_scratch(count, width),
        compiler_params=pltpu.CompilerParams(
            collective_id=1 if cot is None else 2, has_side_effects=True, vmem_limit_bytes=VMEM
        ),
        name="middle" if cot is None else "middle_back",
    )(*inputs)


def total_kernel(value_ref, out_ref, got, sems):
    greet(("c", "y", "x"))
    out_ref[...] = value_ref[...]
    for i, axis in enumerate(("c", "y", "x")):
        hop = remote(out_ref, got.at[i], sems.at[0, i], sems.at[1, i], axis)
        hop.start()
        hop.wait()
        out_ref[...] = out_ref[...] + got[i]


def plane_total(value, identity):
    vmem = pl.BlockSpec(memory_space=pltpu.VMEM)
    return pl.pallas_call(
        total_kernel,
        in_specs=[vmem],
        out_specs=vmem,
        out_shape=jax.ShapeDtypeStruct(value.shape, F32),
        scratch_shapes=[pltpu.VMEM((3,) + value.shape, F32), pltpu.SemaphoreType.DMA((2, 3))],
        compiler_params=pltpu.CompilerParams(collective_id=identity, has_side_effects=True),
        name="total",
    )(value)


def line_sum(own, inbox, sems):
    z, n = lax.axis_index("z"), lax.axis_size("z")

    def copy(way, k):
        d = k if way else n - 1 - k
        slot = jnp.where(d == z - 1, n, d) if way else d
        return pltpu.make_async_remote_copy(
            src_ref=own(d),
            dst_ref=inbox(slot),
            send_sem=sems.at[0, way, k],
            recv_sem=sems.at[1, way, k],
            device_id={"z": z + 1 - 2 * way},
            device_id_type=pl.DeviceIdType.MESH,
        )

    def add(way, k, d, slot):
        pltpu.make_async_remote_copy(
            src_ref=own(d),
            dst_ref=inbox(slot),
            send_sem=sems.at[0, way, k],
            recv_sem=sems.at[1, way, k],
            device_id={"z": z},
            device_id_type=pl.DeviceIdType.MESH,
        ).wait_recv()
        held = own(d)
        held[...] = (held[...].astype(F32) + inbox(slot)[...].astype(F32)).astype(held.dtype)

    def kick(k):
        @pl.when(z == 0)
        def _():
            copy(0, k).start()

        @pl.when(z == n - 1)
        def _():
            copy(1, k).start()

    def pass_on(way, k):
        d = k if way else n - 1 - k

        @pl.when((z > 0) & (z < n - 1) & (d < z if way else d > z))
        def _():
            add(way, k, d, d)
            copy(way, k).start()

    def end():
        @pl.when(z > 0)
        def _():
            add(0, n - 1 - z, z, z)

        @pl.when(z < n - 1)
        def _():
            add(1, z, z, n)

    def finish():
        for k in range(n - 1):
            for way in (0, 1):
                d = k if way else n - 1 - k

                @pl.when(d < z if way else d > z)
                def _(way=way):
                    copy(way, k).wait_send()

    return kick, pass_on, end, finish


def last_kernel(
    part_ref, rows_ref, gain_ref, grad_ref, little_ref, down_ref, middle_ref, weight_ref, slice_ref, cross_ref,
    out_ref, little_out, result_ref, got_ref, crossed_ref,
    held, inbox, swap, little, little_in, little_c, little_y, little_box,
    local, weight_sems, little_sems, hop_sems, swap_sems, got_sems, own_sems, cross_sems, *scratch,
):
    x, z, y, c = (lax.axis_index(a) for a in ("x", "z", "y", "c"))
    n = lax.axis_size("z")
    greet_all()
    cut = weight_ref.shape[4]
    loads = []
    for i, (ref, at) in enumerate(((weight_ref, 0), (slice_ref, cut))):
        into = held.at[:, :, :, :, pl.ds(at, ref.shape[4])]
        loads.append(pltpu.make_async_copy(ref, into, local.at[i]))
        loads[i].start()
    half = len(scratch) // 2
    begin, wide, thin, end = reduce_plane(part_ref, scratch[:half])
    begin_down, wide_down, thin_down, end_down = reduce_plane(down_ref, scratch[half:])
    begin()
    begin_down()
    for load in loads:
        load.wait()

    order = ((1, 1), (1, 0), (0, 1), (0, 0))
    sums, places = [], []
    for i, (dy, dc) in enumerate(order):
        yy, cc = (1 - y) if dy else y, (1 - c) if dc else c
        places.append((yy, cc))
        sums.append(
            line_sum(
                lambda d, yy=yy, cc=cc: held.at[d, yy, cc],
                lambda d, yy=yy, cc=cc: inbox.at[d, yy, cc],
                weight_sems.at[i],
            )
        )
    for k in range(n - 1):
        for item in sums:
            item[0](k)
    wide()
    wide_down()

    def pass_all(k):
        for item in sums:
            for near in (0, 1):

                @pl.when(z < n // 2)
                def _():
                    item[1](near, k)

                @pl.when(z >= n // 2)
                def _():
                    item[1](1 - near, k)

    pass_all(0)
    thin()
    thin_down()
    cross = remote(cross_ref, crossed_ref, cross_sems.at[0], cross_sems.at[1], "x")
    cross.start()
    for k in range(1, n - 1):
        pass_all(k)

    result_ref[...] = (middle_ref[...] + end_down()).astype(BF)
    rows = rows_ref[...].astype(F32)
    grad, gain_grad = norm_back_parts(rows, gain_ref[...], end())
    out_ref[...] = grad + grad_ref[...]

    little[...] = little_ref[...]
    piece = rows.shape[1] // (4 * n)
    for at in range(n):
        for yy in (0, 1):
            for cc in (0, 1):
                first = (4 * at + 2 * yy + cc) * piece
                little[at, yy, cc, 0:1, 0:piece] = gain_grad[:, first : first + piece]
    hop = remote(little, little_in, hop_sems.at[0, 0], hop_sems.at[1, 0], "x")
    hop.start()
    hop.wait()
    little[...] = little[...] + little_in[...]
    hop = remote(little.at[:, :, 1 - c], little_c, hop_sems.at[0, 1], hop_sems.at[1, 1], "c")
    hop.start()
    hop.wait()
    for yy in (0, 1):
        little_c[:, yy] = little_c[:, yy] + little[:, yy, c]
    hop = remote(little_c.at[:, 1 - y], little_y, hop_sems.at[0, 2], hop_sems.at[1, 2], "y")
    hop.start()
    hop.wait()
    little_y[...] = little_y[...] + little_c[:, y]
    little_sum = line_sum(lambda d: little_y.at[d], lambda d: little_box.at[d], little_sems)
    for k in range(n - 1):
        little_sum[0](k)
    for k in range(n - 1):
        for way in (0, 1):
            little_sum[1](way, k)
    little_sum[2]()
    little_out[...] = little_y[z]

    moves, crossed, kept = [], [], []

    def forward(i):
        yy, cc = places[i]
        if i < 3:
            moves[i].wait_recv()
        keep = pltpu.make_async_copy(swap.at[cc, yy], got_ref.at[x, cc, yy], own_sems.at[i])
        keep.start()
        kept.append(keep)
        move = remote(
            swap.at[cc, yy], got_ref.at[x, cc, yy], got_sems.at[0, i], got_sems.at[1, i], "x"
        )
        move.start()
        crossed.append(move)

    for i, (yy, cc) in enumerate(places):
        sums[i][2]()
        if i < 3:
            move = pltpu.make_async_remote_copy(
                src_ref=held.at[z, yy, cc],
                dst_ref=swap.at[c, y],
                send_sem=swap_sems.at[0, i],
                recv_sem=swap_sems.at[1, i],
                device_id={"y": yy, "c": cc},
                device_id_type=pl.DeviceIdType.MESH,
            )
            move.start()
            moves.append(move)
        else:
            swap[c, y] = held[z, yy, cc]
        if i > 0:
            forward(i - 1)
    forward(3)
    cross.wait()
    for copy in kept + crossed:
        copy.wait()
    for move in moves:
        move.wait_send()
    for item in sums + [little_sum]:
        item[3]()


def last_call(part, rows, gain, grad, little, down, middle, weight, slices, cross):
    n = lax.axis_size("z")
    count, width = rows.shape
    block, pack = (weight.shape[3], weight.shape[4] + slices.shape[4]), little.shape[3:]
    vmem, hbm = pl.BlockSpec(memory_space=pltpu.VMEM), pl.BlockSpec(memory_space=pl.ANY)
    dma = pltpu.SemaphoreType.DMA
    return pl.pallas_call(
        last_kernel,
        in_specs=[vmem] * 7 + [hbm] * 3,
        out_specs=[vmem, vmem, vmem, hbm, hbm],
        out_shape=[
            jax.ShapeDtypeStruct((count, width), F32),
            jax.ShapeDtypeStruct(pack, F32),
            jax.ShapeDtypeStruct((count, width), BF),
            jax.ShapeDtypeStruct((2, 2, 2) + block, BF),
            jax.ShapeDtypeStruct(cross.shape, BF),
        ],
        scratch_shapes=[
            pltpu.VMEM((n, 2, 2) + block, BF),
            pltpu.VMEM((n + 1, 2, 2) + block, BF),
            pltpu.VMEM((2, 2) + block, BF),
            pltpu.VMEM((n, 2, 2) + pack, F32),
            pltpu.VMEM((n, 2, 2) + pack, F32),
            pltpu.VMEM((n, 2) + pack, F32),
            pltpu.VMEM((n,) + pack, F32),
            pltpu.VMEM((n + 1,) + pack, F32),
            dma((2,)),
            dma((4, 2, 2, n)),
            dma((2, 2, n)),
            dma((2, 3)),
            dma((2, 3)),
            dma((2, 4)),
            dma((4,)),
            dma((2,)),
        ]
        + sum_scratch(count, width)
        + sum_scratch(count, width),
        compiler_params=pltpu.CompilerParams(
            collective_id=3, has_side_effects=True, vmem_limit_bytes=60 * 1024 * 1024
        ),
        name="last",
    )(part, rows, gain, grad, little, down, middle, weight, slices, cross)


def start_kernel(
    rows_ref, little_ref, own_ref, blocks_ref, cot_ref,
    hidden_ref, all_ref, shared_ref, weight_ref, incoming_ref,
    block, little, hidden_sems, shared_sems, cot_sems, local, little_sems, line_sems, across_sems,
):
    x, z, y, c = (lax.axis_index(a) for a in ("x", "z", "y", "c"))
    n = lax.axis_size("z")
    greet_all()
    width = own_ref.shape[1]

    def shared_at(x, z, y, c):
        cols = pl.ds(pl.multiple_of(x * width, 128), width)
        return shared_ref.at[z, y, c, :, cols]

    own_shared = pltpu.make_async_copy(own_ref, shared_at(x, z, y, c), local.at[0])
    own_shared.start()
    own_weight = pltpu.make_async_copy(blocks_ref.at[c, y], weight_ref.at[z, y, c], local.at[1])
    own_weight.start()
    own_cot = pltpu.make_async_copy(cot_ref, incoming_ref.at[y, c, x], local.at[3])
    own_cot.start()

    shared_line = line_item(lambda at: shared_at(x, at, y, c), line_sems.at[0], own_ref)
    little_line = line_item(lambda at: little.at[at], line_sems.at[1])
    shared_line[0](0)
    little[z, y, c] = little_ref[...]
    hop = remote(little.at[z, y, c], little.at[z, y, c], little_sems.at[0, 0], little_sems.at[1, 0], "c")
    hop.start()

    moves = []
    for i, (dy, dc) in enumerate(((0, 1), (1, 0), (1, 1))):
        where = {"y": (1 - y) if dy else y, "c": (1 - c) if dc else c}
        src = blocks_ref.at[where["c"], where["y"]]
        move = pltpu.make_async_remote_copy(
            src_ref=src,
            dst_ref=weight_ref.at[z, y, c],
            send_sem=across_sems.at[0, i],
            recv_sem=across_sems.at[1, i],
            device_id=where,
            device_id_type=pl.DeviceIdType.MESH,
        )
        move.start()
        moves.append(move)

    lines = []
    for i, (dy, dc) in enumerate(((0, 0), (0, 1), (1, 0), (1, 1))):
        yy, cc = (1 - y) if dy else y, (1 - c) if dc else c
        lines.append(
            line_item(
                lambda at, yy=yy, cc=cc: weight_ref.at[at, yy, cc],
                line_sems.at[2 + i],
                blocks_ref.at[c, y] if i == 0 else None,
            )
        )
    lines[0][0](0)
    hop.wait()
    second = remote(little.at[z, y], little.at[z, y], little_sems.at[0, 1], little_sems.at[1, 1], "y")
    second.start()
    second.wait()
    little_line[0](0)
    for k in range(1, n):
        shared_line[1](k - 1)
        if k < n - 1:
            shared_line[0](k)
        little_line[1](k - 1)
        if k < n - 1:
            little_line[0](k)
    for i in range(3):
        moves[i].wait_recv()
        lines[1 + i][0](0)

    rows = rows_ref[...].astype(F32)
    rows = rows * factor_of(rows)
    piece = rows.shape[1] // (4 * n)
    gain = jnp.concatenate(
        [
            little[at, yy, cc, 0:1, 0:piece]
            for at in range(n)
            for yy in (0, 1)
            for cc in (0, 1)
        ],
        axis=1,
    )
    block[...] = (rows * gain).astype(BF)
    all_ref[...] = little[...]
    count = rows.shape[0]
    own_hidden = pltpu.make_async_copy(block, hidden_ref.at[y, c, x], local.at[2])
    own_hidden.start()

    hidden_steps = gather_regions(
        lambda x, y, c: hidden_ref.at[y, c, x],
        lambda ref, i: ref.at[pl.ds(i * (count // 2), count // 2)],
        hidden_sems,
        own_hidden.wait,
        block,
    )

    def shared_region(x, y, c):
        cols = pl.ds(pl.multiple_of(x * width, 128), width)
        return shared_ref.at[:, y, c, :, cols]

    shared_steps = gather_regions(
        shared_region,
        lambda ref, i: ref.at[pl.ds(i * (n // 2), n // 2)],
        shared_sems,
        own_shared.wait,
    )
    cot_steps = gather_regions(
        lambda x, y, c: incoming_ref.at[y, c, x],
        lambda ref, i: ref.at[pl.ds(i * (count // 2), count // 2)],
        cot_sems,
        own_cot.wait,
        cot_ref,
    )
    hidden_steps[0]()
    shared_steps[0]()
    cot_steps[0]()
    for k in range(1, n):
        for send, arrive, finish in lines:
            arrive(k - 1)
            if k < n - 1:
                send(k)
        if k == 1:
            hidden_steps[1]()
            shared_steps[1]()
    cot_steps[1]()
    hidden_steps[2]()
    shared_steps[2]()
    cot_steps[2]()
    own_weight.wait()
    for move in moves:
        move.wait_send()
    for send, arrive, finish in [shared_line, little_line] + lines:
        finish()


def start_call(rows, little, own, blocks, cot):
    n, parts = lax.axis_size("z"), blocks.shape
    count, width = rows.shape
    vmem, hbm = pl.BlockSpec(memory_space=pltpu.VMEM), pl.BlockSpec(memory_space=pl.ANY)
    dma = pltpu.SemaphoreType.DMA
    return pl.pallas_call(
        start_kernel,
        in_specs=[vmem, vmem, hbm, hbm, hbm],
        out_specs=[hbm, vmem, hbm, hbm, hbm],
        out_shape=[
            jax.ShapeDtypeStruct((2, 2, 2, count, width), BF),
            jax.ShapeDtypeStruct((n, 2, 2) + little.shape, F32),
            jax.ShapeDtypeStruct((n, 2, 2, own.shape[0], 2 * own.shape[1]), BF),
            jax.ShapeDtypeStruct((n, 2, 2) + parts[2:], BF),
            jax.ShapeDtypeStruct((2, 2, 2, count, width), BF),
        ],
        scratch_shapes=[
            pltpu.VMEM((count, width), BF),
            pltpu.VMEM((n, 2, 2) + little.shape, F32),
            dma((2, 8)),
            dma((2, 8)),
            dma((2, 8)),
            dma((4,)),
            dma((2, 2)),
            dma((6, 2, 2, n - 1)),
            dma((2, 3)),
        ],
        compiler_params=pltpu.CompilerParams(
            collective_id=0, has_side_effects=True, vmem_limit_bytes=VMEM
        ),
        name="start",
    )(rows, little, own, blocks, cot)


def flip(value, *axes):
    count = 2 ** len(axes)
    pairs = [(i, count - 1 - i) for i in range(count)]
    axes = tuple(sorted(axes, key=MESH_AXES.index))
    return lax.ppermute(value, axes, pairs)


def ordered(own, other, axis):
    second = lax.axis_index(axis) == 1
    return jnp.where(second, other, own), jnp.where(second, own, other)


def column_halves(values, axis):
    at = lax.axis_index(axis)
    halves = [v.shape[1] // 2 for v in values]
    kept = [lax.dynamic_slice_in_dim(v, at * h, h, 1) for v, h in zip(values, halves)]
    away = [lax.dynamic_slice_in_dim(v, (1 - at) * h, h, 1) for v, h in zip(values, halves)]
    return kept, jnp.concatenate([v.astype(BF) for v in away], axis=1)


def column_added(kept, got):
    sums, at = [], 0
    for v in kept:
        sums.append(v.astype(F32) + got[:, at : at + v.shape[1]].astype(F32))
        at += v.shape[1]
    return sums


def part_index():
    return 4 * lax.axis_index("x") + 2 * lax.axis_index("c") + lax.axis_index("y")


def half_columns(weight):
    half = weight.shape[1] // 2
    return lax.dynamic_slice_in_dim(weight, lax.axis_index("x") * half, half, 1)


def exchange(blocks, high, low):
    h, l = lax.axis_index(high), lax.axis_index(low)

    def block(dh, dl):
        return lax.dynamic_index_in_dim(blocks, 2 * (h ^ dh) + (l ^ dl), 0, keepdims=False)

    own, by_low = block(0, 0), flip(block(0, 1), low)
    by_high, by_both = flip(block(1, 0), high), flip(block(1, 1), high, low)
    near, far = ordered(own, by_low, low), ordered(by_high, by_both, low)
    first, second = ordered(near[0], far[0], high), ordered(near[1], far[1], high)
    return [[first[0], second[0]], [first[1], second[1]]]


def fetch_units(weights):
    rows, n = weights[0].shape[0], lax.axis_size("z")
    blocks = []
    for w in weights:
        units = w.reshape(rows, n, 2, 2, 2, -1)
        units = lax.dynamic_index_in_dim(units, lax.axis_index("x"), 4, keepdims=False)
        blocks.append(units.transpose(3, 2, 0, 1, 4).reshape(4, rows, -1))
    got = exchange(jnp.concatenate(blocks, axis=2), "c", "y")
    moved = jnp.concatenate([got[0][0], got[1][0], got[0][1], got[1][1]])
    return lax.all_gather(moved, "z", axis=0, tiled=True)


def exchange_units(part):
    rows = part.shape[0] // 4
    part = part.reshape(2, 2, rows, -1).transpose(1, 0, 2, 3).reshape(4, rows, -1)
    return jnp.stack([jnp.stack(g) for g in exchange(part, "c", "y")])


def unit_shards(own, across, count):
    n, rows = lax.axis_size("z"), own.shape[2]
    whole = jnp.stack(ordered(own, across, "x"))
    whole = whole.reshape(2, 2, 2, rows, count, n, -1).transpose(4, 3, 5, 2, 1, 0, 6)
    return [whole[i].reshape(rows, -1).astype(F32) for i in range(count)]


def fetch_rows(weight):
    if lax.axis_size("z") != 4:
        whole = lax.all_gather(weight, FSDP, axis=0, tiled=True)
        rows = whole.shape[0] // PARTS
        return lax.dynamic_slice_in_dim(whole, part_index() * rows, rows, 0)
    got = exchange(lax.all_gather(half_columns(weight), "z", axis=0, tiled=False), "x", "c")
    return jnp.concatenate(
        [jnp.concatenate([got[0][c], got[1][c]], axis=1) for c in (0, 1)], axis=0
    )


def fetch_rows_of(weights):
    if lax.axis_size("z") != 4:
        return jnp.concatenate([fetch_rows(w) for w in weights])
    pieces = [w.shape[0] for w in weights]
    whole, outs, at = fetch_rows(jnp.concatenate(weights)), [], 0
    whole = whole.reshape(2, sum(pieces), -1)
    for count in pieces:
        outs.append(whole[:, at : at + count].reshape(2 * count, -1))
        at += count
    return jnp.concatenate(outs)


def rows_moved(grad, pieces):
    cols = grad.shape[1] // 2
    splits = [grad[sum(pieces[:i]) : sum(pieces[: i + 1])].astype(BF) for i in range(len(pieces))]
    if lax.axis_size("z") != 4:
        parts = []
        for g in splits:
            whole = jnp.zeros((g.shape[0] * PARTS, 2 * cols), BF)
            parts.append(
                lax.dynamic_update_slice_in_dim(whole, g, part_index() * g.shape[0], 0)
            )
        return parts
    halves = jnp.concatenate([g.reshape(2, g.shape[0] // 2, -1) for g in splits], axis=1)
    block = halves.reshape(2, -1, 2, cols).transpose(2, 0, 1, 3)
    got = exchange(block.reshape(4, -1, cols), "x", "c")
    return jnp.stack([got[0][0], got[0][1], got[1][0], got[1][1]])


def rows_sum(moved, down):
    n, width = lax.axis_size("z"), down.shape[1] // 2
    down = down.reshape(n, -1, 2, width).transpose(0, 2, 1, 3).reshape(n, -1, width)
    if n != 4:
        parts = []
        for whole in moved:
            part = lax.psum_scatter(whole, FSDP, scatter_dimension=0, tiled=True)
            parts.append(half_columns(lax.psum(part, "x")))
        return jnp.concatenate(parts + [lax.psum_scatter(down, "z")])
    return lax.psum_scatter(jnp.concatenate([moved, down], axis=1), "z")


def after(value, earlier):
    return lax.optimization_barrier((value, earlier))[0]


def packed(first, arrays):
    lead = first.shape[0]
    flat = jnp.concatenate([a.reshape(lead, -1) for a in arrays], axis=1)
    flat = jnp.pad(flat, ((0, 0), (0, -(flat.shape[1] + 128) % 1024)))
    first = jnp.pad(first, ((0, 0), (0, 128 - first.shape[1])))
    return jnp.concatenate([first, flat], axis=1).reshape(lead, -1, 128)


def shards(
    tokens,
    cotangent,
    mixer_gain,
    query_weight,
    key_weight,
    value_weight,
    attn_out_weight,
    mamba_in_weight,
    conv_weight,
    conv_bias,
    decay_log,
    step_bias,
    skip_gain,
    mamba_gain,
    mamba_out_weight,
    ffn_gain,
    gate_weight,
    up_weight,
    down_weight,
):
    token_count, model_dim = tokens.shape[1], tokens.shape[2]
    length = 2 * token_count
    inner = MH * MP
    channels = inner + 2 * NST
    part = part_index()
    wide, heads = inner // PARTS, MH // PARTS
    rows = token_count * PARTS
    seqs = rows // length
    fsdp = lax.axis_size("z") * 4

    smalls = [ffn_gain, mamba_gain, conv_bias, conv_weight]
    little = packed(mixer_gain[None].astype(F32), [v[None].astype(F32) for v in smalls])[0]
    count = query_weight.shape[0]
    kvh = HD * lax.axis_index("x")
    map_weight, step_weight = mamba_in_weight[:, 2 * inner : 2 * inner + 2 * NST], mamba_in_weight[:, 2 * inner + 2 * NST :]
    own = jnp.concatenate(
        [
            half_columns(map_weight),
            lax.dynamic_slice_in_dim(key_weight, kvh, HD, 1),
            lax.dynamic_slice_in_dim(value_weight, kvh, HD, 1),
            jnp.pad(half_columns(step_weight), ((0, 0), (0, 128 - MH // 2))),
        ],
        axis=1,
    )
    blocks = [mamba_in_weight[:, :inner], mamba_in_weight[:, inner : 2 * inner], query_weight]
    blocks = [half_columns(w).reshape(count, 2, 2, -1) for w in blocks]
    blocks = jnp.concatenate(blocks, axis=3).transpose(1, 2, 0, 3)
    token_rows = tokens.reshape(token_count, model_dim)
    grad_rows = cotangent.reshape(token_count, model_dim)
    hidden, gathered_little, shared, w_in, incoming = start_call(
        token_rows, little, own, blocks, grad_rows
    )
    hidden = hidden.reshape(rows, model_dim)
    incoming = incoming.reshape(rows, model_dim)
    w_in = w_in.reshape(model_dim, -1)
    shared = shared.reshape(model_dim, -1)
    share = shared.shape[1] // 2
    shared = jnp.concatenate(
        [
            shared[:, :NST],
            shared[:, share : share + NST],
            lax.dynamic_slice_in_dim(shared, lax.axis_index("x") * share + NST, share - NST, 1),
        ],
        axis=1,
    )
    w_out = fetch_rows_of([attn_out_weight, mamba_out_weight])
    w_attn_out, w_mamba_out = w_out[:HD], w_out[HD:]
    w_gateup = fetch_units(after((gate_weight, up_weight), hidden))
    down_half = down_weight.reshape(2, -1, model_dim)
    down_half = lax.dynamic_index_in_dim(down_half, lax.axis_index("x"), 0, keepdims=False)
    ff = gate_weight.shape[1] // PARTS

    gathered_little = gathered_little.reshape(fsdp, -1)
    gain_in = gathered_little[:, : mixer_gain.size].reshape(-1)
    got, at = [], 128
    for s in smalls:
        got.append(gathered_little[:, at : at + s.size].reshape((fsdp,) + s.shape))
        at += s.size
    gain_ffn, gain_mamba, bias_full = (g.reshape(-1) for g in got[:3])
    conv_full = got[3].transpose(1, 0, 2).reshape(4, channels)
    gain_mamba = lax.dynamic_slice_in_dim(gain_mamba, part * wide, wide, 0)

    def own_heads(v):
        return lax.dynamic_slice_in_dim(v.astype(F32), part * heads, heads, 0)

    heads_rows = jnp.stack([own_heads(v) for v in (decay_log, step_bias, skip_gain)])
    heads_rows = jnp.pad(heads_rows, ((0, 5), (0, 2 * MP - heads)))
    params = [
        lax.dynamic_slice_in_dim(conv_full, part * wide, wide, 1),
        lax.dynamic_slice_in_dim(bias_full, part * wide, wide, 0)[None],
        conv_full[:, inner:],
        bias_full[None, inner:],
        heads_rows,
    ]
    tables = rope_tables(length, HD)

    projected = mm(hidden, w_in)
    common = mm(hidden, shared).astype(BF)
    scanned, gated, squares, attended = mixer_forward(
        seqs, length, projected, common, params, tables
    )

    squares = plane_total(squares.reshape(-1, 128), 4)
    factor = lax.rsqrt(squares / inner + EPSILON).reshape(rows, 1)
    normal = gated * factor
    normed = (normal * gain_mamba).astype(BF)
    mixed = jnp.concatenate([attended, normed], axis=1)
    w_out = jnp.concatenate([w_attn_out, w_mamba_out], axis=0)
    block = (2, 2, 2, token_count, model_dim)
    mixer_sum = mm(mixed, w_out).astype(BF).reshape(block)
    second, middle, w_down = middle_calls(mixer_sum, token_rows, gain_ffn[None], down_half)
    w_down = w_down.reshape(ff, model_dim)
    second = second.reshape(rows, model_dim)
    gate_up = mm(second, w_gateup)
    gate_act, up_act = gate_up[:, :ff], gate_up[:, ff:]
    sig_g = jax.nn.sigmoid(gate_act)
    active = (gate_act * sig_g * up_act).astype(BF)

    grad_active = across(incoming, w_down)
    grad_gate = grad_active * up_act * sig_g * (1.0 + gate_act * (1.0 - sig_g))
    grad_up = grad_active * gate_act * sig_g
    grad_gateup = jnp.concatenate([grad_gate.astype(BF), grad_up.astype(BF)], axis=1)
    grad_wgateup = outer_product(second, grad_gateup)
    sum_gateup = lax.psum_scatter(grad_wgateup.astype(BF).reshape(-1, 4 * count, 2 * ff), "z")
    grad_second = across(grad_gateup, w_gateup).astype(BF).reshape(block)
    grad_mixer, grad_middle, grad_gain_ffn = middle_calls(
        grad_second, middle, gain_ffn[None], cot=grad_rows
    )
    grad_mixer = grad_mixer.reshape(rows, model_dim)
    grad_out = outer_product(mixed, grad_mixer)
    moved_out = rows_moved(grad_out, [HD, wide])
    grad_mixer, active = after((grad_mixer, active), grad_out)
    grad_down = outer_product(active, incoming).astype(BF)
    grad_mixer, active = after((grad_mixer, active), grad_down)
    sum_rows = rows_sum(moved_out, grad_down)
    grad_att = across(grad_mixer, w_attn_out).astype(BF)
    grad_normed = across(grad_mixer, w_mamba_out)
    grad_gain_mamba = jnp.sum(grad_normed * normal, axis=0)
    scaled = grad_normed * gain_mamba
    dots = jnp.sum(scaled * normal, axis=-1).reshape(-1, 128)
    if isinstance(moved_out, jax.Array):
        dots = after(dots, moved_out)
    dots = plane_total(dots, 5).reshape(rows, 1) / inner
    grad_in, grad_common, gxk, gxb, gmk, gmb, gheads = mixer_backward(
        seqs, length, projected, common, params, tables, scanned, grad_normed, gain_mamba[None],
        factor, dots, grad_att,
    )
    shares = [grad_common[:, : 2 * NST], grad_common[:, 2 * NST : 2 * NST + 2 * HD]]
    kept, away = column_halves(shares, "c")
    grad_hidden = across(after(grad_in, away), w_in)
    shares = column_added(kept, flip(away, "c"))
    kept, away = column_halves(shares, "y")
    grad_hidden = grad_hidden + across(after(grad_common, away), shared)
    grad_hidden = grad_hidden.astype(BF).reshape(block)
    shares = column_added(kept, flip(away, "y"))
    kept, away = column_halves(shares[:1], "x")
    grad_win = outer_product(hidden, after(grad_in, (away, grad_hidden))).astype(BF)
    grad_win = grad_win.reshape(-1, 2, 2, count, grad_win.shape[1])
    shares = [shares[1]] + column_added(kept, flip(away, "x"))
    slices = [v.astype(BF) for v in shares] + [grad_common[:, 2 * NST + 2 * HD :]]
    grad_slices = outer_product(hidden, jnp.concatenate(slices, axis=1)).astype(BF)
    grad_slices = grad_slices.reshape(-1, 2, 2, count, grad_slices.shape[1])
    result = mm(active, w_down).astype(BF).reshape(block)

    conv_grad = jnp.zeros((4, channels), F32)
    conv_grad = lax.dynamic_update_slice_in_dim(conv_grad, gxk, part * wide, 1)
    conv_grad = conv_grad.at[:, inner:].set(gmk)
    bias_grad = jnp.zeros((channels,), F32)
    bias_grad = lax.dynamic_update_slice_in_dim(bias_grad, gxb[0], part * wide, 0)
    bias_grad = bias_grad.at[inner:].set(gmb[0])
    gain_grad = lax.dynamic_update_slice_in_dim(
        jnp.zeros((inner,), F32), grad_gain_mamba, part * wide, 0
    )
    head_grad = lax.dynamic_update_slice_in_dim(
        jnp.zeros((3, MH), F32), gheads[:3, :heads], part * heads, 1
    )
    scattered = [grad_gain_ffn, gain_grad, bias_grad]
    little = [v.reshape(fsdp, -1) for v in scattered]
    little.append(conv_grad.reshape(4, fsdp, -1).transpose(1, 0, 2).reshape(fsdp, -1))
    little.append(jnp.broadcast_to(head_grad.reshape(1, -1), (fsdp, 3 * MH)))
    little = packed(jnp.zeros((fsdp, count), F32), little)
    little = little.reshape((-1, 2, 2) + little.shape[1:])
    moved = exchange_units(sum_gateup)
    moved = after(moved, grad_in)
    moved_across = flip(moved, "x")
    grad_hidden = after(grad_hidden, moved_across)
    tokens_grad, total, output, got_in, rows_across = last_call(
        grad_hidden, token_rows, gain_in[None], grad_middle, little, result, middle, grad_win,
        grad_slices, sum_rows,
    )
    output = output.reshape(1, token_count, model_dim)
    tokens_grad = tokens_grad.reshape(1, token_count, model_dim)
    total = total.reshape(-1)
    got, at = [total[:count]], 128
    for like in (ffn_gain, mamba_gain, conv_bias, conv_weight, head_grad):
        got.append(total[at : at + like.size].reshape(like.shape))
        at += like.size

    shard_gate, shard_up = unit_shards(moved, moved_across, 2)
    low, high = ordered(sum_rows, rows_across, "x")
    out_rows = sum_rows.shape[0] - ff // lax.axis_size("z") * model_dim // sum_rows.shape[1]
    shard_out = jnp.concatenate([low[:out_rows], high[:out_rows]], axis=1).astype(F32)
    shard_attn_out = shard_out[: attn_out_weight.shape[0]]
    shard_mamba_out = shard_out[attn_out_weight.shape[0] :]
    shard_down = jnp.concatenate([low[out_rows:], high[out_rows:]]).astype(F32)
    shard_down = shard_down.reshape(2, 2, -1, model_dim // 2).transpose(0, 2, 1, 3)
    shard_down = shard_down.reshape(-1, model_dim)

    def columns(first, width):
        return got_in[..., first : first + width]

    def by_part(first, width):
        return columns(first, width).transpose(3, 0, 1, 2, 4).reshape(count, -1)

    at = HD + 2 * wide
    kv = columns(at, HD // 2).transpose(1, 3, 0, 2, 4)
    mapped = columns(at + HD // 2, NST // 4).transpose(3, 1, 2, 0, 4).reshape(count, -1)
    stepped = columns(at + HD // 2 + NST // 4, MH // 2).astype(F32).sum(axis=(1, 2))
    stepped = stepped.transpose(1, 0, 2).reshape(count, -1)
    shard_query = by_part(2 * wide, HD).astype(F32)
    shard_key, shard_value = (kv[i].reshape(count, -1).astype(F32) for i in (0, 1))
    shard_mamba_in = jnp.concatenate(
        [v.astype(F32) for v in (by_part(0, wide), by_part(wide, wide), mapped, stepped)], axis=1
    )

    return (
        output,
        tokens_grad,
        got[0],
        shard_query,
        shard_key,
        shard_value,
        shard_attn_out,
        shard_mamba_in,
        got[4],
        got[3],
        got[5][0],
        got[5][1],
        got[5][2],
        got[2],
        shard_mamba_out,
        got[1],
        shard_gate,
        shard_up,
        shard_down,
    )


def solution(mesh):
    fsdp = mesh.shape["fsdp"]
    grid = Mesh(mesh.devices.reshape(2, fsdp // 4, 2, 2), ("x", "z", "y", "c"))
    rows, flat, whole = P(FSDP, None), P(FSDP), P()
    stream = P(FSDP, "x", None)
    weights = (
        flat, rows, rows, rows, rows, rows, P(None, FSDP), flat, whole, whole, whole,
        flat, rows, flat, rows, rows, rows,
    )
    return jax.shard_map(
        shards,
        mesh=grid,
        in_specs=(stream, stream) + weights,
        out_specs=(stream, stream) + weights,
        check_vma=False,
    )
```

```python
import math

import jax
import jax.numpy as jnp
from jax import lax
from jax.experimental import pallas as pl
from jax.experimental.pallas import tpu as pltpu
from jax.sharding import Mesh
from jax.sharding import PartitionSpec as P

HQ = 8
KVH = 2
HD = 128
MH = 48
MP = 64
NST = 256
EPSILON = 1e-05
ROPE_BASE = 100000000000.0
MASKED = -1e30
BF = jnp.bfloat16
F32 = jnp.float32
MESH_AXES = ("x", "z", "y", "c")
FSDP = ("z", "y", "c")
PARTS = 8
VMEM = 48 * 1024 * 1024


def mm(left, right):
    return jnp.dot(left, right, preferred_element_type=F32)


def outer_product(left, right):
    return lax.dot_general(left, right, (((0,), (0,)), ((), ())), preferred_element_type=F32)


def across(left, right):
    return lax.dot_general(left, right, (((1,), (1,)), ((), ())), preferred_element_type=F32)


def rope_tables(length, head_size):
    half_size = head_size // 2
    frequency = jnp.exp(
        jnp.arange(half_size, dtype=F32) * (-2.0 * math.log(ROPE_BASE) / head_size)
    )
    angles = jnp.arange(length, dtype=F32)[:, None] * frequency[None, :]
    cosine, sine = jnp.cos(angles), jnp.sin(angles)
    return [jnp.concatenate(v, axis=1) for v in ([cosine, cosine], [-sine, sine])]


def silu_parts(values):
    sig = 1.0 / (1.0 + jnp.exp(-values))
    return values * sig, sig


def shifted(values, count):
    if count == 0:
        return values
    rows = values.shape[0]
    at = lax.broadcasted_iota(jnp.int32, values.shape, 0)
    kept = (at >= count) if count > 0 else (at < rows + count)
    return jnp.where(kept, pltpu.roll(values, count % rows, 0), 0.0)


def conv_silu(signal, kernel, bias):
    taps = kernel.shape[0]
    total = bias + signal * kernel[taps - 1 : taps]
    for back in range(1, taps):
        total = total + shifted(signal, back) * kernel[taps - 1 - back : taps - back]
    value, sig = silu_parts(total)
    return value, sig * (1.0 + total * (1.0 - sig))


def conv_grads(signal, kernel, grad):
    taps = kernel.shape[0]
    back = grad * kernel[taps - 1 : taps]
    rows = []
    for count in range(taps - 1, 0, -1):
        rows.append(jnp.sum(shifted(signal, count) * grad, axis=0, keepdims=True))
        back = back + shifted(grad, -count) * kernel[taps - 1 - count : taps - count]
    rows.append(jnp.sum(signal * grad, axis=0, keepdims=True))
    return back, jnp.concatenate(rows, axis=0), jnp.sum(grad, axis=0, keepdims=True)


def dot(left, right, dims=((1,), (0,)), precision=None):
    return lax.dot_general(
        left, right, (dims, ((), ())), preferred_element_type=F32, precision=precision
    )


ROWS = ((0,), (0,))
LANES = ((1,), (1,))
PRECISE = lax.Precision.HIGHEST


def step_place():
    return (MH // PARTS) * (2 * lax.axis_index("c") + lax.axis_index("y"))


def scan_parts(x_ref, m_refs, s_ref, xk_ref, xb_ref, mk_ref, mb_ref, h_ref):
    length = x_ref.shape[0]
    xin = x_ref[...].astype(BF).astype(F32)
    maps = jnp.concatenate([ref[...].astype(BF).astype(F32) for ref in m_refs], axis=1)
    xs, xslope = conv_silu(xin, xk_ref[...], xb_ref[...])
    mv, mslope = conv_silu(maps, mk_ref[...], mb_ref[...])
    mv = mv.astype(BF)
    bees, cees = mv[:, :NST], mv[:, NST:]
    raw = pltpu.roll(s_ref[...].astype(BF).astype(F32), 2 * MP - step_place(), 1) + h_ref[1:2]
    dt = jnp.maximum(raw, 0.0) + jnp.log1p(jnp.exp(-jnp.abs(raw)))
    rate = -jnp.exp(h_ref[0:1])
    t = lax.broadcasted_iota(jnp.int32, (length, length), 0)
    s = lax.broadcasted_iota(jnp.int32, (length, length), 1)
    lower = (t >= s).astype(F32)
    cum = dot(lower, dt * rate, precision=PRECISE)
    coupling = dot(cees, bees, LANES)
    return xin, maps, xs, xslope, mslope, bees, cees, raw, dt, rate, lower, cum, coupling


def lane_pair(values, first):
    lane = lax.broadcasted_iota(jnp.int32, (values.shape[0], 2 * MP), 1)
    return jnp.where(lane < MP, values[:, first : first + 1], values[:, first + 1 : first + 2])


def decay_of(cum, cumt, lower, head):
    gap = cum[:, head : head + 1] - cumt[head : head + 1, :]
    return jnp.exp(jnp.where(lower > 0.0, gap, MASKED))


def rotated(ref, cos_ref, sin_ref):
    value = ref[...].astype(BF).astype(F32)
    return (value * cos_ref[...] + pltpu.roll(value, HD // 2, 1) * sin_ref[...]).astype(BF)


def causal_scores(rq, rk):
    length = rq.shape[0]
    t = lax.broadcasted_iota(jnp.int32, (length, length), 0)
    s = lax.broadcasted_iota(jnp.int32, (length, length), 1)
    scores = jnp.where(t >= s, dot(rq, rk, LANES) * HD ** (-0.5), MASKED)
    highest = jnp.max(scores, axis=1, keepdims=True)
    weights = jnp.exp(scores - highest)
    return weights, jnp.sum(weights, axis=1, keepdims=True)


def mixer_kernel(
    x_ref, m0_ref, m1_ref, m2_ref, m3_ref, s_ref, z_ref, q_ref, k_ref, v_ref, xk_ref, xb_ref, mk_ref, mb_ref, h_ref,
    cos_ref, sin_ref, scan_ref, gated_ref, square_ref, att_ref,
):
    xin, maps, xs, xslope, mslope, bees, cees, raw, dt, rate, lower, cum, coupling = scan_parts(
        x_ref, (m0_ref, m1_ref, m2_ref, m3_ref), s_ref, xk_ref, xb_ref, mk_ref, mb_ref, h_ref
    )
    cumt = cum.T
    lane = lax.broadcasted_iota(jnp.int32, (xs.shape[0], 2 * MP), 1)
    squares = jnp.zeros((xs.shape[0], 1), F32)
    for pair in range(xs.shape[1] // (2 * MP)):
        cols = slice(2 * MP * pair, 2 * MP * (pair + 1))
        xp = xs[:, cols]
        xr = (xp * lane_pair(dt, 2 * pair)).astype(BF)
        ys = []
        for head in (2 * pair, 2 * pair + 1):
            mixing = (coupling * decay_of(cum, cumt, lower, head)).astype(BF)
            ys.append(dot(mixing, xr))
        y = jnp.where(lane < MP, ys[0], ys[1]) + lane_pair(h_ref[2:3], 2 * pair) * xp
        y = y.astype(BF)
        scan_ref[:, cols] = y
        gated = y.astype(F32) * silu_parts(z_ref[:, cols])[0]
        gated_ref[:, cols] = gated
        squares = squares + jnp.sum(gated * gated, axis=1, keepdims=True)
    square_ref[...] = squares
    weights, total = causal_scores(
        rotated(q_ref, cos_ref, sin_ref), rotated(k_ref, cos_ref, sin_ref)
    )
    att_ref[...] = dot((weights / total).astype(BF), v_ref[...].astype(BF)).astype(BF)


def mixer_back_kernel(
    x_ref, m0_ref, m1_ref, m2_ref, m3_ref, s_ref, z_ref, q_ref, k_ref, v_ref, xk_ref, xb_ref, mk_ref, mb_ref, h_ref,
    cos_ref, sin_ref, scan_ref, gn_ref, gain_ref, factor_ref, dots_ref, ga_ref,
    gin_ref,
    gxk_ref, gxb_ref, gmk_ref, gmb_ref, gh_ref,
):
    xin, maps, xs, xslope, mslope, bees, cees, raw, dt, rate, lower, cum, coupling = scan_parts(
        x_ref, (m0_ref, m1_ref, m2_ref, m3_ref), s_ref, xk_ref, xb_ref, mk_ref, mb_ref, h_ref
    )
    length, width = xs.shape
    cumt = cum.T
    lane = lax.broadcasted_iota(jnp.int32, (length, 2 * MP), 1)
    factor, dots = factor_ref[...], dots_ref[...]
    gcoup = jnp.zeros((length, length), F32)
    gcum = jnp.zeros((length, 2 * MP), F32)
    gdt = jnp.zeros((length, 2 * MP), F32)
    gskip = jnp.zeros((1, 2 * MP), F32)
    gus = []
    for pair in range(width // (2 * MP)):
        cols = slice(2 * MP * pair, 2 * MP * (pair + 1))
        gate, scanned = z_ref[:, cols], scan_ref[:, cols].astype(F32)
        silu_z, sig_z = silu_parts(gate)
        normal = scanned * silu_z * factor
        ggated = factor * (gn_ref[:, cols] * gain_ref[:, cols] - normal * dots)
        gin_ref[:, cols] = (ggated * scanned * sig_z * (1.0 + gate * (1.0 - sig_z))).astype(BF)
        gy = (ggated * silu_z).astype(BF)
        gyf = gy.astype(F32)
        xp, dtp = xs[:, cols], lane_pair(dt, 2 * pair)
        xr = (xp * dtp).astype(BF)
        ys, gxrs = [], []
        for own, head in enumerate((2 * pair, 2 * pair + 1)):
            mine = (lane < MP) if own == 0 else (lane >= MP)
            decay = decay_of(cum, cumt, lower, head)
            mixing = (coupling * decay).astype(BF)
            ys.append(dot(mixing, xr))
            gxrs.append(dot(mixing, gy, ROWS))
            gcoup = gcoup + dot(jnp.where(mine, gy, jnp.zeros_like(gy)), xr, LANES) * decay
        y = jnp.where(lane < MP, ys[0], ys[1])
        gxr = jnp.where(lane < MP, gxrs[0], gxrs[1])
        flow, drive, direct = gyf * y - xr.astype(F32) * gxr, gxr * xp, gyf * xp
        for own, head in enumerate((2 * pair, 2 * pair + 1)):
            mine = (lane < MP) if own == 0 else (lane >= MP)

            def share(v):
                return jnp.sum(jnp.where(mine, v, 0.0), axis=1, keepdims=True)

            gcum = jnp.where(lane == head, share(flow), gcum)
            gdt = jnp.where(lane == head, share(drive), gdt)
            gskip = jnp.where(
                lane[:1] == head, jnp.sum(share(direct), axis=0, keepdims=True), gskip
            )
        gus.append((gxr * dtp + lane_pair(h_ref[2:3], 2 * pair) * gyf) * xslope[:, cols])
    gu = jnp.concatenate(gus, axis=1)
    gx, gxk, gxb = conv_grads(xin, xk_ref[...], gu)
    gin_ref[:, width : 2 * width] = gx.astype(BF)
    gflow = dot(lower, gcum, ROWS, precision=PRECISE)
    gdt = gdt + gflow * rate
    graw = gdt / (1.0 + jnp.exp(-raw))
    graw = jnp.where(lane < width // MP, graw, 0.0)
    common = 2 * width + HD
    gin_ref[:, common + 2 * NST + 2 * HD :] = pltpu.roll(graw, step_place(), 1).astype(BF)
    gdecay = jnp.sum(gflow * dt, axis=0, keepdims=True) * rate
    gcb = gcoup.astype(BF)
    gmaps = jnp.concatenate([dot(gcb, cees, ROWS), dot(gcb, bees)], axis=1) * mslope
    gm, gmk, gmb = conv_grads(maps, mk_ref[...], gmaps)
    gin_ref[:, common : common + 2 * NST] = gm.astype(BF)
    gh = jnp.concatenate([gdecay, jnp.sum(graw, axis=0, keepdims=True), gskip], axis=0)

    @pl.when(pl.program_id(0) == 0)
    def _():
        for ref in (gxk_ref, gxb_ref, gmk_ref, gmb_ref, gh_ref):
            ref[...] = jnp.zeros_like(ref)

    gxk_ref[...] += gxk
    gxb_ref[...] += gxb
    gmk_ref[...] += gmk
    gmb_ref[...] += gmb
    gh_ref[0:3] += gh

    rq, rk = rotated(q_ref, cos_ref, sin_ref), rotated(k_ref, cos_ref, sin_ref)
    weights, total = causal_scores(rq, rk)
    probs = weights / total
    gatt = ga_ref[...].astype(BF)
    kv = common + 2 * NST
    gin_ref[:, kv + HD : kv + 2 * HD] = dot(probs.astype(BF), gatt, ROWS).astype(BF)
    gp = dot(gatt, v_ref[...].astype(BF), LANES)
    gsc = (probs * (gp - jnp.sum(probs * gp, axis=1, keepdims=True))).astype(BF)
    for at, grad in ((2 * width, dot(gsc, rk)), (kv, dot(gsc, rq, ROWS))):
        grad = grad * HD ** (-0.5)
        back = grad * cos_ref[...] - pltpu.roll(grad, HD // 2, 1) * sin_ref[...]
        gin_ref[:, at : at + HD] = back.astype(BF)


def column_block(length, width, at):
    return pl.BlockSpec((length, width), lambda i: (i, at // width))


def mixer_specs(length, wide):
    maps = 2 * wide + HD
    return (
        [column_block(length, wide, wide)]
        + [column_block(length, NST // 2, maps + at) for at in range(0, 2 * NST, NST // 2)]
        + [
            column_block(length, 2 * MP, maps + 2 * NST + 2 * HD),
            column_block(length, wide, 0),
            column_block(length, HD, 2 * wide),
            column_block(length, HD, maps + 2 * NST),
            column_block(length, HD, maps + 2 * NST + HD),
        ]
    )


def whole_specs(arrays):
    return [pl.BlockSpec(a.shape, lambda i: (0, 0)) for a in arrays]


def mixer_forward(seqs, length, projected, params, tables):
    wide = params[0].shape[1]
    outs = [(wide, BF), (wide, F32), (1, F32), (HD, BF)]
    return pl.pallas_call(
        mixer_kernel,
        grid=(seqs,),
        in_specs=mixer_specs(length, wide) + whole_specs(params + tables),
        out_specs=[column_block(length, w, 0) for w, _ in outs],
        out_shape=[jax.ShapeDtypeStruct((seqs * length, w), d) for w, d in outs],
        compiler_params=pltpu.CompilerParams(vmem_limit_bytes=VMEM),
        name="mixer",
    )(*[projected] * 10, *params, *tables)


def mixer_backward(seqs, length, projected, params, tables, scanned, grad_mixed, gain, factor, dots):
    wide = params[0].shape[1]
    outs = [projected.shape[1]]
    sums = [(4, wide), (1, wide), (4, 2 * NST), (1, 2 * NST), (8, 2 * MP)]
    row_specs = [column_block(length, wide, 0), column_block(length, wide, 0)]
    tail_specs = [column_block(length, 1, 0), column_block(length, 1, 0), column_block(length, HD, wide)]
    return pl.pallas_call(
        mixer_back_kernel,
        grid=(seqs,),
        in_specs=mixer_specs(length, wide) + whole_specs(params + tables)
        + row_specs + whole_specs([gain]) + tail_specs,
        out_specs=[column_block(length, w, 0) for w in outs]
        + [pl.BlockSpec(s, lambda i: (0, 0)) for s in sums],
        out_shape=[jax.ShapeDtypeStruct((seqs * length, w), BF) for w in outs]
        + [jax.ShapeDtypeStruct(s, F32) for s in sums],
        compiler_params=pltpu.CompilerParams(vmem_limit_bytes=VMEM),
        name="mixer_back",
    )(
        *[projected] * 10, *params, *tables, scanned, grad_mixed, gain, factor, dots, grad_mixed,
    )


def remote(src, dst, send, recv, axis):
    other = 1 - lax.axis_index(axis)
    return pltpu.make_async_remote_copy(
        src_ref=src,
        dst_ref=dst,
        send_sem=send,
        recv_sem=recv,
        device_id={axis: other},
        device_id_type=pl.DeviceIdType.MESH,
    )


def greet(axes):
    barrier = pltpu.get_barrier_semaphore()
    for axis in axes:
        other = 1 - lax.axis_index(axis)
        pl.semaphore_signal(
            barrier, inc=1, device_id={axis: other}, device_id_type=pl.DeviceIdType.MESH
        )
    pl.semaphore_wait(barrier, len(axes))


def line_item(region, sems, sources=None):
    z, n = lax.axis_index("z"), lax.axis_size("z")

    def copy(way, k, at, src):
        return pltpu.make_async_remote_copy(
            src_ref=src,
            dst_ref=region(at),
            send_sem=sems.at[0, way, k],
            recv_sem=sems.at[1, way, k],
            device_id={"z": z + 1 - 2 * way},
            device_id_type=pl.DeviceIdType.MESH,
        )

    def send(k):
        src = sources if k == 0 and sources is not None else None

        @pl.when((z + 1 < n) & (z - k >= 0))
        def _():
            copy(0, k, z - k, region(z - k) if src is None else src).start()

        @pl.when((z >= 1) & (z + k < n))
        def _():
            copy(1, k, z + k, region(z + k) if src is None else src).start()

    def arrive(k):
        @pl.when(z - 1 - k >= 0)
        def _():
            copy(0, k, z - 1 - k, region(z - 1 - k)).wait_recv()

        @pl.when(z + 1 + k < n)
        def _():
            copy(1, k, z + 1 + k, region(z + 1 + k)).wait_recv()

    def finish():
        for k in range(n - 1):
            src = sources if k == 0 and sources is not None else None

            @pl.when((z + 1 < n) & (z - k >= 0))
            def _(k=k, src=src):
                copy(0, k, z - k, region(z - k) if src is None else src).wait_send()

            @pl.when((z >= 1) & (z + k < n))
            def _(k=k, src=src):
                copy(1, k, z + k, region(z + k) if src is None else src).wait_send()

    return send, arrive, finish


def gather_regions(region, half, sems, own_ready, own=None):
    x, y, c = (lax.axis_index(a) for a in ("x", "y", "c"))
    sent = []

    def send(i, ref, axis, src=None):
        src = ref if src is None else src
        copy = remote(src, ref, sems.at[0, i], sems.at[1, i], axis)
        copy.start()
        sent.append(copy)

    def got(i, ref, axis):
        remote(ref, ref, sems.at[0, i], sems.at[1, i], axis).wait_recv()

    def begin():
        if own is None:
            own_ready()
        for i, axis in enumerate(("x", "y", "c")):
            send(i, region(x, y, c), axis, own)

    def forward():
        got(0, region(1 - x, y, c), "x")
        send(3, half(region(1 - x, y, c), 0), "y")
        send(4, region(1 - x, y, c), "c")
        got(1, region(x, 1 - y, c), "y")
        send(5, half(region(x, 1 - y, c), 1), "x")
        send(6, region(x, 1 - y, c), "c")

    def end():
        got(3, half(region(1 - x, 1 - y, c), 0), "y")
        got(5, half(region(1 - x, 1 - y, c), 1), "x")
        send(7, region(1 - x, 1 - y, c), "c")
        got(2, region(x, y, 1 - c), "c")
        got(4, region(1 - x, y, 1 - c), "c")
        got(6, region(x, 1 - y, 1 - c), "c")
        got(7, region(1 - x, 1 - y, 1 - c), "c")
        for copy in sent:
            copy.wait_send()
        if own is not None:
            own_ready()

    return begin, forward, end


def greet_all():
    barrier = pltpu.get_barrier_semaphore()
    x, z, y, c = (lax.axis_index(a) for a in ("x", "z", "y", "c"))
    n = lax.axis_size("z")

    def tell(where):
        pl.semaphore_signal(
            barrier, inc=1, device_id=where, device_id_type=pl.DeviceIdType.MESH
        )

    for where in ({"x": 1 - x}, {"y": 1 - y}, {"c": 1 - c}, {"y": 1 - y, "c": 1 - c}):
        tell(where)

    @pl.when(z >= 1)
    def _():
        tell({"z": z - 1})

    @pl.when(z + 1 < n)
    def _():
        tell({"z": z + 1})

    pl.semaphore_wait(barrier, 4 + jnp.minimum(z, 1) + jnp.minimum(n - 1 - z, 1))


def sum_scratch(count, width):
    half = width // 2
    return [
        pltpu.VMEM((2, 2, 2, count, half), BF),
        pltpu.VMEM((2, 2, count, half), BF),
        pltpu.VMEM((2, 2, count, half), BF),
        pltpu.VMEM((2, count, half), BF),
        pltpu.VMEM((2, count, half), BF),
        pltpu.SemaphoreType.DMA((2, 6)),
    ]


def reduce_plane(part, scratch, firsts=("y", "x")):
    core, wide_in, wide_out, thin_in, thin_out, sems = scratch
    half = part.shape[4] // 2
    x, y, c = (lax.axis_index(a) for a in ("x", "y", "c"))
    seconds = ["x" if axis == "y" else "y" for axis in firsts]
    cols = [slice(0, half), slice(half, 2 * half)]

    def chip(i, yy, xx):
        return part[yy, c, xx, :, cols[i]].astype(F32) + core[i, yy, xx].astype(F32)

    def kept(i, index):
        mine = chip(i, y, index) if firsts[i] == "y" else chip(i, index, x)
        return mine + wide_in[i, index].astype(F32)

    copies = [
        remote(part.at[:, 1 - c, :, :, cols[i]], core.at[i], sems.at[0, i], sems.at[1, i], "c")
        for i in (0, 1)
    ]
    wides = [
        remote(wide_out.at[i], wide_in.at[i], sems.at[0, 2 + i], sems.at[1, 2 + i], firsts[i])
        for i in (0, 1)
    ]
    thins = [
        remote(thin_out.at[i], thin_in.at[i], sems.at[0, 4 + i], sems.at[1, 4 + i], seconds[i])
        for i in (0, 1)
    ]

    def begin():
        for copy in copies:
            copy.start()

    def wide(which=(0, 1)):
        for i in which:
            copies[i].wait()
            for k in (0, 1):
                away = chip(i, 1 - y, k) if firsts[i] == "y" else chip(i, k, 1 - x)
                wide_out[i, k] = away.astype(BF)
            wides[i].start()

    def thin():
        for i in (0, 1):
            wides[i].wait()
            thin_out[i] = kept(i, 1 - x if firsts[i] == "y" else 1 - y).astype(BF)
            thins[i].start()

    def end():
        outs = []
        for i in (0, 1):
            thins[i].wait()
            outs.append(kept(i, x if firsts[i] == "y" else y) + thin_in[i].astype(F32))
        return jnp.concatenate(outs, axis=1)

    return begin, wide, thin, end


def gathered(block, out, sems, local):
    x, y, c = (lax.axis_index(a) for a in ("x", "y", "c"))
    half = block.shape[0] // 2
    own = pltpu.make_async_copy(block, out.at[y, c, x], local)
    own.start()
    steps = gather_regions(
        lambda x, y, c: out.at[y, c, x],
        lambda ref, i: ref.at[pl.ds(i * half, half)],
        sems,
        own.wait,
        block,
    )
    return steps


def factor_of(values):
    return lax.rsqrt(jnp.mean(values * values, axis=1, keepdims=True) + EPSILON)


def norm_back_parts(values, scaling, grad):
    factor = factor_of(values)
    normal = values * factor
    scaled = grad * scaling
    inner = jnp.mean(scaled * normal, axis=1, keepdims=True)
    return factor * (scaled - normal * inner), jnp.sum(grad * normal, axis=0, keepdims=True)


def middle_kernel(
    part_ref, rows_ref, gain_ref, down_ref, out_ref, middle_ref, whole_ref,
    block, sems, local, down_sems, *scratch,
):
    z, n = lax.axis_index("z"), lax.axis_size("z")
    greet_all()
    begin, wide, thin, end = reduce_plane(part_ref, scratch)
    begin()
    own = pltpu.make_async_copy(down_ref, whole_ref.at[z], local.at[1])
    own.start()
    send, arrive, finish = line_item(lambda at: whole_ref.at[at], down_sems, down_ref)
    send(0)

    def more(k):
        if k < n:
            arrive(k - 1)
        if k < n - 1:
            send(k)

    wide()
    more(1)
    thin()
    middle = rows_ref[...].astype(F32) + end()
    middle_ref[...] = middle
    block[...] = (middle * factor_of(middle) * gain_ref[...]).astype(BF)
    first, *steps = gathered(block, out_ref, sems, local.at[0])
    first()
    more(2)
    for step in steps:
        step()
    for k in range(3, n):
        more(k)
    own.wait()
    finish()


def middle_back_kernel(
    part_ref, rows_ref, gain_ref, cot_ref, out_ref, grad_ref, gain_grad_ref,
    block, sems, local, *scratch,
):
    greet(("x", "y", "c"))
    begin, wide, thin, end = reduce_plane(part_ref, scratch)
    begin()
    wide()
    thin()
    grad, gain_grad_ref[...] = norm_back_parts(rows_ref[...], gain_ref[...], end())
    grad = grad + cot_ref[...].astype(F32)
    grad_ref[...] = grad
    block[...] = grad.astype(BF)
    for step in gathered(block, out_ref, sems, local.at[0]):
        step()


def middle_calls(part, rows, gain, down=None, cot=None):
    n = lax.axis_size("z")
    count, width = rows.shape
    vmem, hbm = pl.BlockSpec(memory_space=pltpu.VMEM), pl.BlockSpec(memory_space=pl.ANY)
    dma = pltpu.SemaphoreType.DMA
    out = [jax.ShapeDtypeStruct((2, 2, 2, count, width), BF), jax.ShapeDtypeStruct((count, width), F32)]
    scratch = [pltpu.VMEM((count, width), BF), dma((2, 8)), dma((2,))]
    if cot is None:
        inputs, specs = [part, rows, gain, down], [vmem] * 3 + [hbm]
        out += [jax.ShapeDtypeStruct((n,) + down.shape, BF)]
        out_specs = [hbm, vmem, hbm]
        scratch += [dma((2, 2, n))]
    else:
        inputs, specs = [part, rows, gain, cot], [vmem] * 4
        out += [jax.ShapeDtypeStruct((1, width), F32)]
        out_specs = [hbm, vmem, vmem]
    return pl.pallas_call(
        middle_kernel if cot is None else middle_back_kernel,
        in_specs=specs,
        out_specs=out_specs,
        out_shape=out,
        scratch_shapes=scratch + sum_scratch(count, width),
        compiler_params=pltpu.CompilerParams(
            collective_id=1 if cot is None else 2, has_side_effects=True, vmem_limit_bytes=VMEM
        ),
        name="middle" if cot is None else "middle_back",
    )(*inputs)


def total_kernel(value_ref, out_ref, got, sems):
    greet(("c", "y", "x"))
    out_ref[...] = value_ref[...]
    for i, axis in enumerate(("c", "y", "x")):
        hop = remote(out_ref, got.at[i], sems.at[0, i], sems.at[1, i], axis)
        hop.start()
        hop.wait()
        out_ref[...] = out_ref[...] + got[i]


def plane_total(value, identity):
    vmem = pl.BlockSpec(memory_space=pltpu.VMEM)
    return pl.pallas_call(
        total_kernel,
        in_specs=[vmem],
        out_specs=vmem,
        out_shape=jax.ShapeDtypeStruct(value.shape, F32),
        scratch_shapes=[pltpu.VMEM((3,) + value.shape, F32), pltpu.SemaphoreType.DMA((2, 3))],
        compiler_params=pltpu.CompilerParams(collective_id=identity, has_side_effects=True),
        name="total",
    )(value)


def line_sum(own, inbox, sems):
    z, n = lax.axis_index("z"), lax.axis_size("z")

    def copy(way, k):
        d = k if way else n - 1 - k
        slot = jnp.where(d == z - 1, n, d) if way else d
        return pltpu.make_async_remote_copy(
            src_ref=own(d),
            dst_ref=inbox(slot),
            send_sem=sems.at[0, way, k],
            recv_sem=sems.at[1, way, k],
            device_id={"z": z + 1 - 2 * way},
            device_id_type=pl.DeviceIdType.MESH,
        )

    def add(way, k, d, slot):
        pltpu.make_async_remote_copy(
            src_ref=own(d),
            dst_ref=inbox(slot),
            send_sem=sems.at[0, way, k],
            recv_sem=sems.at[1, way, k],
            device_id={"z": z},
            device_id_type=pl.DeviceIdType.MESH,
        ).wait_recv()
        held = own(d)
        held[...] = (held[...].astype(F32) + inbox(slot)[...].astype(F32)).astype(held.dtype)

    def kick(k):
        @pl.when(z == 0)
        def _():
            copy(0, k).start()

        @pl.when(z == n - 1)
        def _():
            copy(1, k).start()

    def pass_on(way, k):
        d = k if way else n - 1 - k

        @pl.when((z > 0) & (z < n - 1) & (d < z if way else d > z))
        def _():
            add(way, k, d, d)
            copy(way, k).start()

    def end():
        @pl.when(z > 0)
        def _():
            add(0, n - 1 - z, z, z)

        @pl.when(z < n - 1)
        def _():
            add(1, z, z, n)

    def finish():
        for k in range(n - 1):
            for way in (0, 1):
                d = k if way else n - 1 - k

                @pl.when(d < z if way else d > z)
                def _(way=way):
                    copy(way, k).wait_send()

    return kick, pass_on, end, finish


def column_sums(grad_ref, first, boxes, sems, local):
    own, by_c, for_y, by_y, for_x, by_x, out = boxes
    x, y, c = (lax.axis_index(a) for a in ("x", "y", "c"))

    def cols(side):
        maps = pl.ds(pl.multiple_of(first + side * NST, 128), NST)
        kv = pl.ds(pl.multiple_of(first + 2 * NST + side * HD, 128), HD)
        return (maps, pl.ds(0, NST)), (kv, pl.ds(NST, HD))

    steps = pl.ds(first + 2 * NST + 2 * HD, 128)
    loads = [
        pltpu.make_async_copy(grad_ref.at[:, src], own.at[:, dst], local.at[i])
        for i, (src, dst) in enumerate(cols(c))
    ]
    loads.append(pltpu.make_async_copy(grad_ref.at[:, steps], out.at[:, pl.ds(128, 128)], local.at[2]))
    across = [
        remote(grad_ref.at[:, src], by_c.at[:, dst], sems.at[0, i], sems.at[1, i], "c")
        for i, (src, dst) in enumerate(cols(1 - c))
    ]
    over_y = remote(for_y, by_y, sems.at[0, 2], sems.at[1, 2], "y")
    over_x = remote(for_x, by_x, sems.at[0, 3], sems.at[1, 3], "x")

    def begin():
        for copy in loads + across:
            copy.start()

    def halves(value, side):
        maps, kv = value[:, :NST], value[:, NST:]
        maps = jnp.where(side == 0, maps[:, : NST // 2], maps[:, NST // 2 :])
        kv = jnp.where(side == 0, kv[:, : HD // 2], kv[:, HD // 2 :])
        return maps, kv

    def second():
        for copy in loads + across:
            copy.wait()
        maps, kv = halves(own[...].astype(F32) + by_c[...].astype(F32), 1 - y)
        for_y[...] = jnp.concatenate([maps, kv, kv], axis=1).astype(BF)
        over_y.start()

    def summed():
        got = by_y[...].astype(F32)
        maps, kv = halves(own[...].astype(F32) + by_c[...].astype(F32), y)
        return maps + got[:, : NST // 2], kv + got[:, NST // 2 : NST // 2 + HD // 2]

    def third():
        over_y.wait()
        maps, kv = summed()
        away = jnp.where(x == 0, maps[:, NST // 4 :], maps[:, : NST // 4])
        for_x[...] = jnp.concatenate([away, away], axis=1).astype(BF)
        over_x.start()

    def end():
        over_x.wait()
        maps, kv = summed()
        maps = jnp.where(x == 0, maps[:, : NST // 4], maps[:, NST // 4 :])
        maps = maps + by_x[...].astype(F32)[:, : NST // 4]
        out[:, 0:128] = jnp.concatenate([kv, maps], axis=1).astype(BF)

    return begin, second, third, end


def hand_out(held, swap, got, places, sems, own_sems):
    x, y, c = (lax.axis_index(a) for a in ("x", "y", "c"))
    moves, kept = [], []

    def give(i):
        yy, cc = places[i]
        if i == 3:
            swap[c, y] = held(yy, cc)[...]
            return
        move = pltpu.make_async_remote_copy(
            src_ref=held(yy, cc),
            dst_ref=swap.at[c, y],
            send_sem=sems.at[0, i],
            recv_sem=sems.at[1, i],
            device_id={"y": yy, "c": cc},
            device_id_type=pl.DeviceIdType.MESH,
        )
        move.start()
        moves.append(move)

    def forward(i):
        yy, cc = places[i]
        if i < 3:
            moves[i].wait_recv()
        keep = pltpu.make_async_copy(swap.at[cc, yy], got.at[x, cc, yy], own_sems.at[i])
        move = remote(swap.at[cc, yy], got.at[x, cc, yy], sems.at[0, 3 + i], sems.at[1, 3 + i], "x")
        for copy in (keep, move):
            copy.start()
            kept.append(copy)

    def finish():
        for copy in kept:
            copy.wait()
        for move in moves:
            move.wait_send()

    return give, forward, finish


def last_kernel(
    part_ref, rows_ref, gain_ref, grad_ref, little_ref, weight_ref, common_ref, hidden_ref,
    rows_in, down_in,
    out_ref, little_out, got_ref, few_ref, rows_out, down_out,
    held, inbox, few, few_box, swap, few_swap, little, little_in, little_c, little_y, little_box,
    hidden, col_own, col_c, col_y_out, col_y_in, col_x_out, col_x_in, slices,
    local, weight_sems, few_sems, little_sems, hop_sems, swap_sems, few_swap_sems, own_sems,
    cross_sems, col_sems, col_local, *scratch,
):
    x, z, y, c = (lax.axis_index(a) for a in ("x", "z", "y", "c"))
    n = lax.axis_size("z")
    greet_all()
    load = pltpu.make_async_copy(weight_ref, held, local.at[0])
    load.start()
    load_hidden = pltpu.make_async_copy(hidden_ref, hidden, local.at[1])
    load_hidden.start()
    begin, wide, thin, end = reduce_plane(part_ref, scratch)
    boxes = (col_own, col_c, col_y_out, col_y_in, col_x_out, col_x_in, slices)
    col_begin, col_second, col_third, col_end = column_sums(
        common_ref, common_ref.shape[1] // 2, boxes, col_sems, col_local
    )
    col_begin()
    begin()
    load.wait()

    order = ((1, 1), (1, 0), (0, 1), (0, 0))
    sums, places = [], []
    for i, (dy, dc) in enumerate(order):
        yy, cc = (1 - y) if dy else y, (1 - c) if dc else c
        places.append((yy, cc))
        sums.append(
            line_sum(
                lambda d, yy=yy, cc=cc: held.at[d, yy, cc],
                lambda d, yy=yy, cc=cc: inbox.at[d, yy, cc],
                weight_sems.at[i],
            )
        )
    few_sum = line_sum(lambda d: few.at[d], lambda d: few_box.at[d], few_sems)
    for k in range(n - 1):
        for item in sums:
            item[0](k)
    crosses = []
    for i, (src, dst) in enumerate(((rows_in, rows_out), (down_in, down_out))):
        crosses.append(remote(src, dst, cross_sems.at[0, i], cross_sems.at[1, i], "x"))
        crosses[i].start()
    col_second()
    wide((0,))

    def pass_all(k):
        for item in sums:
            for near in (0, 1):

                @pl.when(z < n // 2)
                def _():
                    item[1](near, k)

                @pl.when(z >= n // 2)
                def _():
                    item[1](1 - near, k)

    pass_all(0)
    col_third()
    wide((1,))
    col_end()
    load_hidden.wait()
    product = dot(slices[...], hidden[...], ROWS).T.astype(BF)
    piece = product.shape[0] // (4 * n)
    for at in range(n):
        for yy in (0, 1):
            for cc in (0, 1):
                first = (4 * at + 2 * yy + cc) * piece
                few[at, yy, cc] = product[first : first + piece]
    for k in range(n - 1):
        few_sum[0](k)
    for k in range(1, n - 1):
        pass_all(k)
    thin()

    rows = rows_ref[...].astype(F32)
    grad, gain_grad = norm_back_parts(rows, gain_ref[...], end())
    out_ref[...] = grad + grad_ref[...]

    little[...] = little_ref[...]
    for at in range(n):
        for yy in (0, 1):
            for cc in (0, 1):
                first = (4 * at + 2 * yy + cc) * piece
                little[at, yy, cc, 0:1, 0:piece] = gain_grad[:, first : first + piece]
    hop = remote(little, little_in, hop_sems.at[0, 0], hop_sems.at[1, 0], "x")
    hop.start()
    hop.wait()
    little[...] = little[...] + little_in[...]
    hop = remote(little.at[:, :, 1 - c], little_c, hop_sems.at[0, 1], hop_sems.at[1, 1], "c")
    hop.start()
    hop.wait()
    for yy in (0, 1):
        little_c[:, yy] = little_c[:, yy] + little[:, yy, c]
    hop = remote(little_c.at[:, 1 - y], little_y, hop_sems.at[0, 2], hop_sems.at[1, 2], "y")
    hop.start()
    hop.wait()
    little_y[...] = little_y[...] + little_c[:, y]
    little_sum = line_sum(lambda d: little_y.at[d], lambda d: little_box.at[d], little_sems)
    for k in range(n - 1):
        little_sum[0](k)

    give, forward, finish = hand_out(
        lambda yy, cc: held.at[z, yy, cc], swap, got_ref, places, swap_sems, own_sems.at[0]
    )
    few_give, few_forward, few_finish = hand_out(
        lambda yy, cc: few.at[z, yy, cc], few_swap, few_ref, places, few_swap_sems, own_sems.at[1]
    )
    for i in range(4):
        sums[i][2]()
        give(i)
        if i > 0:
            forward(i - 1)
        if i < n - 1:
            for way in (0, 1):
                few_sum[1](way, i)
    forward(3)
    for k in range(4, n - 1):
        for way in (0, 1):
            few_sum[1](way, k)
    few_sum[2]()
    for i in range(4):
        few_give(i)
    for k in range(n - 1):
        for way in (0, 1):
            little_sum[1](way, k)
    little_sum[2]()
    little_out[...] = little_y[z]
    for i in range(4):
        few_forward(i)
    for cross in crosses:
        cross.wait()
    finish()
    few_finish()
    for item in sums + [few_sum, little_sum]:
        item[3]()


def last_call(part, rows, gain, grad, little, weight, common, hidden, sum_rows, sum_down):
    n = lax.axis_size("z")
    count, width = rows.shape
    total, piece = hidden.shape[0], weight.shape[3]
    block, small, pack = weight.shape[3:], (piece, 256), little.shape[3:]
    vmem, hbm = pl.BlockSpec(memory_space=pltpu.VMEM), pl.BlockSpec(memory_space=pl.ANY)
    dma = pltpu.SemaphoreType.DMA
    return pl.pallas_call(
        last_kernel,
        in_specs=[vmem] * 5 + [hbm] * 5,
        out_specs=[vmem, vmem, hbm, hbm, hbm, hbm],
        out_shape=[
            jax.ShapeDtypeStruct((count, width), F32),
            jax.ShapeDtypeStruct(pack, F32),
            jax.ShapeDtypeStruct((2, 2, 2) + block, BF),
            jax.ShapeDtypeStruct((2, 2, 2) + small, BF),
            jax.ShapeDtypeStruct(sum_rows.shape, BF),
            jax.ShapeDtypeStruct(sum_down.shape, BF),
        ],
        scratch_shapes=[
            pltpu.VMEM((n, 2, 2) + block, BF),
            pltpu.VMEM((n + 1, 2, 2) + block, BF),
            pltpu.VMEM((n, 2, 2) + small, BF),
            pltpu.VMEM((n + 1, 2, 2) + small, BF),
            pltpu.VMEM((2, 2) + block, BF),
            pltpu.VMEM((2, 2) + small, BF),
            pltpu.VMEM((n, 2, 2) + pack, F32),
            pltpu.VMEM((n, 2, 2) + pack, F32),
            pltpu.VMEM((n, 2) + pack, F32),
            pltpu.VMEM((n,) + pack, F32),
            pltpu.VMEM((n + 1,) + pack, F32),
            pltpu.VMEM(hidden.shape, BF),
            pltpu.VMEM((total, NST + HD), BF),
            pltpu.VMEM((total, NST + HD), BF),
            pltpu.VMEM((total, 256), BF),
            pltpu.VMEM((total, 256), BF),
            pltpu.VMEM((total, 128), BF),
            pltpu.VMEM((total, 128), BF),
            pltpu.VMEM((total, 256), BF),
            dma((2,)),
            dma((4, 2, 2, n)),
            dma((2, 2, n)),
            dma((2, 2, n)),
            dma((2, 3)),
            dma((2, 7)),
            dma((2, 7)),
            dma((2, 4)),
            dma((2, 2)),
            dma((2, 4)),
            dma((3,)),
        ]
        + sum_scratch(count, width),
        compiler_params=pltpu.CompilerParams(
            collective_id=3, has_side_effects=True, vmem_limit_bytes=58 * 1024 * 1024
        ),
        name="last",
    )(part, rows, gain, grad, little, weight, common, hidden, sum_rows, sum_down)


def start_kernel(
    rows_ref, little_ref, own_ref, blocks_ref, units_ref, cot_ref,
    hidden_ref, all_ref, weight_ref, unit_ref, incoming_ref,
    block, little, hidden_sems, map_sems, kv_sems, cot_sems, local, little_sems, line_sems, across_sems,
):
    x, z, y, c = (lax.axis_index(a) for a in ("x", "z", "y", "c"))
    n = lax.axis_size("z")
    width, count = blocks_ref.shape[3], rows_ref.shape[0]
    own_maps, own_kv = own_ref.at[:, pl.ds(0, NST)], own_ref.at[:, pl.ds(NST, 2 * HD + 128)]
    greet_all()

    def map_cols(x):
        return pl.ds(pl.multiple_of(width + x * NST, 128), NST)

    kv_cols = pl.ds(width + 2 * NST, 2 * HD + 128)
    in_cols = pl.ds(0, width)

    def moves_of(blocks, place, base):
        moves = []
        for i, (dy, dc) in enumerate(((0, 1), (1, 0), (1, 1))):
            where = {"y": (1 - y) if dy else y, "c": (1 - c) if dc else c}
            move = pltpu.make_async_remote_copy(
                src_ref=blocks.at[where["c"], where["y"]],
                dst_ref=place(y, c),
                send_sem=across_sems.at[0, base + i],
                recv_sem=across_sems.at[1, base + i],
                device_id=where,
                device_id_type=pl.DeviceIdType.MESH,
            )
            move.start()
            moves.append(move)
        return moves

    map_line = line_item(
        lambda at: weight_ref.at[at, y, c, :, map_cols(x)], line_sems.at[0], own_maps
    )
    kv_line = line_item(lambda at: weight_ref.at[at, y, c, :, kv_cols], line_sems.at[6], own_kv)
    little_line = line_item(lambda at: little.at[at], line_sems.at[1])
    lines = []
    for i, (dy, dc) in enumerate(((0, 0), (0, 1), (1, 0), (1, 1))):
        yy, cc = (1 - y) if dy else y, (1 - c) if dc else c
        lines.append(
            line_item(
                lambda at, yy=yy, cc=cc: weight_ref.at[at, yy, cc, :, in_cols],
                line_sems.at[2 + i],
                blocks_ref.at[c, y] if i == 0 else None,
            )
        )

    little[z, y, c] = little_ref[...]
    hop = remote(
        little.at[z, y, c], little.at[z, y, c], little_sems.at[0, 0], little_sems.at[1, 0], "c"
    )
    hop.start()
    map_line[0](0)
    kv_line[0](0)
    hop.wait()
    hop = remote(little.at[z, y], little.at[z, y], little_sems.at[0, 1], little_sems.at[1, 1], "y")
    hop.start()
    hop.wait()
    little_line[0](0)
    lines[0][0](0)
    moves = moves_of(blocks_ref, lambda y, c: weight_ref.at[z, y, c, :, in_cols], 0)

    owns = [
        pltpu.make_async_copy(own_maps, weight_ref.at[z, y, c, :, map_cols(x)], local.at[0]),
        pltpu.make_async_copy(own_kv, weight_ref.at[z, y, c, :, kv_cols], local.at[5]),
        pltpu.make_async_copy(
            blocks_ref.at[c, y], weight_ref.at[z, y, c, :, in_cols], local.at[1]
        ),
    ]
    own_unit = pltpu.make_async_copy(units_ref.at[c, y], unit_ref.at[y, c], local.at[2])
    own_cot = pltpu.make_async_copy(cot_ref, incoming_ref.at[y, c, x], local.at[3])
    own_hidden = pltpu.make_async_copy(block, hidden_ref.at[y, c, x], local.at[4])
    for copy in owns + [own_unit, own_cot]:
        copy.start()

    def half_rows(ref, i):
        return ref.at[pl.ds(i * (count // 2), count // 2)]

    cot_steps = gather_regions(
        lambda x, y, c: incoming_ref.at[y, c, x], half_rows, cot_sems, own_cot.wait, cot_ref
    )
    hidden_steps = gather_regions(
        lambda x, y, c: hidden_ref.at[y, c, x], half_rows, hidden_sems, own_hidden.wait, block
    )
    map_steps = gather_regions(
        lambda x, y, c: weight_ref.at[:, y, c, :, map_cols(x)],
        lambda ref, i: ref.at[pl.ds(i * (n // 2), n // 2)],
        map_sems,
        owns[0].wait,
    )

    def kv_copy(i, y, c, axis):
        ref = weight_ref.at[:, y, c, :, kv_cols]
        return remote(ref, ref, kv_sems.at[0, i], kv_sems.at[1, i], axis)

    cot_steps[0]()
    rows = rows_ref[...].astype(F32)
    rows = rows * factor_of(rows)
    for k in range(1, n):
        for send, arrive, finish in (little_line, map_line, kv_line):
            arrive(k - 1)
            if k < n - 1:
                send(k)

    piece = rows.shape[1] // (4 * n)
    gain = jnp.concatenate(
        [
            little[at, yy, cc, 0:1, 0:piece]
            for at in range(n)
            for yy in (0, 1)
            for cc in (0, 1)
        ],
        axis=1,
    )
    block[...] = (rows * gain).astype(BF)
    own_hidden.start()
    hidden_steps[0]()
    owns[1].wait()
    kv_copy(0, y, c, "y").start()
    kv_copy(1, y, c, "c").start()
    map_steps[0]()
    for i in range(3):
        moves[i].wait_recv()
        lines[1 + i][0](0)
    all_ref[...] = little[...]
    cot_steps[1]()

    def more(k):
        if k < n:
            for send, arrive, finish in lines:
                arrive(k - 1)
                if k < n - 1:
                    send(k)

    more(1)
    hidden_steps[1]()
    more(2)
    kv_copy(0, 1 - y, c, "y").wait_recv()
    kv_copy(2, 1 - y, c, "c").start()
    map_steps[1]()
    moves += moves_of(units_ref, lambda y, c: unit_ref.at[y, c], 3)
    for k in range(3, n):
        more(k)
    cot_steps[2]()
    hidden_steps[2]()
    map_steps[2]()
    kv_copy(1, y, 1 - c, "c").wait_recv()
    kv_copy(2, 1 - y, 1 - c, "c").wait_recv()
    kv_copy(0, y, c, "y").wait_send()
    kv_copy(1, y, c, "c").wait_send()
    kv_copy(2, 1 - y, c, "c").wait_send()
    owns[2].wait()
    own_unit.wait()
    for move in moves[3:]:
        move.wait_recv()
    for move in moves:
        move.wait_send()
    for send, arrive, finish in [map_line, kv_line, little_line] + lines:
        finish()


def start_call(rows, little, own, blocks, units, cot):
    n = lax.axis_size("z")
    count, width = rows.shape
    vmem, hbm = pl.BlockSpec(memory_space=pltpu.VMEM), pl.BlockSpec(memory_space=pl.ANY)
    dma = pltpu.SemaphoreType.DMA
    return pl.pallas_call(
        start_kernel,
        in_specs=[vmem, vmem, hbm, hbm, hbm, hbm],
        out_specs=[hbm, vmem, hbm, hbm, hbm],
        out_shape=[
            jax.ShapeDtypeStruct((2, 2, 2, count, width), BF),
            jax.ShapeDtypeStruct((n, 2, 2) + little.shape, F32),
            jax.ShapeDtypeStruct(
                (n, 2, 2, own.shape[0], blocks.shape[3] + own.shape[1] + NST), BF
            ),
            jax.ShapeDtypeStruct(units.shape, BF),
            jax.ShapeDtypeStruct((2, 2, 2, count, width), BF),
        ],
        scratch_shapes=[
            pltpu.VMEM((count, width), BF),
            pltpu.VMEM((n, 2, 2) + little.shape, F32),
            dma((2, 8)),
            dma((2, 8)),
            dma((2, 3)),
            dma((2, 8)),
            dma((6,)),
            dma((2, 2)),
            dma((7, 2, 2, n - 1)),
            dma((2, 6)),
        ],
        compiler_params=pltpu.CompilerParams(
            collective_id=0, has_side_effects=True, vmem_limit_bytes=VMEM
        ),
        name="start",
    )(rows, little, own, blocks, units, cot)


def prepare_kernel(
    query_ref, key_ref, value_ref, mamba_ref, gate_ref, up_ref, own_ref, blocks_ref, units_ref
):
    x, n = lax.axis_index("x"), lax.axis_size("z")
    inner = MH * MP
    wide = inner // PARTS

    def half(ref, start, width, at, count):
        return ref[:, pl.ds(pl.multiple_of(start + x * width + at, 128), count)]

    own_ref[:, :NST] = half(mamba_ref, 2 * inner, NST, 0, NST)
    own_ref[:, NST : NST + HD] = half(key_ref, 0, HD, 0, HD)
    own_ref[:, NST + HD : NST + 2 * HD] = half(value_ref, 0, HD, 0, HD)
    steps = mamba_ref[:, 2 * inner + 2 * NST :].astype(F32)
    steps = jnp.where(x == 0, steps[:, : MH // 2], steps[:, MH // 2 :])
    rest = jnp.zeros((steps.shape[0], 128 - MH // 2), F32)
    own_ref[:, NST + 2 * HD :] = jnp.concatenate([steps, rest], axis=1).astype(BF)
    for c in (0, 1):
        for y in (0, 1):
            j = 2 * c + y
            blocks_ref[c, y, :, :wide] = half(mamba_ref, 0, inner // 2, j * wide, wide)
            blocks_ref[c, y, :, wide : 2 * wide] = half(
                mamba_ref, inner, inner // 2, j * wide, wide
            )
            blocks_ref[c, y, :, 2 * wide :] = half(query_ref, 0, 4 * HD, j * HD, HD)
    unit = units_ref.shape[3] // 2 // n
    for at, ref in enumerate((gate_ref, up_ref)):
        for z in range(n):
            for y in (0, 1):
                for c in (0, 1):
                    first = ((z * 2 + y) * 2 + c) * 2 * unit
                    into = pl.ds((at * n + z) * unit, unit)
                    units_ref[c, y, :, into] = half(ref, first, unit, 0, unit)


def prepare(query, key, value, mamba, gate, up):
    rows, wide = query.shape[0], MH * MP // PARTS
    vmem = pl.BlockSpec(memory_space=pltpu.VMEM)
    return pl.pallas_call(
        prepare_kernel,
        in_specs=[vmem] * 6,
        out_specs=[vmem] * 3,
        out_shape=[
            jax.ShapeDtypeStruct((rows, NST + 2 * HD + 128), BF),
            jax.ShapeDtypeStruct((2, 2, rows, 2 * wide + HD), BF),
            jax.ShapeDtypeStruct((2, 2, rows, 2 * gate.shape[1] // PARTS), BF),
        ],
        compiler_params=pltpu.CompilerParams(vmem_limit_bytes=VMEM),
        name="prepare",
    )(query, key, value, mamba, gate, up)


def units_kernel(own_ref, across_ref, gate_ref, up_ref):
    x, n = lax.axis_index("x"), lax.axis_size("z")
    unit = own_ref.shape[3] // 2 // n
    for at, ref in enumerate((gate_ref, up_ref)):
        for z in range(n):
            cols = pl.ds((at * n + z) * unit, unit)
            pieces = []
            for y in (0, 1):
                for c in (0, 1):
                    own, other = own_ref[c, y, :, cols], across_ref[c, y, :, cols]
                    pieces += [jnp.where(x == 0, own, other), jnp.where(x == 0, other, own)]
            ref[:, 8 * unit * z : 8 * unit * (z + 1)] = jnp.concatenate(
                [p.astype(F32) for p in pieces], axis=1
            )


def units_call(own, across):
    vmem = pl.BlockSpec(memory_space=pltpu.VMEM)
    shape = jax.ShapeDtypeStruct((own.shape[2], PARTS * own.shape[3] // 2), F32)
    return pl.pallas_call(
        units_kernel,
        in_specs=[vmem] * 2,
        out_specs=[vmem] * 2,
        out_shape=[shape, shape],
        compiler_params=pltpu.CompilerParams(vmem_limit_bytes=VMEM),
        name="units",
    )(own, across)


def finish_kernel(
    got_ref, few_ref, own_ref, across_ref, own_down, across_down,
    query_ref, key_ref, value_ref, mamba_ref, out_ref, attn_ref, down_ref,
):
    x = lax.axis_index("x")
    inner = MH * MP
    wide = inner // PARTS
    steps = []
    for xx in (0, 1):
        total = 0.0
        for c in (0, 1):
            for y in (0, 1):
                j = 4 * xx + 2 * c + y
                block = got_ref[xx, c, y].astype(F32)
                mamba_ref[:, j * wide : (j + 1) * wide] = block[:, :wide]
                mamba_ref[:, inner + j * wide : inner + (j + 1) * wide] = block[:, wide : 2 * wide]
                query_ref[:, j * HD : (j + 1) * HD] = block[:, 2 * wide : 2 * wide + HD]
                total = total + few_ref[xx, c, y, :, 128:].astype(F32)
        steps.append(total[:, : MH // 2])
    def pair(first, second, start, width):
        return jnp.concatenate([v[:, start : start + width].astype(F32) for v in (first, second)], axis=1)

    for xx in (0, 1):
        cols = slice(xx * HD, (xx + 1) * HD)
        key_ref[:, cols] = pair(few_ref[xx, 0, 0], few_ref[xx, 0, 1], 0, HD // 2)
        value_ref[:, cols] = pair(few_ref[xx, 1, 0], few_ref[xx, 1, 1], 0, HD // 2)
    for c in (0, 1):
        for y in (0, 1):
            first = 2 * inner + (2 * c + y) * (NST // 2)
            mamba_ref[:, first : first + NST // 2] = pair(
                few_ref[0, c, y], few_ref[1, c, y], HD // 2, NST // 4
            )
    mamba_ref[:, 2 * inner + 2 * NST :] = jnp.concatenate(steps, axis=1)

    own, across = own_ref[...], across_ref[...]
    sides = [jnp.where(x == 0, own, across), jnp.where(x == 0, across, own)]
    half, first = own.shape[1], out_ref.shape[0]
    second = first + attn_ref.shape[0]
    units = down_ref.shape[0] // 2
    for xx in (0, 1):
        side = sides[xx].astype(F32)
        cols = slice(xx * half, (xx + 1) * half)
        out_ref[:, cols] = side[:first]
        attn_ref[:, cols] = side[first:second]
        mine = own_down[...].astype(F32), across_down[...].astype(F32)
        down_ref[xx * units : (xx + 1) * units] = jnp.where(x == xx, *mine)


def finish_call(got, few, own, across, own_down, across_down, shapes):
    vmem = pl.BlockSpec(memory_space=pltpu.VMEM)
    return pl.pallas_call(
        finish_kernel,
        in_specs=[vmem] * 6,
        out_specs=[vmem] * 7,
        out_shape=[jax.ShapeDtypeStruct(v, F32) for v in shapes],
        compiler_params=pltpu.CompilerParams(vmem_limit_bytes=VMEM),
        name="finish",
    )(got, few, own, across, own_down, across_down)


def flip(value, *axes):
    count = 2 ** len(axes)
    pairs = [(i, count - 1 - i) for i in range(count)]
    axes = tuple(sorted(axes, key=MESH_AXES.index))
    return lax.ppermute(value, axes, pairs)


def ordered(own, other, axis):
    second = lax.axis_index(axis) == 1
    return jnp.where(second, other, own), jnp.where(second, own, other)


def halves_of(value, axis, dim):
    at = lax.axis_index(axis)
    kept = lax.dynamic_index_in_dim(value, at, dim, keepdims=False)
    return kept, lax.dynamic_index_in_dim(value, 1 - at, dim, keepdims=False).astype(BF)


def part_index():
    return 4 * lax.axis_index("x") + 2 * lax.axis_index("c") + lax.axis_index("y")


def half_columns(weight):
    half = weight.shape[1] // 2
    return lax.dynamic_slice_in_dim(weight, lax.axis_index("x") * half, half, 1)


def exchange_blocks(blocks, high, low):
    h, l = lax.axis_index(high), lax.axis_index(low)
    return [
        lax.dynamic_index_in_dim(blocks, 2 * (h ^ dh) + (l ^ dl), 0, keepdims=False)
        for dh in (0, 1)
        for dl in (0, 1)
    ]


def exchanged(blocks, high, low, late):
    own, for_low, for_high, for_both = blocks
    got = [flip(for_low, low), flip(for_high, high), flip(for_both, high, low)]
    by_low, by_high, by_both = after(got, late)
    near, far = ordered(own, by_low, low), ordered(by_high, by_both, low)
    first, second = ordered(near[0], far[0], high), ordered(near[1], far[1], high)
    return [[first[0], second[0]], [first[1], second[1]]]


def sum_blocks(part):
    rows = part.shape[0] // 4
    y, c = lax.axis_index("y"), lax.axis_index("c")
    return [
        lax.dynamic_slice_in_dim(part, (2 * (y ^ dy) + (c ^ dc)) * rows, rows, 0)
        for dc in (0, 1)
        for dy in (0, 1)
    ]


def whole_rows(weights):
    parts = []
    for w in weights:
        whole = lax.all_gather(w, FSDP, axis=0, tiled=True)
        rows = whole.shape[0] // PARTS
        parts.append(lax.dynamic_slice_in_dim(whole, part_index() * rows, rows, 0))
    return jnp.concatenate(parts)


def joined_rows(got, pieces):
    whole = jnp.stack([jnp.concatenate([got[0][c], got[1][c]], axis=1) for c in (0, 1)])
    outs, at = [], 0
    for count in pieces:
        outs.append(whole[:, at : at + count].reshape(2 * count, -1))
        at += count
    return jnp.concatenate(outs)


def rows_blocks(grad, pieces):
    cols, grad = grad.shape[1] // 2, grad.astype(BF)
    if lax.axis_size("z") != 4:
        parts = []
        for i, count in enumerate(pieces):
            g = grad[sum(pieces[:i]) : sum(pieces[: i + 1])]
            whole = jnp.zeros((count * PARTS, 2 * cols), BF)
            parts.append(
                lax.dynamic_update_slice_in_dim(whole, g, part_index() * g.shape[0], 0)
            )
        return parts
    x, c = lax.axis_index("x"), lax.axis_index("c")
    blocks = []
    for dx in (0, 1):
        for dc in (0, 1):
            block, at = [], 0
            for count in pieces:
                start = (at + (c ^ dc) * (count // 2), (x ^ dx) * cols)
                block.append(lax.dynamic_slice(grad, start, (count // 2, cols)))
                at += count
            blocks.append(jnp.concatenate(block))
    return blocks


def rows_sum(moved):
    if lax.axis_size("z") != 4:
        parts = []
        for whole in moved:
            part = lax.psum_scatter(whole, FSDP, scatter_dimension=0, tiled=True)
            parts.append(half_columns(lax.psum(part, "x")))
        return jnp.concatenate(parts)
    moved = jnp.stack([moved[0][0], moved[0][1], moved[1][0], moved[1][1]])
    return lax.psum_scatter(moved, "z")


def after(value, earlier):
    return lax.optimization_barrier((value, earlier))[0]


def packed(first, arrays):
    lead = first.shape[0]
    flat = jnp.concatenate([a.reshape(lead, -1) for a in arrays], axis=1)
    flat = jnp.pad(flat, ((0, 0), (0, -(flat.shape[1] + 128) % 1024)))
    first = jnp.pad(first, ((0, 0), (0, 128 - first.shape[1])))
    return jnp.concatenate([first, flat], axis=1).reshape(lead, -1, 128)


def shards(
    tokens,
    cotangent,
    mixer_gain,
    query_weight,
    key_weight,
    value_weight,
    attn_out_weight,
    mamba_in_weight,
    conv_weight,
    conv_bias,
    decay_log,
    step_bias,
    skip_gain,
    mamba_gain,
    mamba_out_weight,
    ffn_gain,
    gate_weight,
    up_weight,
    down_weight,
):
    token_count, model_dim = tokens.shape[1], tokens.shape[2]
    length = 2 * token_count
    inner = MH * MP
    channels = inner + 2 * NST
    part = part_index()
    wide, heads = inner // PARTS, MH // PARTS
    rows = token_count * PARTS
    seqs = rows // length
    fsdp = lax.axis_size("z") * 4

    smalls = [ffn_gain, mamba_gain, conv_bias, conv_weight]
    little = packed(mixer_gain[None].astype(F32), [v[None].astype(F32) for v in smalls])[0]
    count = query_weight.shape[0]
    own, blocks, units = prepare(
        query_weight, key_weight, value_weight, mamba_in_weight, gate_weight, up_weight
    )
    token_rows = tokens.reshape(token_count, model_dim)
    grad_rows = cotangent.reshape(token_count, model_dim)
    hidden, gathered_little, w_in, units, incoming = start_call(
        token_rows, little, own, blocks, units, grad_rows
    )
    hidden = hidden.reshape(rows, model_dim)
    incoming = incoming.reshape(rows, model_dim)
    w_in = w_in.reshape(model_dim, -1)
    fast = lax.axis_size("z") == 4
    out_weights = [mamba_out_weight, attn_out_weight]
    out_pieces = [w.shape[0] for w in out_weights]
    if fast:
        out_blocks = half_columns(jnp.concatenate(out_weights))
        out_blocks = lax.all_gather(out_blocks, "z", axis=0, tiled=False)
        out_blocks = exchange_blocks(out_blocks, "x", "c")
    w_gateup = lax.all_gather(units.reshape(4 * count, -1), "z", axis=0, tiled=True)
    down_half = down_weight.reshape(2, -1, model_dim)
    down_half = lax.dynamic_index_in_dim(down_half, lax.axis_index("x"), 0, keepdims=False)
    ff = gate_weight.shape[1] // PARTS

    gathered_little = gathered_little.reshape(fsdp, -1)
    gain_in = gathered_little[:, : mixer_gain.size].reshape(-1)
    got, at = [], 128
    for s in smalls:
        got.append(gathered_little[:, at : at + s.size].reshape((fsdp,) + s.shape))
        at += s.size
    gain_ffn, gain_mamba, bias_full = (g.reshape(-1) for g in got[:3])
    conv_full = got[3].transpose(1, 0, 2).reshape(4, channels)
    gain_mamba = lax.dynamic_slice_in_dim(gain_mamba, part * wide, wide, 0)

    def own_heads(v):
        return lax.dynamic_slice_in_dim(v.astype(F32), part * heads, heads, 0)

    heads_rows = jnp.stack([own_heads(v) for v in (decay_log, step_bias, skip_gain)])
    heads_rows = jnp.pad(heads_rows, ((0, 5), (0, 2 * MP - heads)))
    params = [
        lax.dynamic_slice_in_dim(conv_full, part * wide, wide, 1),
        lax.dynamic_slice_in_dim(bias_full, part * wide, wide, 0)[None],
        conv_full[:, inner:],
        bias_full[None, inner:],
        heads_rows,
    ]
    tables = rope_tables(length, HD)

    projected = mm(after(hidden, out_blocks) if fast else hidden, w_in)
    scanned, gated, squares, attended = mixer_forward(seqs, length, projected, params, tables)

    if fast:
        w_out = joined_rows(exchanged(out_blocks, "x", "c", squares), out_pieces)
    else:
        w_out = whole_rows(out_weights)
    squares = plane_total(squares.reshape(-1, 128), 4)
    factor = lax.rsqrt(squares / inner + EPSILON).reshape(rows, 1)
    normal = gated * factor
    normed = (normal * gain_mamba).astype(BF)
    mixed = jnp.concatenate([normed, attended], axis=1)
    block = (2, 2, 2, token_count, model_dim)
    mixer_sum = mm(mixed, w_out).astype(BF).reshape(block)
    second, middle, w_down = middle_calls(mixer_sum, token_rows, gain_ffn[None], down_half)
    w_down = w_down.reshape(ff, model_dim)
    second = second.reshape(rows, model_dim)
    gate_up = mm(second, w_gateup)
    gate_act, up_act = gate_up[:, :ff], gate_up[:, ff:]
    sig_g = jax.nn.sigmoid(gate_act)
    active = (gate_act * sig_g * up_act).astype(BF)

    grad_active = across(incoming, w_down)
    grad_gate = grad_active * up_act * sig_g * (1.0 + gate_act * (1.0 - sig_g))
    grad_up = grad_active * gate_act * sig_g
    grad_gateup = jnp.concatenate([grad_gate.astype(BF), grad_up.astype(BF)], axis=1)
    grad_wgateup = outer_product(second, grad_gateup)
    sum_gateup = lax.psum_scatter(grad_wgateup.astype(BF).reshape(-1, 4 * count, 2 * ff), "z")
    grad_second = across(grad_gateup, w_gateup).astype(BF).reshape(block)
    grad_mixer, grad_middle, grad_gain_ffn = middle_calls(
        grad_second, middle, gain_ffn[None], cot=grad_rows
    )
    grad_mixer = grad_mixer.reshape(rows, model_dim)
    grad_mixed = across(grad_mixer, w_out)
    grad_normed = grad_mixed[:, :wide]
    grad_gain_mamba = jnp.sum(grad_normed * normal, axis=0)
    scaled = grad_normed * gain_mamba
    dots = plane_total(jnp.sum(scaled * normal, axis=-1).reshape(-1, 128), 5)
    grad_mixer, active, sum_gateup = after((grad_mixer, active, sum_gateup), dots)
    grad_out = outer_product(mixed, grad_mixer)
    row_blocks = rows_blocks(grad_out, [wide, HD])
    active = after(active, row_blocks)
    sides = active.reshape(2, 2, 2 * token_count, ff)
    result_kept, result_away = (
        mm(v, w_down).astype(BF).reshape(2, 2, token_count, model_dim)
        for v in halves_of(sides, "c", 1)
    )
    result_got = flip(result_away, "c")
    grad_down = outer_product(after(active, result_away), incoming).astype(BF)
    sum_down = lax.psum_scatter(
        grad_down.reshape(-1, ff // lax.axis_size("z"), model_dim), "z"
    )
    gateup_blocks = sum_blocks(sum_gateup)
    dots = after(dots, (gateup_blocks, grad_down))
    row_sums = exchanged(row_blocks, "x", "c", dots) if fast else row_blocks
    result_got = after(result_got, dots)
    half = model_dim // 2
    lefts = [halves_of(v[..., :half], "y", 0) for v in (result_kept, result_got)]
    rights = [halves_of(v[..., half:], "x", 1) for v in (result_kept, result_got)]
    left, right = ((a[1].astype(F32) + b[1].astype(F32)).astype(BF) for a, b in (lefts, rights))
    dots = after(dots, (left, right)).reshape(rows, 1) / inner

    grad_in, gxk, gxb, gmk, gmb, gheads = mixer_backward(
        seqs, length, projected, params, tables, scanned, grad_mixed, gain_mamba[None], factor, dots
    )
    sum_rows = rows_sum(after(row_sums, grad_in))
    moved = exchanged(gateup_blocks, "c", "y", grad_in)
    moved = jnp.stack([jnp.stack(g) for g in moved])
    moved_across = flip(moved, "x")
    left, right = after((flip(left, "y"), flip(right, "x")), grad_in)
    lefts = [halves_of(v, "x", 0) for v in (lefts[0][0], lefts[1][0], left)]
    rights = [halves_of(v, "y", 0) for v in (rights[0][0], rights[1][0], right)]

    def three(values, index):
        return sum(v[index].astype(F32) for v in values)

    left, right = three(lefts, 1).astype(BF), three(rights, 1).astype(BF)
    grad_in = after(grad_in, (moved, left, right))
    grad_hidden = across(grad_in, w_in).astype(BF).reshape(block)
    grad_win = outer_product(hidden, grad_in[:, : 2 * wide + HD]).astype(BF)
    grad_win = grad_win.reshape(-1, 2, 2, count, grad_win.shape[1])
    left, right = after((flip(left, "x"), flip(right, "y")), grad_win)
    result = jnp.concatenate(
        [three(lefts, 0) + left.astype(F32), three(rights, 0) + right.astype(F32)], axis=1
    )
    output = (middle + result).astype(BF).reshape(1, token_count, model_dim)
    shard_gate, shard_up = units_call(moved, after(moved_across, grad_win))

    conv_grad = jnp.zeros((4, channels), F32)
    conv_grad = lax.dynamic_update_slice_in_dim(conv_grad, gxk, part * wide, 1)
    conv_grad = conv_grad.at[:, inner:].set(gmk)
    bias_grad = jnp.zeros((channels,), F32)
    bias_grad = lax.dynamic_update_slice_in_dim(bias_grad, gxb[0], part * wide, 0)
    bias_grad = bias_grad.at[inner:].set(gmb[0])
    gain_grad = lax.dynamic_update_slice_in_dim(
        jnp.zeros((inner,), F32), grad_gain_mamba, part * wide, 0
    )
    head_grad = lax.dynamic_update_slice_in_dim(
        jnp.zeros((3, MH), F32), gheads[:3, :heads], part * heads, 1
    )
    scattered = [grad_gain_ffn, gain_grad, bias_grad]
    little = [v.reshape(fsdp, -1) for v in scattered]
    little.append(conv_grad.reshape(4, fsdp, -1).transpose(1, 0, 2).reshape(fsdp, -1))
    little.append(jnp.broadcast_to(head_grad.reshape(1, -1), (fsdp, 3 * MH)))
    little = packed(jnp.zeros((fsdp, count), F32), little)
    little = little.reshape((-1, 2, 2) + little.shape[1:])
    tokens_grad, total, got_in, got_few, rows_across, down_across = last_call(
        grad_hidden, token_rows, gain_in[None], grad_middle, little, grad_win, grad_in, hidden,
        sum_rows, sum_down,
    )
    tokens_grad = tokens_grad.reshape(1, token_count, model_dim)
    total = total.reshape(-1)
    got, at = [total[:count]], 128
    for like in (ffn_gain, mamba_gain, conv_bias, conv_weight, head_grad):
        got.append(total[at : at + like.size].reshape(like.shape))
        at += like.size

    weights = [query_weight, key_weight, value_weight, mamba_in_weight]
    weights += [mamba_out_weight, attn_out_weight, down_weight]
    (
        shard_query, shard_key, shard_value, shard_mamba_in,
        shard_mamba_out, shard_attn_out, shard_down,
    ) = finish_call(
        got_in, got_few, sum_rows, rows_across, sum_down, down_across, [w.shape for w in weights]
    )

    return (
        output,
        tokens_grad,
        got[0],
        shard_query,
        shard_key,
        shard_value,
        shard_attn_out,
        shard_mamba_in,
        got[4],
        got[3],
        got[5][0],
        got[5][1],
        got[5][2],
        got[2],
        shard_mamba_out,
        got[1],
        shard_gate,
        shard_up,
        shard_down,
    )


def solution(mesh):
    fsdp = mesh.shape["fsdp"]
    grid = Mesh(mesh.devices.reshape(2, fsdp // 4, 2, 2), ("x", "z", "y", "c"))
    rows, flat, whole = P(FSDP, None), P(FSDP), P()
    stream = P(FSDP, "x", None)
    weights = (
        flat, rows, rows, rows, rows, rows, P(None, FSDP), flat, whole, whole, whole,
        flat, rows, flat, rows, rows, rows,
    )
    return jax.shard_map(
        shards,
        mesh=grid,
        in_specs=(stream, stream) + weights,
        out_specs=(stream, stream) + weights,
        check_vma=False,
    )
```

```python
import math

import jax
import jax.numpy as jnp
from jax import lax
from jax.experimental import pallas as pl
from jax.experimental.pallas import tpu as pltpu
from jax.sharding import Mesh
from jax.sharding import PartitionSpec as P

HQ = 8
KVH = 2
HD = 128
MH = 48
MP = 64
NST = 256
EPSILON = 1e-05
ROPE_BASE = 100000000000.0
MASKED = -1e30
BF = jnp.bfloat16
F32 = jnp.float32
MESH_AXES = ("x", "z", "y", "c")
FSDP = ("z", "y", "c")
PARTS = 8
VMEM = 48 * 1024 * 1024


def mm(left, right):
    return jnp.dot(left, right, preferred_element_type=F32)


def outer_product(left, right):
    return lax.dot_general(left, right, (((0,), (0,)), ((), ())), preferred_element_type=F32)


def across(left, right):
    return lax.dot_general(left, right, (((1,), (1,)), ((), ())), preferred_element_type=F32)


def rope_tables(length, head_size):
    half_size = head_size // 2
    frequency = jnp.exp(
        jnp.arange(half_size, dtype=F32) * (-2.0 * math.log(ROPE_BASE) / head_size)
    )
    angles = jnp.arange(length, dtype=F32)[:, None] * frequency[None, :]
    cosine, sine = jnp.cos(angles), jnp.sin(angles)
    return [jnp.concatenate(v, axis=1) for v in ([cosine, cosine], [-sine, sine])]


def silu_parts(values):
    sig = 1.0 / (1.0 + jnp.exp(-values))
    return values * sig, sig


def shifted(values, count):
    if count == 0:
        return values
    rows = values.shape[0]
    at = lax.broadcasted_iota(jnp.int32, values.shape, 0)
    kept = (at >= count) if count > 0 else (at < rows + count)
    return jnp.where(kept, pltpu.roll(values, count % rows, 0), 0.0)


def conv_silu(signal, kernel, bias):
    taps = kernel.shape[0]
    total = bias + signal * kernel[taps - 1 : taps]
    for back in range(1, taps):
        total = total + shifted(signal, back) * kernel[taps - 1 - back : taps - back]
    value, sig = silu_parts(total)
    return value, sig * (1.0 + total * (1.0 - sig))


def conv_grads(signal, kernel, grad):
    taps = kernel.shape[0]
    back = grad * kernel[taps - 1 : taps]
    rows = []
    for count in range(taps - 1, 0, -1):
        rows.append(jnp.sum(shifted(signal, count) * grad, axis=0, keepdims=True))
        back = back + shifted(grad, -count) * kernel[taps - 1 - count : taps - count]
    rows.append(jnp.sum(signal * grad, axis=0, keepdims=True))
    return back, jnp.concatenate(rows, axis=0), jnp.sum(grad, axis=0, keepdims=True)


def dot(left, right, dims=((1,), (0,)), precision=None):
    return lax.dot_general(
        left, right, (dims, ((), ())), preferred_element_type=F32, precision=precision
    )


ROWS = ((0,), (0,))
LANES = ((1,), (1,))
PRECISE = lax.Precision.HIGHEST


def step_place():
    return (MH // PARTS) * (2 * lax.axis_index("c") + lax.axis_index("y"))


def scan_parts(x_ref, m_refs, s_ref, xk_ref, xb_ref, mk_ref, mb_ref, h_ref):
    length = x_ref.shape[0]
    xin = x_ref[...].astype(BF).astype(F32)
    maps = jnp.concatenate([ref[...].astype(BF).astype(F32) for ref in m_refs], axis=1)
    xs, xslope = conv_silu(xin, xk_ref[...], xb_ref[...])
    mv, mslope = conv_silu(maps, mk_ref[...], mb_ref[...])
    mv = mv.astype(BF)
    bees, cees = mv[:, :NST], mv[:, NST:]
    raw = pltpu.roll(s_ref[...].astype(BF).astype(F32), 2 * MP - step_place(), 1) + h_ref[1:2]
    dt = jnp.maximum(raw, 0.0) + jnp.log1p(jnp.exp(-jnp.abs(raw)))
    rate = -jnp.exp(h_ref[0:1])
    t = lax.broadcasted_iota(jnp.int32, (length, length), 0)
    s = lax.broadcasted_iota(jnp.int32, (length, length), 1)
    lower = (t >= s).astype(F32)
    cum = dot(lower, dt * rate, precision=PRECISE)
    coupling = dot(cees, bees, LANES)
    return xin, maps, xs, xslope, mslope, bees, cees, raw, dt, rate, lower, cum, coupling


def lane_pair(values, first):
    lane = lax.broadcasted_iota(jnp.int32, (values.shape[0], 2 * MP), 1)
    return jnp.where(lane < MP, values[:, first : first + 1], values[:, first + 1 : first + 2])


def decay_of(cum, cumt, lower, head):
    gap = cum[:, head : head + 1] - cumt[head : head + 1, :]
    return jnp.exp(jnp.where(lower > 0.0, gap, MASKED))


def rotated(ref, cos_ref, sin_ref):
    value = ref[...].astype(BF).astype(F32)
    return (value * cos_ref[...] + pltpu.roll(value, HD // 2, 1) * sin_ref[...]).astype(BF)


def causal_scores(rq, rk):
    length = rq.shape[0]
    t = lax.broadcasted_iota(jnp.int32, (length, length), 0)
    s = lax.broadcasted_iota(jnp.int32, (length, length), 1)
    scores = jnp.where(t >= s, dot(rq, rk, LANES) * HD ** (-0.5), MASKED)
    highest = jnp.max(scores, axis=1, keepdims=True)
    weights = jnp.exp(scores - highest)
    return weights, jnp.sum(weights, axis=1, keepdims=True)


def mixer_kernel(
    x_ref, m0_ref, m1_ref, m2_ref, m3_ref, s_ref, z_ref, q_ref, k_ref, v_ref, xk_ref, xb_ref, mk_ref, mb_ref, h_ref,
    cos_ref, sin_ref, scan_ref, gated_ref, square_ref, att_ref,
):
    xin, maps, xs, xslope, mslope, bees, cees, raw, dt, rate, lower, cum, coupling = scan_parts(
        x_ref, (m0_ref, m1_ref, m2_ref, m3_ref), s_ref, xk_ref, xb_ref, mk_ref, mb_ref, h_ref
    )
    cumt = cum.T
    lane = lax.broadcasted_iota(jnp.int32, (xs.shape[0], 2 * MP), 1)
    squares = jnp.zeros((xs.shape[0], 1), F32)
    for pair in range(xs.shape[1] // (2 * MP)):
        cols = slice(2 * MP * pair, 2 * MP * (pair + 1))
        xp = xs[:, cols]
        xr = (xp * lane_pair(dt, 2 * pair)).astype(BF)
        ys = []
        for head in (2 * pair, 2 * pair + 1):
            mixing = (coupling * decay_of(cum, cumt, lower, head)).astype(BF)
            ys.append(dot(mixing, xr))
        y = jnp.where(lane < MP, ys[0], ys[1]) + lane_pair(h_ref[2:3], 2 * pair) * xp
        y = y.astype(BF)
        scan_ref[:, cols] = y
        gated = y.astype(F32) * silu_parts(z_ref[:, cols])[0]
        gated_ref[:, cols] = gated
        squares = squares + jnp.sum(gated * gated, axis=1, keepdims=True)
    square_ref[...] = squares
    weights, total = causal_scores(
        rotated(q_ref, cos_ref, sin_ref), rotated(k_ref, cos_ref, sin_ref)
    )
    att_ref[...] = dot((weights / total).astype(BF), v_ref[...].astype(BF)).astype(BF)


def mixer_back_kernel(
    x_ref, m0_ref, m1_ref, m2_ref, m3_ref, s_ref, z_ref, q_ref, k_ref, v_ref, xk_ref, xb_ref, mk_ref, mb_ref, h_ref,
    cos_ref, sin_ref, scan_ref, gn_ref, gain_ref, factor_ref, dots_ref, ga_ref,
    gin_ref,
    gxk_ref, gxb_ref, gmk_ref, gmb_ref, gh_ref,
):
    xin, maps, xs, xslope, mslope, bees, cees, raw, dt, rate, lower, cum, coupling = scan_parts(
        x_ref, (m0_ref, m1_ref, m2_ref, m3_ref), s_ref, xk_ref, xb_ref, mk_ref, mb_ref, h_ref
    )
    length, width = xs.shape
    cumt = cum.T
    lane = lax.broadcasted_iota(jnp.int32, (length, 2 * MP), 1)
    factor, dots = factor_ref[...], dots_ref[...]
    gcoup = jnp.zeros((length, length), F32)
    gcum = jnp.zeros((length, 2 * MP), F32)
    gdt = jnp.zeros((length, 2 * MP), F32)
    gskip = jnp.zeros((1, 2 * MP), F32)
    gus = []
    for pair in range(width // (2 * MP)):
        cols = slice(2 * MP * pair, 2 * MP * (pair + 1))
        gate, scanned = z_ref[:, cols], scan_ref[:, cols].astype(F32)
        silu_z, sig_z = silu_parts(gate)
        normal = scanned * silu_z * factor
        ggated = factor * (gn_ref[:, cols] * gain_ref[:, cols] - normal * dots)
        gin_ref[:, cols] = (ggated * scanned * sig_z * (1.0 + gate * (1.0 - sig_z))).astype(BF)
        gy = (ggated * silu_z).astype(BF)
        gyf = gy.astype(F32)
        xp, dtp = xs[:, cols], lane_pair(dt, 2 * pair)
        xr = (xp * dtp).astype(BF)
        ys, gxrs = [], []
        for own, head in enumerate((2 * pair, 2 * pair + 1)):
            mine = (lane < MP) if own == 0 else (lane >= MP)
            decay = decay_of(cum, cumt, lower, head)
            mixing = (coupling * decay).astype(BF)
            ys.append(dot(mixing, xr))
            gxrs.append(dot(mixing, gy, ROWS))
            gcoup = gcoup + dot(jnp.where(mine, gy, jnp.zeros_like(gy)), xr, LANES) * decay
        y = jnp.where(lane < MP, ys[0], ys[1])
        gxr = jnp.where(lane < MP, gxrs[0], gxrs[1])
        flow, drive, direct = gyf * y - xr.astype(F32) * gxr, gxr * xp, gyf * xp
        for own, head in enumerate((2 * pair, 2 * pair + 1)):
            mine = (lane < MP) if own == 0 else (lane >= MP)

            def share(v):
                return jnp.sum(jnp.where(mine, v, 0.0), axis=1, keepdims=True)

            gcum = jnp.where(lane == head, share(flow), gcum)
            gdt = jnp.where(lane == head, share(drive), gdt)
            gskip = jnp.where(
                lane[:1] == head, jnp.sum(share(direct), axis=0, keepdims=True), gskip
            )
        gus.append((gxr * dtp + lane_pair(h_ref[2:3], 2 * pair) * gyf) * xslope[:, cols])
    gu = jnp.concatenate(gus, axis=1)
    gx, gxk, gxb = conv_grads(xin, xk_ref[...], gu)
    gin_ref[:, width : 2 * width] = gx.astype(BF)
    gflow = dot(lower, gcum, ROWS, precision=PRECISE)
    gdt = gdt + gflow * rate
    graw = gdt / (1.0 + jnp.exp(-raw))
    graw = jnp.where(lane < width // MP, graw, 0.0)
    common = 2 * width + HD
    gin_ref[:, common + 2 * NST + 2 * HD :] = pltpu.roll(graw, step_place(), 1).astype(BF)
    gdecay = jnp.sum(gflow * dt, axis=0, keepdims=True) * rate
    gcb = gcoup.astype(BF)
    gmaps = jnp.concatenate([dot(gcb, cees, ROWS), dot(gcb, bees)], axis=1) * mslope
    gm, gmk, gmb = conv_grads(maps, mk_ref[...], gmaps)
    gin_ref[:, common : common + 2 * NST] = gm.astype(BF)
    gh = jnp.concatenate([gdecay, jnp.sum(graw, axis=0, keepdims=True), gskip], axis=0)

    @pl.when(pl.program_id(0) == 0)
    def _():
        for ref in (gxk_ref, gxb_ref, gmk_ref, gmb_ref, gh_ref):
            ref[...] = jnp.zeros_like(ref)

    gxk_ref[...] += gxk
    gxb_ref[...] += gxb
    gmk_ref[...] += gmk
    gmb_ref[...] += gmb
    gh_ref[0:3] += gh

    rq, rk = rotated(q_ref, cos_ref, sin_ref), rotated(k_ref, cos_ref, sin_ref)
    weights, total = causal_scores(rq, rk)
    probs = weights / total
    gatt = ga_ref[...].astype(BF)
    kv = common + 2 * NST
    gin_ref[:, kv + HD : kv + 2 * HD] = dot(probs.astype(BF), gatt, ROWS).astype(BF)
    gp = dot(gatt, v_ref[...].astype(BF), LANES)
    gsc = (probs * (gp - jnp.sum(probs * gp, axis=1, keepdims=True))).astype(BF)
    for at, grad in ((2 * width, dot(gsc, rk)), (kv, dot(gsc, rq, ROWS))):
        grad = grad * HD ** (-0.5)
        back = grad * cos_ref[...] - pltpu.roll(grad, HD // 2, 1) * sin_ref[...]
        gin_ref[:, at : at + HD] = back.astype(BF)


def column_block(length, width, at):
    return pl.BlockSpec((length, width), lambda i: (i, at // width))


def mixer_specs(length, wide):
    maps = 2 * wide + HD
    return (
        [column_block(length, wide, wide)]
        + [column_block(length, NST // 2, maps + at) for at in range(0, 2 * NST, NST // 2)]
        + [
            column_block(length, 2 * MP, maps + 2 * NST + 2 * HD),
            column_block(length, wide, 0),
            column_block(length, HD, 2 * wide),
            column_block(length, HD, maps + 2 * NST),
            column_block(length, HD, maps + 2 * NST + HD),
        ]
    )


def whole_specs(arrays):
    return [pl.BlockSpec(a.shape, lambda i: (0, 0)) for a in arrays]


def mixer_forward(seqs, length, projected, params, tables):
    wide = params[0].shape[1]
    outs = [(wide, BF), (wide, F32), (1, F32), (HD, BF)]
    return pl.pallas_call(
        mixer_kernel,
        grid=(seqs,),
        in_specs=mixer_specs(length, wide) + whole_specs(params + tables),
        out_specs=[column_block(length, w, 0) for w, _ in outs],
        out_shape=[jax.ShapeDtypeStruct((seqs * length, w), d) for w, d in outs],
        compiler_params=pltpu.CompilerParams(vmem_limit_bytes=VMEM),
        name="mixer",
    )(*[projected] * 10, *params, *tables)


def mixer_backward(seqs, length, projected, params, tables, scanned, grad_mixed, gain, factor, dots):
    wide = params[0].shape[1]
    outs = [projected.shape[1]]
    sums = [(4, wide), (1, wide), (4, 2 * NST), (1, 2 * NST), (8, 2 * MP)]
    row_specs = [column_block(length, wide, 0), column_block(length, wide, 0)]
    tail_specs = [column_block(length, 1, 0), column_block(length, 1, 0), column_block(length, HD, wide)]
    return pl.pallas_call(
        mixer_back_kernel,
        grid=(seqs,),
        in_specs=mixer_specs(length, wide) + whole_specs(params + tables)
        + row_specs + whole_specs([gain]) + tail_specs,
        out_specs=[column_block(length, w, 0) for w in outs]
        + [pl.BlockSpec(s, lambda i: (0, 0)) for s in sums],
        out_shape=[jax.ShapeDtypeStruct((seqs * length, w), BF) for w in outs]
        + [jax.ShapeDtypeStruct(s, F32) for s in sums],
        compiler_params=pltpu.CompilerParams(vmem_limit_bytes=VMEM),
        name="mixer_back",
    )(
        *[projected] * 10, *params, *tables, scanned, grad_mixed, gain, factor, dots, grad_mixed,
    )


def remote(src, dst, send, recv, axis):
    other = 1 - lax.axis_index(axis)
    return pltpu.make_async_remote_copy(
        src_ref=src,
        dst_ref=dst,
        send_sem=send,
        recv_sem=recv,
        device_id={axis: other},
        device_id_type=pl.DeviceIdType.MESH,
    )


def greet(axes):
    barrier = pltpu.get_barrier_semaphore()
    for axis in axes:
        other = 1 - lax.axis_index(axis)
        pl.semaphore_signal(
            barrier, inc=1, device_id={axis: other}, device_id_type=pl.DeviceIdType.MESH
        )
    pl.semaphore_wait(barrier, len(axes))


def line_item(region, sems, sources=None):
    z, n = lax.axis_index("z"), lax.axis_size("z")

    def copy(way, k, at, src):
        return pltpu.make_async_remote_copy(
            src_ref=src,
            dst_ref=region(at),
            send_sem=sems.at[0, way, k],
            recv_sem=sems.at[1, way, k],
            device_id={"z": z + 1 - 2 * way},
            device_id_type=pl.DeviceIdType.MESH,
        )

    def send(k):
        src = sources if k == 0 and sources is not None else None

        @pl.when((z + 1 < n) & (z - k >= 0))
        def _():
            copy(0, k, z - k, region(z - k) if src is None else src).start()

        @pl.when((z >= 1) & (z + k < n))
        def _():
            copy(1, k, z + k, region(z + k) if src is None else src).start()

    def arrive(k):
        @pl.when(z - 1 - k >= 0)
        def _():
            copy(0, k, z - 1 - k, region(z - 1 - k)).wait_recv()

        @pl.when(z + 1 + k < n)
        def _():
            copy(1, k, z + 1 + k, region(z + 1 + k)).wait_recv()

    def finish():
        for k in range(n - 1):
            src = sources if k == 0 and sources is not None else None

            @pl.when((z + 1 < n) & (z - k >= 0))
            def _(k=k, src=src):
                copy(0, k, z - k, region(z - k) if src is None else src).wait_send()

            @pl.when((z >= 1) & (z + k < n))
            def _(k=k, src=src):
                copy(1, k, z + k, region(z + k) if src is None else src).wait_send()

    return send, arrive, finish


def gather_regions(region, half, sems, own_ready, own=None):
    x, y, c = (lax.axis_index(a) for a in ("x", "y", "c"))
    sent = []

    def send(i, ref, axis, src=None):
        src = ref if src is None else src
        copy = remote(src, ref, sems.at[0, i], sems.at[1, i], axis)
        copy.start()
        sent.append(copy)

    def got(i, ref, axis):
        remote(ref, ref, sems.at[0, i], sems.at[1, i], axis).wait_recv()

    def begin():
        if own is None:
            own_ready()
        for i, axis in enumerate(("x", "y", "c")):
            send(i, region(x, y, c), axis, own)

    def forward():
        got(0, region(1 - x, y, c), "x")
        send(3, half(region(1 - x, y, c), 0), "y")
        send(4, region(1 - x, y, c), "c")
        got(1, region(x, 1 - y, c), "y")
        send(5, half(region(x, 1 - y, c), 1), "x")
        send(6, region(x, 1 - y, c), "c")

    def end():
        got(3, half(region(1 - x, 1 - y, c), 0), "y")
        got(5, half(region(1 - x, 1 - y, c), 1), "x")
        send(7, region(1 - x, 1 - y, c), "c")
        got(2, region(x, y, 1 - c), "c")
        got(4, region(1 - x, y, 1 - c), "c")
        got(6, region(x, 1 - y, 1 - c), "c")
        got(7, region(1 - x, 1 - y, 1 - c), "c")
        for copy in sent:
            copy.wait_send()
        if own is not None:
            own_ready()

    return begin, forward, end


def greet_all():
    barrier = pltpu.get_barrier_semaphore()
    x, z, y, c = (lax.axis_index(a) for a in ("x", "z", "y", "c"))
    n = lax.axis_size("z")

    def tell(where):
        pl.semaphore_signal(
            barrier, inc=1, device_id=where, device_id_type=pl.DeviceIdType.MESH
        )

    for where in ({"x": 1 - x}, {"y": 1 - y}, {"c": 1 - c}, {"y": 1 - y, "c": 1 - c}):
        tell(where)

    @pl.when(z >= 1)
    def _():
        tell({"z": z - 1})

    @pl.when(z + 1 < n)
    def _():
        tell({"z": z + 1})

    pl.semaphore_wait(barrier, 4 + jnp.minimum(z, 1) + jnp.minimum(n - 1 - z, 1))


def sum_scratch(count, width):
    half = width // 2
    return [
        pltpu.VMEM((2, 2, 2, count, half), BF),
        pltpu.VMEM((2, 2, count, half), BF),
        pltpu.VMEM((2, 2, count, half), BF),
        pltpu.VMEM((2, count, half), BF),
        pltpu.VMEM((2, count, half), BF),
        pltpu.SemaphoreType.DMA((2, 6)),
    ]


def reduce_plane(part, scratch, firsts=("y", "x")):
    core, wide_in, wide_out, thin_in, thin_out, sems = scratch
    half = part.shape[4] // 2
    x, y, c = (lax.axis_index(a) for a in ("x", "y", "c"))
    seconds = ["x" if axis == "y" else "y" for axis in firsts]
    cols = [slice(0, half), slice(half, 2 * half)]

    def chip(i, yy, xx):
        return part[yy, c, xx, :, cols[i]].astype(F32) + core[i, yy, xx].astype(F32)

    def kept(i, index):
        mine = chip(i, y, index) if firsts[i] == "y" else chip(i, index, x)
        return mine + wide_in[i, index].astype(F32)

    copies = [
        remote(part.at[:, 1 - c, :, :, cols[i]], core.at[i], sems.at[0, i], sems.at[1, i], "c")
        for i in (0, 1)
    ]
    wides = [
        remote(wide_out.at[i], wide_in.at[i], sems.at[0, 2 + i], sems.at[1, 2 + i], firsts[i])
        for i in (0, 1)
    ]
    thins = [
        remote(thin_out.at[i], thin_in.at[i], sems.at[0, 4 + i], sems.at[1, 4 + i], seconds[i])
        for i in (0, 1)
    ]

    def begin():
        for copy in copies:
            copy.start()

    def wide(which=(0, 1)):
        for i in which:
            copies[i].wait()
            for k in (0, 1):
                away = chip(i, 1 - y, k) if firsts[i] == "y" else chip(i, k, 1 - x)
                wide_out[i, k] = away.astype(BF)
            wides[i].start()

    def thin():
        for i in (0, 1):
            wides[i].wait()
            thin_out[i] = kept(i, 1 - x if firsts[i] == "y" else 1 - y).astype(BF)
            thins[i].start()

    def end():
        outs = []
        for i in (0, 1):
            thins[i].wait()
            outs.append(kept(i, x if firsts[i] == "y" else y) + thin_in[i].astype(F32))
        return jnp.concatenate(outs, axis=1)

    return begin, wide, thin, end


def gathered(block, out, sems, local):
    x, y, c = (lax.axis_index(a) for a in ("x", "y", "c"))
    half = block.shape[0] // 2
    own = pltpu.make_async_copy(block, out.at[y, c, x], local)
    own.start()
    steps = gather_regions(
        lambda x, y, c: out.at[y, c, x],
        lambda ref, i: ref.at[pl.ds(i * half, half)],
        sems,
        own.wait,
        block,
    )
    return steps


def factor_of(values):
    return lax.rsqrt(jnp.mean(values * values, axis=1, keepdims=True) + EPSILON)


def norm_back_parts(values, scaling, grad):
    factor = factor_of(values)
    normal = values * factor
    scaled = grad * scaling
    inner = jnp.mean(scaled * normal, axis=1, keepdims=True)
    return factor * (scaled - normal * inner), jnp.sum(grad * normal, axis=0, keepdims=True)


def middle_kernel(
    part_ref, rows_ref, gain_ref, down_ref, out_ref, middle_ref, whole_ref,
    block, sems, local, down_sems, *scratch,
):
    z, n = lax.axis_index("z"), lax.axis_size("z")
    greet_all()
    begin, wide, thin, end = reduce_plane(part_ref, scratch)
    begin()
    own = pltpu.make_async_copy(down_ref, whole_ref.at[z], local.at[1])
    own.start()
    send, arrive, finish = line_item(lambda at: whole_ref.at[at], down_sems, down_ref)
    send(0)

    def more(k):
        if k < n:
            arrive(k - 1)
        if k < n - 1:
            send(k)

    wide()
    more(1)
    thin()
    middle = rows_ref[...].astype(F32) + end()
    middle_ref[...] = middle
    block[...] = (middle * factor_of(middle) * gain_ref[...]).astype(BF)
    first, *steps = gathered(block, out_ref, sems, local.at[0])
    first()
    more(2)
    for step in steps:
        step()
    for k in range(3, n):
        more(k)
    own.wait()
    finish()


def middle_back_kernel(
    part_ref, rows_ref, gain_ref, cot_ref, out_ref, grad_ref, gain_grad_ref,
    block, sems, local, *scratch,
):
    greet(("x", "y", "c"))
    begin, wide, thin, end = reduce_plane(part_ref, scratch)
    begin()
    wide()
    thin()
    grad, gain_grad_ref[...] = norm_back_parts(rows_ref[...], gain_ref[...], end())
    grad = grad + cot_ref[...].astype(F32)
    grad_ref[...] = grad
    block[...] = grad.astype(BF)
    for step in gathered(block, out_ref, sems, local.at[0]):
        step()


def middle_calls(part, rows, gain, down=None, cot=None):
    n = lax.axis_size("z")
    count, width = rows.shape
    vmem, hbm = pl.BlockSpec(memory_space=pltpu.VMEM), pl.BlockSpec(memory_space=pl.ANY)
    dma = pltpu.SemaphoreType.DMA
    out = [jax.ShapeDtypeStruct((2, 2, 2, count, width), BF), jax.ShapeDtypeStruct((count, width), F32)]
    scratch = [pltpu.VMEM((count, width), BF), dma((2, 8)), dma((2,))]
    if cot is None:
        inputs, specs = [part, rows, gain, down], [vmem] * 3 + [hbm]
        out += [jax.ShapeDtypeStruct((n,) + down.shape, BF)]
        out_specs = [hbm, vmem, hbm]
        scratch += [dma((2, 2, n))]
    else:
        inputs, specs = [part, rows, gain, cot], [vmem] * 4
        out += [jax.ShapeDtypeStruct((1, width), F32)]
        out_specs = [hbm, vmem, vmem]
    return pl.pallas_call(
        middle_kernel if cot is None else middle_back_kernel,
        in_specs=specs,
        out_specs=out_specs,
        out_shape=out,
        scratch_shapes=scratch + sum_scratch(count, width),
        compiler_params=pltpu.CompilerParams(
            collective_id=1 if cot is None else 2, has_side_effects=True, vmem_limit_bytes=VMEM
        ),
        name="middle" if cot is None else "middle_back",
    )(*inputs)


def total_kernel(value_ref, out_ref, got, sems):
    greet(("c", "y", "x"))
    out_ref[...] = value_ref[...]
    for i, axis in enumerate(("c", "y", "x")):
        hop = remote(out_ref, got.at[i], sems.at[0, i], sems.at[1, i], axis)
        hop.start()
        hop.wait()
        out_ref[...] = out_ref[...] + got[i]


def plane_total(value, identity):
    vmem = pl.BlockSpec(memory_space=pltpu.VMEM)
    return pl.pallas_call(
        total_kernel,
        in_specs=[vmem],
        out_specs=vmem,
        out_shape=jax.ShapeDtypeStruct(value.shape, F32),
        scratch_shapes=[pltpu.VMEM((3,) + value.shape, F32), pltpu.SemaphoreType.DMA((2, 3))],
        compiler_params=pltpu.CompilerParams(collective_id=identity, has_side_effects=True),
        name="total",
    )(value)


def line_sum(own, inbox, sems):
    z, n = lax.axis_index("z"), lax.axis_size("z")

    def copy(way, k):
        d = k if way else n - 1 - k
        slot = jnp.where(d == z - 1, n, d) if way else d
        return pltpu.make_async_remote_copy(
            src_ref=own(d),
            dst_ref=inbox(slot),
            send_sem=sems.at[0, way, k],
            recv_sem=sems.at[1, way, k],
            device_id={"z": z + 1 - 2 * way},
            device_id_type=pl.DeviceIdType.MESH,
        )

    def add(way, k, d, slot):
        pltpu.make_async_remote_copy(
            src_ref=own(d),
            dst_ref=inbox(slot),
            send_sem=sems.at[0, way, k],
            recv_sem=sems.at[1, way, k],
            device_id={"z": z},
            device_id_type=pl.DeviceIdType.MESH,
        ).wait_recv()
        held = own(d)
        held[...] = (held[...].astype(F32) + inbox(slot)[...].astype(F32)).astype(held.dtype)

    def kick(k):
        @pl.when(z == 0)
        def _():
            copy(0, k).start()

        @pl.when(z == n - 1)
        def _():
            copy(1, k).start()

    def pass_on(way, k):
        d = k if way else n - 1 - k

        @pl.when((z > 0) & (z < n - 1) & (d < z if way else d > z))
        def _():
            add(way, k, d, d)
            copy(way, k).start()

    def end():
        @pl.when(z > 0)
        def _():
            add(0, n - 1 - z, z, z)

        @pl.when(z < n - 1)
        def _():
            add(1, z, z, n)

    def finish():
        for k in range(n - 1):
            for way in (0, 1):
                d = k if way else n - 1 - k

                @pl.when(d < z if way else d > z)
                def _(way=way):
                    copy(way, k).wait_send()

    return kick, pass_on, end, finish


def column_sums(grad_ref, grad, first, boxes, sems):
    by_c, for_y, by_y, for_x, by_x, out = boxes
    x, y, c = (lax.axis_index(a) for a in ("x", "y", "c"))

    def cols(side):
        maps = pl.ds(pl.multiple_of(first + side * NST, 128), NST)
        kv = pl.ds(pl.multiple_of(first + 2 * NST + side * HD, 128), HD)
        return (maps, pl.ds(0, NST)), (kv, pl.ds(NST, HD))

    def own():
        return jnp.concatenate([grad[:, src] for src, _ in cols(c)], axis=1).astype(F32)

    across = [
        remote(grad_ref.at[:, src], by_c.at[:, dst], sems.at[0, i], sems.at[1, i], "c")
        for i, (src, dst) in enumerate(cols(1 - c))
    ]
    over_y = remote(for_y, by_y, sems.at[0, 2], sems.at[1, 2], "y")
    over_x = remote(for_x, by_x, sems.at[0, 3], sems.at[1, 3], "x")

    def begin():
        for copy in across:
            copy.start()

    def halves(value, side):
        maps, kv = value[:, :NST], value[:, NST:]
        maps = jnp.where(side == 0, maps[:, : NST // 2], maps[:, NST // 2 :])
        kv = jnp.where(side == 0, kv[:, : HD // 2], kv[:, HD // 2 :])
        return maps, kv

    def second():
        for copy in across:
            copy.wait()
        maps, kv = halves(own() + by_c[...].astype(F32), 1 - y)
        for_y[...] = jnp.concatenate([maps, kv, kv], axis=1).astype(BF)
        over_y.start()

    def summed():
        got = by_y[...].astype(F32)
        maps, kv = halves(own() + by_c[...].astype(F32), y)
        return maps + got[:, : NST // 2], kv + got[:, NST // 2 : NST // 2 + HD // 2]

    def third():
        over_y.wait()
        maps, kv = summed()
        away = jnp.where(x == 0, maps[:, NST // 4 :], maps[:, : NST // 4])
        for_x[...] = jnp.concatenate([away, away], axis=1).astype(BF)
        over_x.start()

    def end():
        over_x.wait()
        maps, kv = summed()
        maps = jnp.where(x == 0, maps[:, : NST // 4], maps[:, NST // 4 :])
        maps = maps + by_x[...].astype(F32)[:, : NST // 4]
        out[:, 0:128] = jnp.concatenate([kv, maps], axis=1).astype(BF)
        out[:, 128:256] = grad[:, first + 2 * NST + 2 * HD :]

    return begin, second, third, end


def hand_out(held, swap, got, places, sems, own_sems):
    x, y, c = (lax.axis_index(a) for a in ("x", "y", "c"))
    moves, kept = [], []

    def give(i):
        yy, cc = places[i]
        if i == 3:
            swap[c, y] = held(yy, cc)[...]
            return
        move = pltpu.make_async_remote_copy(
            src_ref=held(yy, cc),
            dst_ref=swap.at[c, y],
            send_sem=sems.at[0, i],
            recv_sem=sems.at[1, i],
            device_id={"y": yy, "c": cc},
            device_id_type=pl.DeviceIdType.MESH,
        )
        move.start()
        moves.append(move)

    def forward(i):
        yy, cc = places[i]
        if i < 3:
            moves[i].wait_recv()
        keep = pltpu.make_async_copy(swap.at[cc, yy], got.at[x, cc, yy], own_sems.at[i])
        move = remote(swap.at[cc, yy], got.at[x, cc, yy], sems.at[0, 3 + i], sems.at[1, 3 + i], "x")
        for copy in (keep, move):
            copy.start()
            kept.append(copy)

    def finish():
        for copy in kept:
            copy.wait()
        for move in moves:
            move.wait_send()

    return give, forward, finish


def last_kernel(
    rows_ref, gain_ref, grad_ref, little_ref, weight_ref, common_ref, hidden_ref, project_ref,
    rows_in, out_ref, little_out, got_ref, few_ref, rows_out,
    held, inbox, few, few_box, swap, few_swap, little, little_in, little_c, little_y, little_box,
    hidden, common, project, part, col_c, col_y_out, col_y_in, col_x_out, col_x_in, slices,
    local, weight_sems, few_sems, little_sems, hop_sems, swap_sems, few_swap_sems, own_sems,
    cross_sems, col_sems, *scratch,
):
    x, z, y, c = (lax.axis_index(a) for a in ("x", "z", "y", "c"))
    n = lax.axis_size("z")
    greet_all()
    pairs = ((weight_ref, held), (common_ref, common), (project_ref, project), (hidden_ref, hidden))
    loads = [pltpu.make_async_copy(*pair, local.at[i]) for i, pair in enumerate(pairs)]
    for load in loads:
        load.start()
    begin, wide, thin, end = reduce_plane(part, scratch)
    boxes = (col_c, col_y_out, col_y_in, col_x_out, col_x_in, slices)
    col_begin, col_second, col_third, col_end = column_sums(
        common_ref, common, common_ref.shape[1] // 2, boxes, col_sems
    )
    col_begin()
    count = rows_ref.shape[0]

    def product_of(cc, yy):
        for xx in (0, 1):
            first = pl.multiple_of((4 * yy + 2 * cc + xx) * count, 16)
            block = common[pl.ds(first, count), :]
            part[yy, cc, xx] = dot(block, project[...], LANES).astype(BF)

    order = ((1, 1), (1, 0), (0, 1), (0, 0))
    sums, places = [], []
    for i, (dy, dc) in enumerate(order):
        yy, cc = (1 - y) if dy else y, (1 - c) if dc else c
        places.append((yy, cc))
        sums.append(
            line_sum(
                lambda d, yy=yy, cc=cc: held.at[d, yy, cc],
                lambda d, yy=yy, cc=cc: inbox.at[d, yy, cc],
                weight_sems.at[i],
            )
        )
    few_sum = line_sum(lambda d: few.at[d], lambda d: few_box.at[d], few_sems)
    cross = remote(rows_in, rows_out, cross_sems.at[0], cross_sems.at[1], "x")
    loads[0].wait()
    for k in range(n - 1):
        for item in sums:
            item[0](k)

    def pass_on(item, k, far):
        @pl.when(z < n // 2)
        def _():
            item[1](far, k)

        @pl.when(z >= n // 2)
        def _():
            item[1](1 - far, k)

    loads[1].wait()
    col_second()
    loads[2].wait()
    product_of(1 - c, 0)
    pass_on(sums[0], 0, 0)
    product_of(1 - c, 1)
    begin()
    pass_on(sums[1], 0, 0)
    pass_on(sums[0], 0, 1)
    product_of(c, 0)
    pass_on(sums[2], 0, 0)
    pass_on(sums[1], 0, 1)
    product_of(c, 1)
    pass_on(sums[3], 0, 0)
    pass_on(sums[2], 0, 1)
    wide()
    pass_on(sums[3], 0, 1)
    col_third()
    if n > 2:
        for i in (0, 1, 2, 3):
            pass_on(sums[i], 1, 0)
    col_end()
    loads[3].wait()
    product = dot(slices[...], hidden[...], ROWS).T.astype(BF)
    piece = product.shape[0] // (4 * n)
    for at in range(n):
        for yy in (0, 1):
            for cc in (0, 1):
                first = (4 * at + 2 * yy + cc) * piece
                few[at, yy, cc] = product[first : first + piece]
    for k in range(n - 1):
        few_sum[0](k)
    for k in range(1, n - 1):
        for item in sums:
            for far in (0, 1):
                if k > 1 or far == 1:
                    pass_on(item, k, far)
    thin()
    cross.start()

    rows = rows_ref[...].astype(F32)
    grad, gain_grad = norm_back_parts(rows, gain_ref[...], end())
    out_ref[...] = grad + grad_ref[...]
    little[...] = little_ref[...]
    for at in range(n):
        for yy in (0, 1):
            for cc in (0, 1):
                first = (4 * at + 2 * yy + cc) * piece
                little[at, yy, cc, 0:1, 0:piece] = gain_grad[:, first : first + piece]
    hop = remote(little, little_in, hop_sems.at[0, 0], hop_sems.at[1, 0], "x")
    hop.start()

    give, forward, finish = hand_out(
        lambda yy, cc: held.at[z, yy, cc], swap, got_ref, places, swap_sems, own_sems.at[0]
    )
    few_give, few_forward, few_finish = hand_out(
        lambda yy, cc: few.at[z, yy, cc], few_swap, few_ref, places, few_swap_sems, own_sems.at[1]
    )
    for i in (0, 1):
        sums[i][2]()
        give(i)
    hop.wait()
    little[...] = little[...] + little_in[...]
    hop = remote(little.at[:, :, 1 - c], little_c, hop_sems.at[0, 1], hop_sems.at[1, 1], "c")
    hop.start()
    forward(0)
    sums[2][2]()
    give(2)
    forward(1)
    hop.wait()
    for yy in (0, 1):
        little_c[:, yy] = little_c[:, yy] + little[:, yy, c]
    hop = remote(little_c.at[:, 1 - y], little_y, hop_sems.at[0, 2], hop_sems.at[1, 2], "y")
    hop.start()
    sums[3][2]()
    give(3)
    forward(2)
    forward(3)
    pass_on(few_sum, 0, 0)
    hop.wait()
    little_y[...] = little_y[...] + little_c[:, y]
    little_sum = line_sum(lambda d: little_y.at[d], lambda d: little_box.at[d], little_sems)
    for k in range(n - 1):
        little_sum[0](k)
    for k in range(n - 1):
        for far in (0, 1):
            if k > 0 or far == 1:
                pass_on(few_sum, k, far)
    few_sum[2]()
    for i in range(4):
        few_give(i)
    for k in range(n - 1):
        for way in (0, 1):
            little_sum[1](way, k)
    little_sum[2]()
    little_out[...] = little_y[z]
    for i in range(4):
        few_forward(i)
    cross.wait()
    finish()
    few_finish()
    for item in sums + [few_sum, little_sum]:
        item[3]()


def last_call(rows, gain, grad, little, weight, common, hidden, project, sum_rows):
    n = lax.axis_size("z")
    count, width = rows.shape
    total, piece = hidden.shape[0], weight.shape[3]
    block, small, pack = weight.shape[3:], (piece, 256), little.shape[3:]
    vmem, hbm = pl.BlockSpec(memory_space=pltpu.VMEM), pl.BlockSpec(memory_space=pl.ANY)
    dma = pltpu.SemaphoreType.DMA
    return pl.pallas_call(
        last_kernel,
        in_specs=[vmem] * 4 + [hbm] * 5,
        out_specs=[vmem, vmem, hbm, hbm, hbm],
        out_shape=[
            jax.ShapeDtypeStruct((count, width), F32),
            jax.ShapeDtypeStruct(pack, F32),
            jax.ShapeDtypeStruct((2, 2, 2) + block, BF),
            jax.ShapeDtypeStruct((2, 2, 2) + small, BF),
            jax.ShapeDtypeStruct(sum_rows.shape, BF),
        ],
        scratch_shapes=[
            pltpu.VMEM((n, 2, 2) + block, BF),
            pltpu.VMEM((n + 1, 2, 2) + block, BF),
            pltpu.VMEM((n, 2, 2) + small, BF),
            pltpu.VMEM((n + 1, 2, 2) + small, BF),
            pltpu.VMEM((2, 2) + block, BF),
            pltpu.VMEM((2, 2) + small, BF),
            pltpu.VMEM((n, 2, 2) + pack, F32),
            pltpu.VMEM((n, 2, 2) + pack, F32),
            pltpu.VMEM((n, 2) + pack, F32),
            pltpu.VMEM((n,) + pack, F32),
            pltpu.VMEM((n + 1,) + pack, F32),
            pltpu.VMEM(hidden.shape, BF),
            pltpu.VMEM(common.shape, BF),
            pltpu.VMEM(project.shape, BF),
            pltpu.VMEM((2, 2, 2, count, width), BF),
            pltpu.VMEM((total, NST + HD), BF),
            pltpu.VMEM((total, 256), BF),
            pltpu.VMEM((total, 256), BF),
            pltpu.VMEM((total, 128), BF),
            pltpu.VMEM((total, 128), BF),
            pltpu.VMEM((total, 256), BF),
            dma((4,)),
            dma((4, 2, 2, n)),
            dma((2, 2, n)),
            dma((2, 2, n)),
            dma((2, 3)),
            dma((2, 7)),
            dma((2, 7)),
            dma((2, 4)),
            dma((2,)),
            dma((2, 4)),
        ]
        + sum_scratch(count, width),
        compiler_params=pltpu.CompilerParams(
            collective_id=3, has_side_effects=True, vmem_limit_bytes=61 * 1024 * 1024
        ),
        name="last",
    )(rows, gain, grad, little, weight, common, hidden, project, sum_rows)


def start_kernel(
    rows_ref, little_ref, own_ref, blocks_ref, units_ref, cot_ref,
    hidden_ref, all_ref, weight_ref, unit_ref, incoming_ref,
    block, little, hidden_sems, map_sems, kv_sems, cot_sems, local, little_sems, line_sems, across_sems,
):
    x, z, y, c = (lax.axis_index(a) for a in ("x", "z", "y", "c"))
    n = lax.axis_size("z")
    width, count = blocks_ref.shape[3], rows_ref.shape[0]
    own_maps, own_kv = own_ref.at[:, pl.ds(0, NST)], own_ref.at[:, pl.ds(NST, 2 * HD + 128)]
    greet_all()

    def map_cols(x):
        return pl.ds(pl.multiple_of(width + x * NST, 128), NST)

    kv_cols = pl.ds(width + 2 * NST, 2 * HD + 128)
    in_cols = pl.ds(0, width)

    def moves_of(blocks, place, base):
        moves = []
        for i, (dy, dc) in enumerate(((0, 1), (1, 0), (1, 1))):
            where = {"y": (1 - y) if dy else y, "c": (1 - c) if dc else c}
            move = pltpu.make_async_remote_copy(
                src_ref=blocks.at[where["c"], where["y"]],
                dst_ref=place(y, c),
                send_sem=across_sems.at[0, base + i],
                recv_sem=across_sems.at[1, base + i],
                device_id=where,
                device_id_type=pl.DeviceIdType.MESH,
            )
            move.start()
            moves.append(move)
        return moves

    map_line = line_item(
        lambda at: weight_ref.at[at, y, c, :, map_cols(x)], line_sems.at[0], own_maps
    )
    kv_line = line_item(lambda at: weight_ref.at[at, y, c, :, kv_cols], line_sems.at[6], own_kv)
    little_line = line_item(lambda at: little.at[at], line_sems.at[1])
    lines = []
    for i, (dy, dc) in enumerate(((0, 0), (0, 1), (1, 0), (1, 1))):
        yy, cc = (1 - y) if dy else y, (1 - c) if dc else c
        lines.append(
            line_item(
                lambda at, yy=yy, cc=cc: weight_ref.at[at, yy, cc, :, in_cols],
                line_sems.at[2 + i],
                blocks_ref.at[c, y] if i == 0 else None,
            )
        )

    little[z, y, c] = little_ref[...]
    hop = remote(
        little.at[z, y, c], little.at[z, y, c], little_sems.at[0, 0], little_sems.at[1, 0], "c"
    )
    hop.start()
    map_line[0](0)
    kv_line[0](0)
    hop.wait()
    hop = remote(little.at[z, y], little.at[z, y], little_sems.at[0, 1], little_sems.at[1, 1], "y")
    hop.start()
    hop.wait()
    little_line[0](0)
    lines[0][0](0)
    moves = moves_of(blocks_ref, lambda y, c: weight_ref.at[z, y, c, :, in_cols], 0)

    owns = [
        pltpu.make_async_copy(own_maps, weight_ref.at[z, y, c, :, map_cols(x)], local.at[0]),
        pltpu.make_async_copy(own_kv, weight_ref.at[z, y, c, :, kv_cols], local.at[5]),
        pltpu.make_async_copy(
            blocks_ref.at[c, y], weight_ref.at[z, y, c, :, in_cols], local.at[1]
        ),
    ]
    own_unit = pltpu.make_async_copy(units_ref.at[c, y], unit_ref.at[y, c], local.at[2])
    own_cot = pltpu.make_async_copy(cot_ref, incoming_ref.at[y, c, x], local.at[3])
    own_hidden = pltpu.make_async_copy(block, hidden_ref.at[y, c, x], local.at[4])
    for copy in owns + [own_unit, own_cot]:
        copy.start()

    def half_rows(ref, i):
        return ref.at[pl.ds(i * (count // 2), count // 2)]

    cot_steps = gather_regions(
        lambda x, y, c: incoming_ref.at[y, c, x], half_rows, cot_sems, own_cot.wait, cot_ref
    )
    hidden_steps = gather_regions(
        lambda x, y, c: hidden_ref.at[y, c, x], half_rows, hidden_sems, own_hidden.wait, block
    )
    map_steps = gather_regions(
        lambda x, y, c: weight_ref.at[:, y, c, :, map_cols(x)],
        lambda ref, i: ref.at[pl.ds(i * (n // 2), n // 2)],
        map_sems,
        owns[0].wait,
    )

    def kv_copy(i, y, c, axis):
        ref = weight_ref.at[:, y, c, :, kv_cols]
        return remote(ref, ref, kv_sems.at[0, i], kv_sems.at[1, i], axis)

    cot_steps[0]()
    rows = rows_ref[...].astype(F32)
    rows = rows * factor_of(rows)
    for k in range(1, n):
        for send, arrive, finish in (little_line, map_line, kv_line):
            arrive(k - 1)
            if k < n - 1:
                send(k)

    piece = rows.shape[1] // (4 * n)
    gain = jnp.concatenate(
        [
            little[at, yy, cc, 0:1, 0:piece]
            for at in range(n)
            for yy in (0, 1)
            for cc in (0, 1)
        ],
        axis=1,
    )
    block[...] = (rows * gain).astype(BF)
    own_hidden.start()
    hidden_steps[0]()
    owns[1].wait()
    kv_copy(0, y, c, "y").start()
    kv_copy(1, y, c, "c").start()
    map_steps[0]()
    for i in range(3):
        moves[i].wait_recv()
        lines[1 + i][0](0)
    all_ref[...] = little[...]
    cot_steps[1]()

    def more(k):
        if k < n:
            for send, arrive, finish in lines:
                arrive(k - 1)
                if k < n - 1:
                    send(k)

    more(1)
    hidden_steps[1]()
    more(2)
    kv_copy(0, 1 - y, c, "y").wait_recv()
    kv_copy(2, 1 - y, c, "c").start()
    map_steps[1]()
    moves += moves_of(units_ref, lambda y, c: unit_ref.at[y, c], 3)
    for k in range(3, n):
        more(k)
    cot_steps[2]()
    hidden_steps[2]()
    map_steps[2]()
    kv_copy(1, y, 1 - c, "c").wait_recv()
    kv_copy(2, 1 - y, 1 - c, "c").wait_recv()
    kv_copy(0, y, c, "y").wait_send()
    kv_copy(1, y, c, "c").wait_send()
    kv_copy(2, 1 - y, c, "c").wait_send()
    owns[2].wait()
    own_unit.wait()
    for move in moves[3:]:
        move.wait_recv()
    for move in moves:
        move.wait_send()
    for send, arrive, finish in [map_line, kv_line, little_line] + lines:
        finish()


def start_call(rows, little, own, blocks, units, cot):
    n = lax.axis_size("z")
    count, width = rows.shape
    vmem, hbm = pl.BlockSpec(memory_space=pltpu.VMEM), pl.BlockSpec(memory_space=pl.ANY)
    dma = pltpu.SemaphoreType.DMA
    return pl.pallas_call(
        start_kernel,
        in_specs=[vmem, vmem, hbm, hbm, hbm, hbm],
        out_specs=[hbm, vmem, hbm, hbm, hbm],
        out_shape=[
            jax.ShapeDtypeStruct((2, 2, 2, count, width), BF),
            jax.ShapeDtypeStruct((n, 2, 2) + little.shape, F32),
            jax.ShapeDtypeStruct(
                (n, 2, 2, own.shape[0], blocks.shape[3] + own.shape[1] + NST), BF
            ),
            jax.ShapeDtypeStruct(units.shape, BF),
            jax.ShapeDtypeStruct((2, 2, 2, count, width), BF),
        ],
        scratch_shapes=[
            pltpu.VMEM((count, width), BF),
            pltpu.VMEM((n, 2, 2) + little.shape, F32),
            dma((2, 8)),
            dma((2, 8)),
            dma((2, 3)),
            dma((2, 8)),
            dma((6,)),
            dma((2, 2)),
            dma((7, 2, 2, n - 1)),
            dma((2, 6)),
        ],
        compiler_params=pltpu.CompilerParams(
            collective_id=0, has_side_effects=True, vmem_limit_bytes=VMEM
        ),
        name="start",
    )(rows, little, own, blocks, units, cot)


def prepare_kernel(
    query_ref, key_ref, value_ref, mamba_ref, gate_ref, up_ref, own_ref, blocks_ref, units_ref
):
    x, n = lax.axis_index("x"), lax.axis_size("z")
    inner = MH * MP
    wide = inner // PARTS

    def turned(start, width, at, count):
        rows = mamba_ref[pl.ds(pl.multiple_of(start + x * width + at, 128), count), :]
        return rows.astype(F32).T.astype(BF)

    def half(ref, start, width, at, count):
        return ref[:, pl.ds(pl.multiple_of(start + x * width + at, 128), count)]

    own_ref[:, :NST] = turned(2 * inner, NST, 0, NST)
    own_ref[:, NST : NST + HD] = half(key_ref, 0, HD, 0, HD)
    own_ref[:, NST + HD : NST + 2 * HD] = half(value_ref, 0, HD, 0, HD)
    steps = mamba_ref[2 * inner + 2 * NST :, :].astype(F32)
    steps = jnp.where(x == 0, steps[: MH // 2], steps[MH // 2 :])
    rest = jnp.zeros((128 - MH // 2, steps.shape[1]), F32)
    own_ref[:, NST + 2 * HD :] = jnp.concatenate([steps, rest], axis=0).T.astype(BF)
    for c in (0, 1):
        for y in (0, 1):
            j = 2 * c + y
            blocks_ref[c, y, :, :wide] = turned(0, inner // 2, j * wide, wide)
            blocks_ref[c, y, :, wide : 2 * wide] = turned(
                inner, inner // 2, j * wide, wide
            )
            blocks_ref[c, y, :, 2 * wide :] = half(query_ref, 0, 4 * HD, j * HD, HD)
    unit = units_ref.shape[3] // 2 // n
    for at, ref in enumerate((gate_ref, up_ref)):
        for z in range(n):
            for y in (0, 1):
                for c in (0, 1):
                    first = ((z * 2 + y) * 2 + c) * 2 * unit
                    into = pl.ds((at * n + z) * unit, unit)
                    units_ref[c, y, :, into] = half(ref, first, unit, 0, unit)


def prepare(query, key, value, mamba, gate, up):
    rows, wide = query.shape[0], MH * MP // PARTS
    vmem = pl.BlockSpec(memory_space=pltpu.VMEM)
    return pl.pallas_call(
        prepare_kernel,
        in_specs=[vmem] * 6,
        out_specs=[vmem] * 3,
        out_shape=[
            jax.ShapeDtypeStruct((rows, NST + 2 * HD + 128), BF),
            jax.ShapeDtypeStruct((2, 2, rows, 2 * wide + HD), BF),
            jax.ShapeDtypeStruct((2, 2, rows, 2 * gate.shape[1] // PARTS), BF),
        ],
        compiler_params=pltpu.CompilerParams(vmem_limit_bytes=VMEM),
        name="prepare",
    )(query, key, value, mamba.T, gate, up)


def units_kernel(own_ref, across_ref, gate_ref, up_ref):
    x, n = lax.axis_index("x"), lax.axis_size("z")
    unit = own_ref.shape[3] // 2 // n
    for at, ref in enumerate((gate_ref, up_ref)):
        for z in range(n):
            cols = pl.ds((at * n + z) * unit, unit)
            pieces = []
            for y in (0, 1):
                for c in (0, 1):
                    own, other = own_ref[c, y, :, cols], across_ref[c, y, :, cols]
                    pieces += [jnp.where(x == 0, own, other), jnp.where(x == 0, other, own)]
            ref[:, 8 * unit * z : 8 * unit * (z + 1)] = jnp.concatenate(
                [p.astype(F32) for p in pieces], axis=1
            )


def units_call(own, across):
    vmem = pl.BlockSpec(memory_space=pltpu.VMEM)
    shape = jax.ShapeDtypeStruct((own.shape[2], PARTS * own.shape[3] // 2), F32)
    return pl.pallas_call(
        units_kernel,
        in_specs=[vmem] * 2,
        out_specs=[vmem] * 2,
        out_shape=[shape, shape],
        compiler_params=pltpu.CompilerParams(vmem_limit_bytes=VMEM),
        name="units",
    )(own, across)


def finish_kernel(
    got_ref, few_ref, own_ref, across_ref, own_down, across_down,
    query_ref, key_ref, value_ref, mamba_ref, out_ref, attn_ref, down_ref,
):
    x = lax.axis_index("x")
    inner = MH * MP
    wide = inner // PARTS
    steps = []
    for xx in (0, 1):
        total = 0.0
        for c in (0, 1):
            for y in (0, 1):
                j = 4 * xx + 2 * c + y
                block = got_ref[xx, c, y].astype(F32)
                mamba_ref[j * wide : (j + 1) * wide, :] = block[:, :wide].T
                mamba_ref[inner + j * wide : inner + (j + 1) * wide, :] = block[:, wide : 2 * wide].T
                query_ref[:, j * HD : (j + 1) * HD] = block[:, 2 * wide : 2 * wide + HD]
                total = total + few_ref[xx, c, y, :, 128:].astype(F32)
        steps.append(total[:, : MH // 2])
    def pair(first, second, start, width):
        return jnp.concatenate([v[:, start : start + width].astype(F32) for v in (first, second)], axis=1)

    for xx in (0, 1):
        cols = slice(xx * HD, (xx + 1) * HD)
        key_ref[:, cols] = pair(few_ref[xx, 0, 0], few_ref[xx, 0, 1], 0, HD // 2)
        value_ref[:, cols] = pair(few_ref[xx, 1, 0], few_ref[xx, 1, 1], 0, HD // 2)
    for c in (0, 1):
        for y in (0, 1):
            first = 2 * inner + (2 * c + y) * (NST // 2)
            mamba_ref[first : first + NST // 2, :] = pair(
                few_ref[0, c, y], few_ref[1, c, y], HD // 2, NST // 4
            ).T
    rest = jnp.zeros((steps[0].shape[0], 128 - MH), F32)
    mamba_ref[2 * inner + 2 * NST :, :] = jnp.concatenate(steps + [rest], axis=1).T[:MH]

    own, across = own_ref[...], across_ref[...]
    sides = [jnp.where(x == 0, own, across), jnp.where(x == 0, across, own)]
    half, first = own.shape[1], out_ref.shape[0]
    second = first + attn_ref.shape[0]
    units = down_ref.shape[0] // 2
    for xx in (0, 1):
        side = sides[xx].astype(F32)
        cols = slice(xx * half, (xx + 1) * half)
        out_ref[:, cols] = side[:first]
        attn_ref[:, cols] = side[first:second]
        mine = own_down[...].astype(F32), across_down[...].astype(F32)
        down_ref[xx * units : (xx + 1) * units] = jnp.where(x == xx, *mine)


def finish_call(got, few, own, across, own_down, across_down, shapes):
    vmem = pl.BlockSpec(memory_space=pltpu.VMEM)
    return pl.pallas_call(
        finish_kernel,
        in_specs=[vmem] * 6,
        out_specs=[vmem] * 7,
        out_shape=[jax.ShapeDtypeStruct(v, F32) for v in shapes],
        compiler_params=pltpu.CompilerParams(vmem_limit_bytes=VMEM),
        name="finish",
    )(got, few, own, across, own_down, across_down)


def flip(value, *axes):
    count = 2 ** len(axes)
    pairs = [(i, count - 1 - i) for i in range(count)]
    axes = tuple(sorted(axes, key=MESH_AXES.index))
    return lax.ppermute(value, axes, pairs)


def ordered(own, other, axis):
    second = lax.axis_index(axis) == 1
    return jnp.where(second, other, own), jnp.where(second, own, other)


def halves_of(value, axis, dim):
    at = lax.axis_index(axis)
    kept = lax.dynamic_index_in_dim(value, at, dim, keepdims=False)
    return kept, lax.dynamic_index_in_dim(value, 1 - at, dim, keepdims=False).astype(BF)


def part_index():
    return 4 * lax.axis_index("x") + 2 * lax.axis_index("c") + lax.axis_index("y")


def half_columns(weight):
    half = weight.shape[1] // 2
    return lax.dynamic_slice_in_dim(weight, lax.axis_index("x") * half, half, 1)


def exchange_blocks(blocks, high, low):
    h, l = lax.axis_index(high), lax.axis_index(low)
    return [
        lax.dynamic_index_in_dim(blocks, 2 * (h ^ dh) + (l ^ dl), 0, keepdims=False)
        for dh in (0, 1)
        for dl in (0, 1)
    ]


def exchanged(blocks, high, low, late):
    own, for_low, for_high, for_both = blocks
    got = [flip(for_low, low), flip(for_high, high), flip(for_both, high, low)]
    by_low, by_high, by_both = after(got, late)
    near, far = ordered(own, by_low, low), ordered(by_high, by_both, low)
    first, second = ordered(near[0], far[0], high), ordered(near[1], far[1], high)
    return [[first[0], second[0]], [first[1], second[1]]]


def sum_blocks(part):
    rows = part.shape[0] // 4
    y, c = lax.axis_index("y"), lax.axis_index("c")
    return [
        lax.dynamic_slice_in_dim(part, (2 * (y ^ dy) + (c ^ dc)) * rows, rows, 0)
        for dc in (0, 1)
        for dy in (0, 1)
    ]


def whole_rows(weights):
    parts = []
    for w in weights:
        whole = lax.all_gather(w, FSDP, axis=0, tiled=True)
        rows = whole.shape[0] // PARTS
        parts.append(lax.dynamic_slice_in_dim(whole, part_index() * rows, rows, 0))
    return jnp.concatenate(parts)


def joined_rows(got, pieces):
    whole = jnp.stack([jnp.concatenate([got[0][c], got[1][c]], axis=1) for c in (0, 1)])
    outs, at = [], 0
    for count in pieces:
        outs.append(whole[:, at : at + count].reshape(2 * count, -1))
        at += count
    return jnp.concatenate(outs)


def rows_blocks(grad, pieces):
    cols, grad = grad.shape[1] // 2, grad.astype(BF)
    if lax.axis_size("z") != 4:
        parts = []
        for i, count in enumerate(pieces):
            g = grad[sum(pieces[:i]) : sum(pieces[: i + 1])]
            whole = jnp.zeros((count * PARTS, 2 * cols), BF)
            parts.append(
                lax.dynamic_update_slice_in_dim(whole, g, part_index() * g.shape[0], 0)
            )
        return parts
    x, c = lax.axis_index("x"), lax.axis_index("c")
    blocks = []
    for dx in (0, 1):
        for dc in (0, 1):
            block, at = [], 0
            for count in pieces:
                start = (at + (c ^ dc) * (count // 2), (x ^ dx) * cols)
                block.append(lax.dynamic_slice(grad, start, (count // 2, cols)))
                at += count
            blocks.append(jnp.concatenate(block))
    return blocks


def rows_stack(moved):
    if lax.axis_size("z") != 4:
        return moved
    return jnp.stack([moved[0][0], moved[0][1], moved[1][0], moved[1][1]])


def rows_sum(moved):
    if lax.axis_size("z") != 4:
        parts = []
        for whole in moved:
            part = lax.psum_scatter(whole, FSDP, scatter_dimension=0, tiled=True)
            parts.append(half_columns(lax.psum(part, "x")))
        return jnp.concatenate(parts)
    return lax.psum_scatter(moved, "z")


def after(value, earlier):
    return lax.optimization_barrier((value, earlier))[0]


def packed(first, arrays):
    lead = first.shape[0]
    flat = jnp.concatenate([a.reshape(lead, -1) for a in arrays], axis=1)
    flat = jnp.pad(flat, ((0, 0), (0, -(flat.shape[1] + 128) % 1024)))
    first = jnp.pad(first, ((0, 0), (0, 128 - first.shape[1])))
    return jnp.concatenate([first, flat], axis=1).reshape(lead, -1, 128)


def shards(
    tokens,
    cotangent,
    mixer_gain,
    query_weight,
    key_weight,
    value_weight,
    attn_out_weight,
    mamba_in_weight,
    conv_weight,
    conv_bias,
    decay_log,
    step_bias,
    skip_gain,
    mamba_gain,
    mamba_out_weight,
    ffn_gain,
    gate_weight,
    up_weight,
    down_weight,
):
    token_count, model_dim = tokens.shape[1], tokens.shape[2]
    length = 2 * token_count
    inner = MH * MP
    channels = inner + 2 * NST
    part = part_index()
    wide, heads = inner // PARTS, MH // PARTS
    rows = token_count * PARTS
    seqs = rows // length
    fsdp = lax.axis_size("z") * 4

    smalls = [ffn_gain, mamba_gain, conv_bias, conv_weight]
    little = packed(mixer_gain[None].astype(F32), [v[None].astype(F32) for v in smalls])[0]
    count = query_weight.shape[0]
    own, blocks, units = prepare(
        query_weight, key_weight, value_weight, mamba_in_weight, gate_weight, up_weight
    )
    token_rows = tokens.reshape(token_count, model_dim)
    grad_rows = cotangent.reshape(token_count, model_dim)
    hidden, gathered_little, w_in, units, incoming = start_call(
        token_rows, little, own, blocks, units, grad_rows
    )
    hidden = hidden.reshape(rows, model_dim)
    incoming = incoming.reshape(rows, model_dim)
    w_in = w_in.reshape(model_dim, -1)
    fast = lax.axis_size("z") == 4
    out_weights = [mamba_out_weight, attn_out_weight]
    out_pieces = [w.shape[0] for w in out_weights]
    if fast:
        out_blocks = half_columns(jnp.concatenate(out_weights))
        out_blocks = lax.all_gather(out_blocks, "z", axis=0, tiled=False)
        out_blocks = exchange_blocks(out_blocks, "x", "c")
    w_gateup = lax.all_gather(units.reshape(4 * count, -1), "z", axis=0, tiled=True)
    down_half = down_weight.reshape(2, -1, model_dim)
    down_half = lax.dynamic_index_in_dim(down_half, lax.axis_index("x"), 0, keepdims=False)
    ff = gate_weight.shape[1] // PARTS

    gathered_little = gathered_little.reshape(fsdp, -1)
    gain_in = gathered_little[:, : mixer_gain.size].reshape(-1)
    got, at = [], 128
    for s in smalls:
        got.append(gathered_little[:, at : at + s.size].reshape((fsdp,) + s.shape))
        at += s.size
    gain_ffn, gain_mamba, bias_full = (g.reshape(-1) for g in got[:3])
    conv_full = got[3].transpose(1, 0, 2).reshape(4, channels)
    gain_mamba = lax.dynamic_slice_in_dim(gain_mamba, part * wide, wide, 0)

    def own_heads(v):
        return lax.dynamic_slice_in_dim(v.astype(F32), part * heads, heads, 0)

    heads_rows = jnp.stack([own_heads(v) for v in (decay_log, step_bias, skip_gain)])
    heads_rows = jnp.pad(heads_rows, ((0, 5), (0, 2 * MP - heads)))
    params = [
        lax.dynamic_slice_in_dim(conv_full, part * wide, wide, 1),
        lax.dynamic_slice_in_dim(bias_full, part * wide, wide, 0)[None],
        conv_full[:, inner:],
        bias_full[None, inner:],
        heads_rows,
    ]
    tables = rope_tables(length, HD)

    projected = mm(after(hidden, out_blocks) if fast else hidden, w_in)
    scanned, gated, squares, attended = mixer_forward(seqs, length, projected, params, tables)

    if fast:
        w_out = joined_rows(exchanged(out_blocks, "x", "c", squares), out_pieces)
    else:
        w_out = whole_rows(out_weights)
    squares = plane_total(squares.reshape(-1, 128), 4)
    factor = lax.rsqrt(squares / inner + EPSILON).reshape(rows, 1)
    normal = gated * factor
    normed = (normal * gain_mamba).astype(BF)
    mixed = jnp.concatenate([normed, attended], axis=1)
    block = (2, 2, 2, token_count, model_dim)
    mixer_sum = mm(mixed, w_out).astype(BF).reshape(block)
    second, middle, w_down = middle_calls(mixer_sum, token_rows, gain_ffn[None], down_half)
    w_down = w_down.reshape(ff, model_dim)
    second = second.reshape(rows, model_dim)
    gate_up = mm(second, w_gateup)
    gate_act, up_act = gate_up[:, :ff], gate_up[:, ff:]
    sig_g = jax.nn.sigmoid(gate_act)
    active = (gate_act * sig_g * up_act).astype(BF)

    grad_active = across(incoming, w_down)
    grad_gate = grad_active * up_act * sig_g * (1.0 + gate_act * (1.0 - sig_g))
    grad_up = grad_active * gate_act * sig_g
    grad_gateup = jnp.concatenate([grad_gate.astype(BF), grad_up.astype(BF)], axis=1)
    grad_wgateup = outer_product(second, grad_gateup)
    sum_gateup = lax.psum_scatter(grad_wgateup.astype(BF).reshape(-1, 4 * count, 2 * ff), "z")
    grad_down = outer_product(active, incoming).astype(BF)
    sum_down = lax.psum_scatter(
        grad_down.reshape(-1, ff // lax.axis_size("z"), model_dim), "z"
    )
    result = mm(active, w_down).astype(BF).reshape(block)
    grad_gateup = after(grad_gateup, (grad_down, result))
    grad_second = across(grad_gateup, w_gateup).astype(BF).reshape(block)
    grad_mixer, grad_middle, grad_gain_ffn = middle_calls(
        grad_second, middle, gain_ffn[None], cot=grad_rows
    )
    grad_mixer = grad_mixer.reshape(rows, model_dim)
    result_kept, result_away = halves_of(after(result, grad_mixer), "c", 1)
    result_got = flip(result_away, "c")
    grad_out = outer_product(mixed, after(grad_mixer, result_away))
    row_blocks = rows_blocks(grad_out, [wide, HD])
    grad_mixed = across(after(grad_mixer, row_blocks), w_out)
    grad_normed = grad_mixed[:, :wide]
    grad_gain_mamba = jnp.sum(grad_normed * normal, axis=0)
    scaled = grad_normed * gain_mamba
    dots = jnp.sum(scaled * normal, axis=-1).reshape(-1, 128)
    result_got = after(result_got, dots)
    half = model_dim // 2
    lefts = [halves_of(v[..., :half], "y", 0) for v in (result_kept, result_got)]
    rights = [halves_of(v[..., half:], "x", 1) for v in (result_kept, result_got)]
    left, right = ((a[1].astype(F32) + b[1].astype(F32)).astype(BF) for a, b in (lefts, rights))
    dots = plane_total(after(dots, (left, right)), 5)
    left, right, sum_gateup = after((left, right, sum_gateup), dots)
    gateup_blocks = sum_blocks(sum_gateup)
    row_sums = exchanged(row_blocks, "x", "c", dots) if fast else row_blocks
    row_sums = rows_stack(row_sums)
    down_across = flip(sum_down, "x")
    dots = after(dots, (gateup_blocks, left, right, row_sums, sum_down)).reshape(rows, 1) / inner

    grad_in, gxk, gxb, gmk, gmb, gheads = mixer_backward(
        seqs, length, projected, params, tables, scanned, grad_mixed, gain_mamba[None], factor, dots
    )
    sum_rows = rows_sum(row_sums)
    moved = exchanged(gateup_blocks, "c", "y", grad_in)
    moved = jnp.stack([jnp.stack(g) for g in moved])
    moved_across = flip(moved, "x")
    left, right = after((flip(left, "y"), flip(right, "x")), grad_in)
    lefts = [halves_of(v, "x", 0) for v in (lefts[0][0], lefts[1][0], left)]
    rights = [halves_of(v, "y", 0) for v in (rights[0][0], rights[1][0], right)]

    def three(values, index):
        return sum(v[index].astype(F32) for v in values)

    left, right = three(lefts, 1).astype(BF), three(rights, 1).astype(BF)
    grad_in = after(grad_in, (moved, left, right))
    grad_win = outer_product(hidden, grad_in[:, : 2 * wide + HD]).astype(BF)
    grad_win = grad_win.reshape(-1, 2, 2, count, grad_win.shape[1])
    got_left, got_right = after((flip(left, "x"), flip(right, "y")), grad_win)
    result = jnp.concatenate(
        [three(lefts, 0) + got_left.astype(F32), three(rights, 0) + got_right.astype(F32)], axis=1
    )
    output = (middle + result).astype(BF).reshape(1, token_count, model_dim)
    shard_gate, shard_up = units_call(moved, after(moved_across, grad_win))

    conv_grad = jnp.zeros((4, channels), F32)
    conv_grad = lax.dynamic_update_slice_in_dim(conv_grad, gxk, part * wide, 1)
    conv_grad = conv_grad.at[:, inner:].set(gmk)
    bias_grad = jnp.zeros((channels,), F32)
    bias_grad = lax.dynamic_update_slice_in_dim(bias_grad, gxb[0], part * wide, 0)
    bias_grad = bias_grad.at[inner:].set(gmb[0])
    gain_grad = lax.dynamic_update_slice_in_dim(
        jnp.zeros((inner,), F32), grad_gain_mamba, part * wide, 0
    )
    head_grad = lax.dynamic_update_slice_in_dim(
        jnp.zeros((3, MH), F32), gheads[:3, :heads], part * heads, 1
    )
    scattered = [grad_gain_ffn, gain_grad, bias_grad]
    little = [v.reshape(fsdp, -1) for v in scattered]
    little.append(conv_grad.reshape(4, fsdp, -1).transpose(1, 0, 2).reshape(fsdp, -1))
    little.append(jnp.broadcast_to(head_grad.reshape(1, -1), (fsdp, 3 * MH)))
    little = packed(jnp.zeros((fsdp, count), F32), little)
    little = little.reshape((-1, 2, 2) + little.shape[1:])
    tokens_grad, total, got_in, got_few, rows_across = last_call(
        token_rows, gain_in[None], grad_middle, little, grad_win, after(grad_in, (left, right)),
        hidden, w_in, sum_rows,
    )
    tokens_grad = tokens_grad.reshape(1, token_count, model_dim)
    total = total.reshape(-1)
    got, at = [total[:count]], 128
    for like in (ffn_gain, mamba_gain, conv_bias, conv_weight, head_grad):
        got.append(total[at : at + like.size].reshape(like.shape))
        at += like.size

    weights = [query_weight, key_weight, value_weight, mamba_in_weight.T]
    weights += [mamba_out_weight, attn_out_weight, down_weight]
    (
        shard_query, shard_key, shard_value, shard_mamba_in,
        shard_mamba_out, shard_attn_out, shard_down,
    ) = finish_call(
        got_in, got_few, sum_rows, rows_across, sum_down, down_across, [w.shape for w in weights]
    )

    return (
        output,
        tokens_grad,
        got[0],
        shard_query,
        shard_key,
        shard_value,
        shard_attn_out,
        shard_mamba_in.T,
        got[4],
        got[3],
        got[5][0],
        got[5][1],
        got[5][2],
        got[2],
        shard_mamba_out,
        got[1],
        shard_gate,
        shard_up,
        shard_down,
    )


def solution(mesh):
    fsdp = mesh.shape["fsdp"]
    grid = Mesh(mesh.devices.reshape(2, fsdp // 4, 2, 2), ("x", "z", "y", "c"))
    rows, flat, whole = P(FSDP, None), P(FSDP), P()
    stream = P(FSDP, "x", None)
    weights = (
        flat, rows, rows, rows, rows, rows, P(None, FSDP), flat, whole, whole, whole,
        flat, rows, flat, rows, rows, rows,
    )
    return jax.shard_map(
        shards,
        mesh=grid,
        in_specs=(stream, stream) + weights,
        out_specs=(stream, stream) + weights,
        check_vma=False,
    )
```

```python
import math

import jax
import jax.numpy as jnp
from jax import lax
from jax.experimental import pallas as pl
from jax.experimental.pallas import tpu as pltpu
from jax.sharding import Mesh
from jax.sharding import PartitionSpec as P

HQ = 8
KVH = 2
HD = 128
MH = 48
MP = 64
NST = 256
EPSILON = 1e-05
ROPE_BASE = 100000000000.0
MASKED = -1e30
BF = jnp.bfloat16
F32 = jnp.float32
MESH_AXES = ("x", "z", "y", "c")
FSDP = ("z", "y", "c")
PARTS = 8
VMEM = 48 * 1024 * 1024


def mm(left, right):
    return jnp.dot(left, right, preferred_element_type=F32)


def outer_product(left, right):
    return lax.dot_general(left, right, (((0,), (0,)), ((), ())), preferred_element_type=F32)


def across(left, right):
    return lax.dot_general(left, right, (((1,), (1,)), ((), ())), preferred_element_type=F32)


def rope_tables(length, head_size):
    half_size = head_size // 2
    frequency = jnp.exp(
        jnp.arange(half_size, dtype=F32) * (-2.0 * math.log(ROPE_BASE) / head_size)
    )
    angles = jnp.arange(length, dtype=F32)[:, None] * frequency[None, :]
    cosine, sine = jnp.cos(angles), jnp.sin(angles)
    return [jnp.concatenate(v, axis=1) for v in ([cosine, cosine], [-sine, sine])]


def silu_parts(values):
    sig = 1.0 / (1.0 + jnp.exp(-values))
    return values * sig, sig


def shifted(values, count):
    if count == 0:
        return values
    rows = values.shape[0]
    at = lax.broadcasted_iota(jnp.int32, values.shape, 0)
    kept = (at >= count) if count > 0 else (at < rows + count)
    return jnp.where(kept, pltpu.roll(values, count % rows, 0), 0.0)


def conv_silu(signal, kernel, bias):
    taps = kernel.shape[0]
    total = bias + signal * kernel[taps - 1 : taps]
    for back in range(1, taps):
        total = total + shifted(signal, back) * kernel[taps - 1 - back : taps - back]
    value, sig = silu_parts(total)
    return value, sig * (1.0 + total * (1.0 - sig))


def conv_grads(signal, kernel, grad):
    taps = kernel.shape[0]
    back = grad * kernel[taps - 1 : taps]
    rows = []
    for count in range(taps - 1, 0, -1):
        rows.append(jnp.sum(shifted(signal, count) * grad, axis=0, keepdims=True))
        back = back + shifted(grad, -count) * kernel[taps - 1 - count : taps - count]
    rows.append(jnp.sum(signal * grad, axis=0, keepdims=True))
    return back, jnp.concatenate(rows, axis=0), jnp.sum(grad, axis=0, keepdims=True)


def dot(left, right, dims=((1,), (0,)), precision=None):
    return lax.dot_general(
        left, right, (dims, ((), ())), preferred_element_type=F32, precision=precision
    )


ROWS = ((0,), (0,))
LANES = ((1,), (1,))
PRECISE = lax.Precision.HIGHEST


def step_place():
    return (MH // PARTS) * (2 * lax.axis_index("c") + lax.axis_index("y"))


def scan_parts(x_ref, m_refs, s_ref, xk_ref, xb_ref, mk_ref, mb_ref, h_ref):
    length = x_ref.shape[0]
    xin = x_ref[...].astype(BF).astype(F32)
    maps = jnp.concatenate([ref[...].astype(BF).astype(F32) for ref in m_refs], axis=1)
    xs, xslope = conv_silu(xin, xk_ref[...], xb_ref[...])
    mv, mslope = conv_silu(maps, mk_ref[...], mb_ref[...])
    mv = mv.astype(BF)
    bees, cees = mv[:, :NST], mv[:, NST:]
    raw = pltpu.roll(s_ref[...].astype(BF).astype(F32), 2 * MP - step_place(), 1) + h_ref[1:2]
    dt = jnp.maximum(raw, 0.0) + jnp.log1p(jnp.exp(-jnp.abs(raw)))
    rate = -jnp.exp(h_ref[0:1])
    t = lax.broadcasted_iota(jnp.int32, (length, length), 0)
    s = lax.broadcasted_iota(jnp.int32, (length, length), 1)
    lower = (t >= s).astype(F32)
    cum = dot(lower, dt * rate, precision=PRECISE)
    coupling = dot(cees, bees, LANES)
    return xin, maps, xs, xslope, mslope, bees, cees, raw, dt, rate, lower, cum, coupling


def lane_pair(values, first):
    lane = lax.broadcasted_iota(jnp.int32, (values.shape[0], 2 * MP), 1)
    return jnp.where(lane < MP, values[:, first : first + 1], values[:, first + 1 : first + 2])


def decay_of(cum, cumt, lower, head):
    gap = cum[:, head : head + 1] - cumt[head : head + 1, :]
    return jnp.exp(jnp.where(lower > 0.0, gap, MASKED))


def rotated(ref, cos_ref, sin_ref):
    value = ref[...].astype(BF).astype(F32)
    return (value * cos_ref[...] + pltpu.roll(value, HD // 2, 1) * sin_ref[...]).astype(BF)


def causal_scores(rq, rk):
    length = rq.shape[0]
    t = lax.broadcasted_iota(jnp.int32, (length, length), 0)
    s = lax.broadcasted_iota(jnp.int32, (length, length), 1)
    scores = jnp.where(t >= s, dot(rq, rk, LANES) * HD ** (-0.5), MASKED)
    highest = jnp.max(scores, axis=1, keepdims=True)
    weights = jnp.exp(scores - highest)
    return weights, jnp.sum(weights, axis=1, keepdims=True)


def mixer_kernel(
    x_ref, m0_ref, m1_ref, m2_ref, m3_ref, s_ref, z_ref, q_ref, k_ref, v_ref, xk_ref, xb_ref, mk_ref, mb_ref, h_ref,
    cos_ref, sin_ref, scan_ref, gated_ref, square_ref, att_ref,
):
    xin, maps, xs, xslope, mslope, bees, cees, raw, dt, rate, lower, cum, coupling = scan_parts(
        x_ref, (m0_ref, m1_ref, m2_ref, m3_ref), s_ref, xk_ref, xb_ref, mk_ref, mb_ref, h_ref
    )
    cumt = cum.T
    lane = lax.broadcasted_iota(jnp.int32, (xs.shape[0], 2 * MP), 1)
    squares = jnp.zeros((xs.shape[0], 1), F32)
    for pair in range(xs.shape[1] // (2 * MP)):
        cols = slice(2 * MP * pair, 2 * MP * (pair + 1))
        xp = xs[:, cols]
        xr = (xp * lane_pair(dt, 2 * pair)).astype(BF)
        ys = []
        for head in (2 * pair, 2 * pair + 1):
            mixing = (coupling * decay_of(cum, cumt, lower, head)).astype(BF)
            ys.append(dot(mixing, xr))
        y = jnp.where(lane < MP, ys[0], ys[1]) + lane_pair(h_ref[2:3], 2 * pair) * xp
        y = y.astype(BF)
        scan_ref[:, cols] = y
        gated = y.astype(F32) * silu_parts(z_ref[:, cols])[0]
        gated_ref[:, cols] = gated
        squares = squares + jnp.sum(gated * gated, axis=1, keepdims=True)
    square_ref[...] = squares
    weights, total = causal_scores(
        rotated(q_ref, cos_ref, sin_ref), rotated(k_ref, cos_ref, sin_ref)
    )
    att_ref[...] = dot((weights / total).astype(BF), v_ref[...].astype(BF)).astype(BF)


def mixer_back_kernel(
    x_ref, m0_ref, m1_ref, m2_ref, m3_ref, s_ref, z_ref, q_ref, k_ref, v_ref, xk_ref, xb_ref, mk_ref, mb_ref, h_ref,
    cos_ref, sin_ref, scan_ref, gn_ref, gain_ref, factor_ref, dots_ref, ga_ref,
    gin_ref,
    gxk_ref, gxb_ref, gmk_ref, gmb_ref, gh_ref,
):
    xin, maps, xs, xslope, mslope, bees, cees, raw, dt, rate, lower, cum, coupling = scan_parts(
        x_ref, (m0_ref, m1_ref, m2_ref, m3_ref), s_ref, xk_ref, xb_ref, mk_ref, mb_ref, h_ref
    )
    length, width = xs.shape
    cumt = cum.T
    lane = lax.broadcasted_iota(jnp.int32, (length, 2 * MP), 1)
    factor, dots = factor_ref[...], dots_ref[...]
    gcoup = jnp.zeros((length, length), F32)
    gcum = jnp.zeros((length, 2 * MP), F32)
    gdt = jnp.zeros((length, 2 * MP), F32)
    gskip = jnp.zeros((1, 2 * MP), F32)
    gus = []
    for pair in range(width // (2 * MP)):
        cols = slice(2 * MP * pair, 2 * MP * (pair + 1))
        gate, scanned = z_ref[:, cols], scan_ref[:, cols].astype(F32)
        silu_z, sig_z = silu_parts(gate)
        normal = scanned * silu_z * factor
        ggated = factor * (gn_ref[:, cols] * gain_ref[:, cols] - normal * dots)
        gin_ref[:, cols] = (ggated * scanned * sig_z * (1.0 + gate * (1.0 - sig_z))).astype(BF)
        gy = (ggated * silu_z).astype(BF)
        gyf = gy.astype(F32)
        xp, dtp = xs[:, cols], lane_pair(dt, 2 * pair)
        xr = (xp * dtp).astype(BF)
        ys, gxrs = [], []
        for own, head in enumerate((2 * pair, 2 * pair + 1)):
            mine = (lane < MP) if own == 0 else (lane >= MP)
            decay = decay_of(cum, cumt, lower, head)
            mixing = (coupling * decay).astype(BF)
            ys.append(dot(mixing, xr))
            gxrs.append(dot(mixing, gy, ROWS))
            gcoup = gcoup + dot(jnp.where(mine, gy, jnp.zeros_like(gy)), xr, LANES) * decay
        y = jnp.where(lane < MP, ys[0], ys[1])
        gxr = jnp.where(lane < MP, gxrs[0], gxrs[1])
        flow, drive, direct = gyf * y - xr.astype(F32) * gxr, gxr * xp, gyf * xp
        for own, head in enumerate((2 * pair, 2 * pair + 1)):
            mine = (lane < MP) if own == 0 else (lane >= MP)

            def share(v):
                return jnp.sum(jnp.where(mine, v, 0.0), axis=1, keepdims=True)

            gcum = jnp.where(lane == head, share(flow), gcum)
            gdt = jnp.where(lane == head, share(drive), gdt)
            gskip = jnp.where(
                lane[:1] == head, jnp.sum(share(direct), axis=0, keepdims=True), gskip
            )
        gus.append((gxr * dtp + lane_pair(h_ref[2:3], 2 * pair) * gyf) * xslope[:, cols])
    gu = jnp.concatenate(gus, axis=1)
    gx, gxk, gxb = conv_grads(xin, xk_ref[...], gu)
    gin_ref[:, width : 2 * width] = gx.astype(BF)
    gflow = dot(lower, gcum, ROWS, precision=PRECISE)
    gdt = gdt + gflow * rate
    graw = gdt / (1.0 + jnp.exp(-raw))
    graw = jnp.where(lane < width // MP, graw, 0.0)
    common = 2 * width + HD
    gin_ref[:, common + 2 * NST + 2 * HD :] = pltpu.roll(graw, step_place(), 1).astype(BF)
    gdecay = jnp.sum(gflow * dt, axis=0, keepdims=True) * rate
    gcb = gcoup.astype(BF)
    gmaps = jnp.concatenate([dot(gcb, cees, ROWS), dot(gcb, bees)], axis=1) * mslope
    gm, gmk, gmb = conv_grads(maps, mk_ref[...], gmaps)
    gin_ref[:, common : common + 2 * NST] = gm.astype(BF)
    gh = jnp.concatenate([gdecay, jnp.sum(graw, axis=0, keepdims=True), gskip], axis=0)

    @pl.when(pl.program_id(0) == 0)
    def _():
        for ref in (gxk_ref, gxb_ref, gmk_ref, gmb_ref, gh_ref):
            ref[...] = jnp.zeros_like(ref)

    gxk_ref[...] += gxk
    gxb_ref[...] += gxb
    gmk_ref[...] += gmk
    gmb_ref[...] += gmb
    gh_ref[0:3] += gh

    rq, rk = rotated(q_ref, cos_ref, sin_ref), rotated(k_ref, cos_ref, sin_ref)
    weights, total = causal_scores(rq, rk)
    probs = weights / total
    gatt = ga_ref[...].astype(BF)
    kv = common + 2 * NST
    gin_ref[:, kv + HD : kv + 2 * HD] = dot(probs.astype(BF), gatt, ROWS).astype(BF)
    gp = dot(gatt, v_ref[...].astype(BF), LANES)
    gsc = (probs * (gp - jnp.sum(probs * gp, axis=1, keepdims=True))).astype(BF)
    for at, grad in ((2 * width, dot(gsc, rk)), (kv, dot(gsc, rq, ROWS))):
        grad = grad * HD ** (-0.5)
        back = grad * cos_ref[...] - pltpu.roll(grad, HD // 2, 1) * sin_ref[...]
        gin_ref[:, at : at + HD] = back.astype(BF)


def column_block(length, width, at):
    return pl.BlockSpec((length, width), lambda i: (i, at // width))


def mixer_specs(length, wide):
    maps = 2 * wide + HD
    return (
        [column_block(length, wide, wide)]
        + [column_block(length, NST // 2, maps + at) for at in range(0, 2 * NST, NST // 2)]
        + [
            column_block(length, 2 * MP, maps + 2 * NST + 2 * HD),
            column_block(length, wide, 0),
            column_block(length, HD, 2 * wide),
            column_block(length, HD, maps + 2 * NST),
            column_block(length, HD, maps + 2 * NST + HD),
        ]
    )


def whole_specs(arrays):
    return [pl.BlockSpec(a.shape, lambda i: (0, 0)) for a in arrays]


def mixer_forward(seqs, length, projected, params, tables):
    wide = params[0].shape[1]
    outs = [(wide, BF), (wide, F32), (1, F32), (HD, BF)]
    return pl.pallas_call(
        mixer_kernel,
        grid=(seqs,),
        in_specs=mixer_specs(length, wide) + whole_specs(params + tables),
        out_specs=[column_block(length, w, 0) for w, _ in outs],
        out_shape=[jax.ShapeDtypeStruct((seqs * length, w), d) for w, d in outs],
        compiler_params=pltpu.CompilerParams(vmem_limit_bytes=VMEM),
        name="mixer",
    )(*[projected] * 10, *params, *tables)


def mixer_backward(seqs, length, projected, params, tables, scanned, grad_mixed, gain, factor, dots):
    wide = params[0].shape[1]
    outs = [projected.shape[1]]
    sums = [(4, wide), (1, wide), (4, 2 * NST), (1, 2 * NST), (8, 2 * MP)]
    row_specs = [column_block(length, wide, 0), column_block(length, wide, 0)]
    tail_specs = [column_block(length, 1, 0), column_block(length, 1, 0), column_block(length, HD, wide)]
    return pl.pallas_call(
        mixer_back_kernel,
        grid=(seqs,),
        in_specs=mixer_specs(length, wide) + whole_specs(params + tables)
        + row_specs + whole_specs([gain]) + tail_specs,
        out_specs=[column_block(length, w, 0) for w in outs]
        + [pl.BlockSpec(s, lambda i: (0, 0)) for s in sums],
        out_shape=[jax.ShapeDtypeStruct((seqs * length, w), BF) for w in outs]
        + [jax.ShapeDtypeStruct(s, F32) for s in sums],
        compiler_params=pltpu.CompilerParams(vmem_limit_bytes=VMEM),
        name="mixer_back",
    )(
        *[projected] * 10, *params, *tables, scanned, grad_mixed, gain, factor, dots, grad_mixed,
    )


def remote(src, dst, send, recv, axis):
    other = 1 - lax.axis_index(axis)
    return pltpu.make_async_remote_copy(
        src_ref=src,
        dst_ref=dst,
        send_sem=send,
        recv_sem=recv,
        device_id={axis: other},
        device_id_type=pl.DeviceIdType.MESH,
    )


def greet(axes):
    barrier = pltpu.get_barrier_semaphore()
    for axis in axes:
        other = 1 - lax.axis_index(axis)
        pl.semaphore_signal(
            barrier, inc=1, device_id={axis: other}, device_id_type=pl.DeviceIdType.MESH
        )
    pl.semaphore_wait(barrier, len(axes))


def line_item(region, sems, sources=None):
    z, n = lax.axis_index("z"), lax.axis_size("z")

    def copy(way, k, at, src):
        return pltpu.make_async_remote_copy(
            src_ref=src,
            dst_ref=region(at),
            send_sem=sems.at[0, way, k],
            recv_sem=sems.at[1, way, k],
            device_id={"z": z + 1 - 2 * way},
            device_id_type=pl.DeviceIdType.MESH,
        )

    def send(k):
        src = sources if k == 0 and sources is not None else None

        @pl.when((z + 1 < n) & (z - k >= 0))
        def _():
            copy(0, k, z - k, region(z - k) if src is None else src).start()

        @pl.when((z >= 1) & (z + k < n))
        def _():
            copy(1, k, z + k, region(z + k) if src is None else src).start()

    def arrive(k):
        @pl.when(z - 1 - k >= 0)
        def _():
            copy(0, k, z - 1 - k, region(z - 1 - k)).wait_recv()

        @pl.when(z + 1 + k < n)
        def _():
            copy(1, k, z + 1 + k, region(z + 1 + k)).wait_recv()

    def finish():
        for k in range(n - 1):
            src = sources if k == 0 and sources is not None else None

            @pl.when((z + 1 < n) & (z - k >= 0))
            def _(k=k, src=src):
                copy(0, k, z - k, region(z - k) if src is None else src).wait_send()

            @pl.when((z >= 1) & (z + k < n))
            def _(k=k, src=src):
                copy(1, k, z + k, region(z + k) if src is None else src).wait_send()

    return send, arrive, finish


def gather_regions(region, half, sems, own_ready, own=None):
    x, y, c = (lax.axis_index(a) for a in ("x", "y", "c"))
    sent = []

    def send(i, ref, axis, src=None):
        src = ref if src is None else src
        copy = remote(src, ref, sems.at[0, i], sems.at[1, i], axis)
        copy.start()
        sent.append(copy)

    def got(i, ref, axis):
        remote(ref, ref, sems.at[0, i], sems.at[1, i], axis).wait_recv()

    def begin():
        if own is None:
            own_ready()
        for i, axis in enumerate(("x", "y", "c")):
            send(i, region(x, y, c), axis, own)

    def forward():
        got(0, region(1 - x, y, c), "x")
        send(3, half(region(1 - x, y, c), 0), "y")
        send(4, region(1 - x, y, c), "c")
        got(1, region(x, 1 - y, c), "y")
        send(5, half(region(x, 1 - y, c), 1), "x")
        send(6, region(x, 1 - y, c), "c")

    def end():
        got(3, half(region(1 - x, 1 - y, c), 0), "y")
        got(5, half(region(1 - x, 1 - y, c), 1), "x")
        send(7, region(1 - x, 1 - y, c), "c")
        got(2, region(x, y, 1 - c), "c")
        got(4, region(1 - x, y, 1 - c), "c")
        got(6, region(x, 1 - y, 1 - c), "c")
        got(7, region(1 - x, 1 - y, 1 - c), "c")
        for copy in sent:
            copy.wait_send()
        if own is not None:
            own_ready()

    return begin, forward, end


def greet_all():
    barrier = pltpu.get_barrier_semaphore()
    x, z, y, c = (lax.axis_index(a) for a in ("x", "z", "y", "c"))
    n = lax.axis_size("z")

    def tell(where):
        pl.semaphore_signal(
            barrier, inc=1, device_id=where, device_id_type=pl.DeviceIdType.MESH
        )

    for where in ({"x": 1 - x}, {"y": 1 - y}, {"c": 1 - c}, {"y": 1 - y, "c": 1 - c}):
        tell(where)

    @pl.when(z >= 1)
    def _():
        tell({"z": z - 1})

    @pl.when(z + 1 < n)
    def _():
        tell({"z": z + 1})

    pl.semaphore_wait(barrier, 4 + jnp.minimum(z, 1) + jnp.minimum(n - 1 - z, 1))


def sum_scratch(count, width):
    half = width // 2
    return [
        pltpu.VMEM((2, 2, 2, count, half), BF),
        pltpu.VMEM((2, 2, count, half), BF),
        pltpu.VMEM((2, 2, count, half), BF),
        pltpu.VMEM((2, count, half), BF),
        pltpu.VMEM((2, count, half), BF),
        pltpu.SemaphoreType.DMA((2, 6)),
    ]


def reduce_plane(part, scratch, firsts=("y", "x")):
    core, wide_in, wide_out, thin_in, thin_out, sems = scratch
    half = part.shape[4] // 2
    x, y, c = (lax.axis_index(a) for a in ("x", "y", "c"))
    seconds = ["x" if axis == "y" else "y" for axis in firsts]
    cols = [slice(0, half), slice(half, 2 * half)]

    def chip(i, yy, xx):
        return part[yy, c, xx, :, cols[i]].astype(F32) + core[i, yy, xx].astype(F32)

    def kept(i, index):
        mine = chip(i, y, index) if firsts[i] == "y" else chip(i, index, x)
        return mine + wide_in[i, index].astype(F32)

    copies = [
        remote(part.at[:, 1 - c, :, :, cols[i]], core.at[i], sems.at[0, i], sems.at[1, i], "c")
        for i in (0, 1)
    ]
    wides = [
        remote(wide_out.at[i], wide_in.at[i], sems.at[0, 2 + i], sems.at[1, 2 + i], firsts[i])
        for i in (0, 1)
    ]
    thins = [
        remote(thin_out.at[i], thin_in.at[i], sems.at[0, 4 + i], sems.at[1, 4 + i], seconds[i])
        for i in (0, 1)
    ]

    def begin():
        for copy in copies:
            copy.start()

    def wide(which=(0, 1)):
        for i in which:
            copies[i].wait()
            for k in (0, 1):
                away = chip(i, 1 - y, k) if firsts[i] == "y" else chip(i, k, 1 - x)
                wide_out[i, k] = away.astype(BF)
            wides[i].start()

    def thin():
        for i in (0, 1):
            wides[i].wait()
            thin_out[i] = kept(i, 1 - x if firsts[i] == "y" else 1 - y).astype(BF)
            thins[i].start()

    def end():
        outs = []
        for i in (0, 1):
            thins[i].wait()
            outs.append(kept(i, x if firsts[i] == "y" else y) + thin_in[i].astype(F32))
        return jnp.concatenate(outs, axis=1)

    return begin, wide, thin, end


def gathered(block, out, sems, local):
    x, y, c = (lax.axis_index(a) for a in ("x", "y", "c"))
    half = block.shape[0] // 2
    own = pltpu.make_async_copy(block, out.at[y, c, x], local)
    own.start()
    steps = gather_regions(
        lambda x, y, c: out.at[y, c, x],
        lambda ref, i: ref.at[pl.ds(i * half, half)],
        sems,
        own.wait,
        block,
    )
    return steps


def factor_of(values):
    return lax.rsqrt(jnp.mean(values * values, axis=1, keepdims=True) + EPSILON)


def norm_back_parts(values, scaling, grad):
    factor = factor_of(values)
    normal = values * factor
    scaled = grad * scaling
    inner = jnp.mean(scaled * normal, axis=1, keepdims=True)
    return factor * (scaled - normal * inner), jnp.sum(grad * normal, axis=0, keepdims=True)


def middle_kernel(
    part_ref, rows_ref, gain_ref, down_ref, out_ref, middle_ref, whole_ref,
    block, sems, local, down_sems, *scratch,
):
    z, n = lax.axis_index("z"), lax.axis_size("z")
    greet_all()
    begin, wide, thin, end = reduce_plane(part_ref, scratch)
    begin()
    own = pltpu.make_async_copy(down_ref, whole_ref.at[z], local.at[1])
    own.start()
    send, arrive, finish = line_item(lambda at: whole_ref.at[at], down_sems, down_ref)
    send(0)

    def more(k):
        if k < n:
            arrive(k - 1)
        if k < n - 1:
            send(k)

    wide()
    more(1)
    thin()
    middle = rows_ref[...].astype(F32) + end()
    middle_ref[...] = middle
    block[...] = (middle * factor_of(middle) * gain_ref[...]).astype(BF)
    first, *steps = gathered(block, out_ref, sems, local.at[0])
    first()
    more(2)
    for step in steps:
        step()
    for k in range(3, n):
        more(k)
    own.wait()
    finish()


def middle_back_kernel(
    part_ref, rows_ref, gain_ref, cot_ref, active_ref, down_ref, incoming_ref,
    out_ref, grad_ref, gain_grad_ref, down_grad_ref, kept_ref, got_ref,
    block, sems, local, incoming, down_grad, result, more_sems, *scratch,
):
    greet(("x", "y", "c"))
    begin, wide, thin, end = reduce_plane(part_ref, scratch)
    begin()
    load = pltpu.make_async_copy(incoming_ref, incoming, more_sems.at[0])
    load.start()
    wide()
    copies, c = [], lax.axis_index("c")
    count = active_ref.shape[0] // 4
    for side in (1, 0):
        for yy in (0, 1):
            rows = pl.multiple_of((2 * yy + ((1 - c) if side else c)) * count, 16)
            into = result.at[side, yy]
            into[...] = dot(active_ref[pl.ds(rows, count), :], down_ref[...]).astype(BF)
            if side:
                copy = remote(into, got_ref.at[yy], more_sems.at[1 + yy], more_sems.at[9 + yy], "c")
            else:
                copy = pltpu.make_async_copy(into, kept_ref.at[yy], more_sems.at[3 + yy])
            copy.start()
            copies.append(copy)
    load.wait()
    units = active_ref.shape[1] // 4
    for i in range(4):
        rows = pl.ds(i * units, units)
        down_grad[rows, :] = dot(active_ref[:, rows], incoming[...], ROWS).astype(BF)
        copies.append(
            pltpu.make_async_copy(down_grad.at[rows], down_grad_ref.at[rows], more_sems.at[5 + i])
        )
        copies[4 + i].start()
    thin()
    grad, gain_grad_ref[...] = norm_back_parts(rows_ref[...], gain_ref[...], end())
    grad = grad + cot_ref[...].astype(F32)
    grad_ref[...] = grad
    block[...] = grad.astype(BF)
    for step in gathered(block, out_ref, sems, local.at[0]):
        step()
    for copy in copies:
        copy.wait()


def middle_calls(part, rows, gain, down, cot=None, active=None, incoming=None):
    n = lax.axis_size("z")
    count, width = rows.shape
    vmem, hbm = pl.BlockSpec(memory_space=pltpu.VMEM), pl.BlockSpec(memory_space=pl.ANY)
    dma = pltpu.SemaphoreType.DMA
    out = [jax.ShapeDtypeStruct((2, 2, 2, count, width), BF), jax.ShapeDtypeStruct((count, width), F32)]
    scratch = [pltpu.VMEM((count, width), BF), dma((2, 8)), dma((2,))]
    if cot is None:
        inputs, specs = [part, rows, gain, down], [vmem] * 3 + [hbm]
        out += [jax.ShapeDtypeStruct((n,) + down.shape, BF)]
        out_specs = [hbm, vmem, hbm]
        scratch += [dma((2, 2, n))]
    else:
        inputs = [part, rows, gain, cot, active, down, incoming]
        specs = [vmem] * 6 + [hbm]
        half = (2, incoming.shape[0] // 4, width)
        out += [jax.ShapeDtypeStruct((1, width), F32), jax.ShapeDtypeStruct(down.shape, BF)]
        out += [jax.ShapeDtypeStruct(half, BF)] * 2
        out_specs = [hbm, vmem, vmem, hbm, hbm, hbm]
        scratch += [pltpu.VMEM(v, BF) for v in (incoming.shape, down.shape, (2,) + half)]
        scratch += [dma((11,))]
    return pl.pallas_call(
        middle_kernel if cot is None else middle_back_kernel,
        in_specs=specs,
        out_specs=out_specs,
        out_shape=out,
        scratch_shapes=scratch + sum_scratch(count, width),
        compiler_params=pltpu.CompilerParams(
            collective_id=1 if cot is None else 2, has_side_effects=True, vmem_limit_bytes=VMEM
        ),
        name="middle" if cot is None else "middle_back",
    )(*inputs)


def total_kernel(value_ref, out_ref, got, sems):
    greet(("c", "y", "x"))
    out_ref[...] = value_ref[...]
    for i, axis in enumerate(("c", "y", "x")):
        hop = remote(out_ref, got.at[i], sems.at[0, i], sems.at[1, i], axis)
        hop.start()
        hop.wait()
        out_ref[...] = out_ref[...] + got[i]


def plane_total(value, identity):
    vmem = pl.BlockSpec(memory_space=pltpu.VMEM)
    return pl.pallas_call(
        total_kernel,
        in_specs=[vmem],
        out_specs=vmem,
        out_shape=jax.ShapeDtypeStruct(value.shape, F32),
        scratch_shapes=[pltpu.VMEM((3,) + value.shape, F32), pltpu.SemaphoreType.DMA((2, 3))],
        compiler_params=pltpu.CompilerParams(collective_id=identity, has_side_effects=True),
        name="total",
    )(value)


def line_sum(own, inbox, sems):
    z, n = lax.axis_index("z"), lax.axis_size("z")

    def copy(way, k):
        d = k if way else n - 1 - k
        slot = jnp.where(d == z - 1, n, d) if way else d
        return pltpu.make_async_remote_copy(
            src_ref=own(d),
            dst_ref=inbox(slot),
            send_sem=sems.at[0, way, k],
            recv_sem=sems.at[1, way, k],
            device_id={"z": z + 1 - 2 * way},
            device_id_type=pl.DeviceIdType.MESH,
        )

    def add(way, k, d, slot):
        pltpu.make_async_remote_copy(
            src_ref=own(d),
            dst_ref=inbox(slot),
            send_sem=sems.at[0, way, k],
            recv_sem=sems.at[1, way, k],
            device_id={"z": z},
            device_id_type=pl.DeviceIdType.MESH,
        ).wait_recv()
        held = own(d)
        held[...] = (held[...].astype(F32) + inbox(slot)[...].astype(F32)).astype(held.dtype)

    def kick(k):
        @pl.when(z == 0)
        def _():
            copy(0, k).start()

        @pl.when(z == n - 1)
        def _():
            copy(1, k).start()

    def pass_on(way, k):
        d = k if way else n - 1 - k

        @pl.when((z > 0) & (z < n - 1) & (d < z if way else d > z))
        def _():
            add(way, k, d, d)
            copy(way, k).start()

    def end():
        @pl.when(z > 0)
        def _():
            add(0, n - 1 - z, z, z)

        @pl.when(z < n - 1)
        def _():
            add(1, z, z, n)

    def finish():
        for k in range(n - 1):
            for way in (0, 1):
                d = k if way else n - 1 - k

                @pl.when(d < z if way else d > z)
                def _(way=way):
                    copy(way, k).wait_send()

    return kick, pass_on, end, finish


def column_sums(grad_ref, grad, first, boxes, sems):
    by_c, for_y, by_y, for_x, by_x, out = boxes
    x, y, c = (lax.axis_index(a) for a in ("x", "y", "c"))

    def cols(side):
        maps = pl.ds(pl.multiple_of(first + side * NST, 128), NST)
        kv = pl.ds(pl.multiple_of(first + 2 * NST + side * HD, 128), HD)
        return (maps, pl.ds(0, NST)), (kv, pl.ds(NST, HD))

    def own():
        return jnp.concatenate([grad[:, src] for src, _ in cols(c)], axis=1).astype(F32)

    across = [
        remote(grad_ref.at[:, src], by_c.at[:, dst], sems.at[0, i], sems.at[1, i], "c")
        for i, (src, dst) in enumerate(cols(1 - c))
    ]
    over_y = remote(for_y, by_y, sems.at[0, 2], sems.at[1, 2], "y")
    over_x = remote(for_x, by_x, sems.at[0, 3], sems.at[1, 3], "x")

    def begin():
        for copy in across:
            copy.start()

    def halves(value, side):
        maps, kv = value[:, :NST], value[:, NST:]
        maps = jnp.where(side == 0, maps[:, : NST // 2], maps[:, NST // 2 :])
        kv = jnp.where(side == 0, kv[:, : HD // 2], kv[:, HD // 2 :])
        return maps, kv

    def second():
        for copy in across:
            copy.wait()
        maps, kv = halves(own() + by_c[...].astype(F32), 1 - y)
        for_y[...] = jnp.concatenate([maps, kv, kv], axis=1).astype(BF)
        over_y.start()

    def summed():
        got = by_y[...].astype(F32)
        maps, kv = halves(own() + by_c[...].astype(F32), y)
        return maps + got[:, : NST // 2], kv + got[:, NST // 2 : NST // 2 + HD // 2]

    def third():
        over_y.wait()
        maps, kv = summed()
        away = jnp.where(x == 0, maps[:, NST // 4 :], maps[:, : NST // 4])
        for_x[...] = jnp.concatenate([away, away], axis=1).astype(BF)
        over_x.start()

    def end():
        over_x.wait()
        maps, kv = summed()
        maps = jnp.where(x == 0, maps[:, : NST // 4], maps[:, NST // 4 :])
        maps = maps + by_x[...].astype(F32)[:, : NST // 4]
        out[:, 0:128] = jnp.concatenate([kv, maps], axis=1).astype(BF)
        out[:, 128:256] = grad[:, first + 2 * NST + 2 * HD :]

    return begin, second, third, end


def hand_out(held, swap, got, places, sems, own_sems):
    x, y, c = (lax.axis_index(a) for a in ("x", "y", "c"))
    moves, kept = [], []

    def give(i):
        yy, cc = places[i]
        if i == 3:
            swap[c, y] = held(yy, cc)[...]
            return
        move = pltpu.make_async_remote_copy(
            src_ref=held(yy, cc),
            dst_ref=swap.at[c, y],
            send_sem=sems.at[0, i],
            recv_sem=sems.at[1, i],
            device_id={"y": yy, "c": cc},
            device_id_type=pl.DeviceIdType.MESH,
        )
        move.start()
        moves.append(move)

    def forward(i):
        yy, cc = places[i]
        if i < 3:
            moves[i].wait_recv()
        keep = pltpu.make_async_copy(swap.at[cc, yy], got.at[x, cc, yy], own_sems.at[i])
        move = remote(swap.at[cc, yy], got.at[x, cc, yy], sems.at[0, 3 + i], sems.at[1, 3 + i], "x")
        for copy in (keep, move):
            copy.start()
            kept.append(copy)

    def finish():
        for copy in kept:
            copy.wait()
        for move in moves:
            move.wait_send()

    return give, forward, finish


def last_kernel(
    rows_ref, gain_ref, grad_ref, little_ref, weight_ref, common_ref, hidden_ref, project_ref,
    rows_in, out_ref, little_out, got_ref, few_ref, rows_out,
    held, inbox, few, few_box, swap, few_swap, little, little_in, little_c, little_y, little_box,
    hidden, common, project, part, col_c, col_y_out, col_y_in, col_x_out, col_x_in, slices,
    local, weight_sems, few_sems, little_sems, hop_sems, swap_sems, few_swap_sems, own_sems,
    cross_sems, col_sems, *scratch,
):
    x, z, y, c = (lax.axis_index(a) for a in ("x", "z", "y", "c"))
    n = lax.axis_size("z")
    greet_all()
    pairs = ((weight_ref, held), (common_ref, common), (project_ref, project), (hidden_ref, hidden))
    loads = [pltpu.make_async_copy(*pair, local.at[i]) for i, pair in enumerate(pairs)]
    for load in loads:
        load.start()
    begin, wide, thin, end = reduce_plane(part, scratch)
    boxes = (col_c, col_y_out, col_y_in, col_x_out, col_x_in, slices)
    col_begin, col_second, col_third, col_end = column_sums(
        common_ref, common, common_ref.shape[1] // 2, boxes, col_sems
    )
    col_begin()
    count = rows_ref.shape[0]

    def product_of(cc, yy):
        for xx in (0, 1):
            first = pl.multiple_of((4 * yy + 2 * cc + xx) * count, 16)
            block = common[pl.ds(first, count), :]
            part[yy, cc, xx] = dot(block, project[...], LANES).astype(BF)

    order = ((1, 1), (1, 0), (0, 1), (0, 0))
    sums, places = [], []
    for i, (dy, dc) in enumerate(order):
        yy, cc = (1 - y) if dy else y, (1 - c) if dc else c
        places.append((yy, cc))
        sums.append(
            line_sum(
                lambda d, yy=yy, cc=cc: held.at[d, yy, cc],
                lambda d, yy=yy, cc=cc: inbox.at[d, yy, cc],
                weight_sems.at[i],
            )
        )
    few_sum = line_sum(lambda d: few.at[d], lambda d: few_box.at[d], few_sems)
    cross = remote(rows_in, rows_out, cross_sems.at[0], cross_sems.at[1], "x")
    loads[0].wait()
    for k in range(n - 1):
        for item in sums:
            item[0](k)

    def pass_on(item, k, far):
        @pl.when(z < n // 2)
        def _():
            item[1](far, k)

        @pl.when(z >= n // 2)
        def _():
            item[1](1 - far, k)

    loads[1].wait()
    col_second()
    loads[2].wait()
    product_of(1 - c, 0)
    pass_on(sums[0], 0, 0)
    product_of(1 - c, 1)
    begin()
    pass_on(sums[1], 0, 0)
    pass_on(sums[0], 0, 1)
    product_of(c, 0)
    pass_on(sums[2], 0, 0)
    pass_on(sums[1], 0, 1)
    product_of(c, 1)
    pass_on(sums[3], 0, 0)
    pass_on(sums[2], 0, 1)
    wide()
    pass_on(sums[3], 0, 1)
    col_third()
    if n > 2:
        for i in (0, 1, 2, 3):
            pass_on(sums[i], 1, 0)
    col_end()
    loads[3].wait()
    product = dot(slices[...], hidden[...], ROWS).T.astype(BF)
    piece = product.shape[0] // (4 * n)
    for at in range(n):
        for yy in (0, 1):
            for cc in (0, 1):
                first = (4 * at + 2 * yy + cc) * piece
                few[at, yy, cc] = product[first : first + piece]
    for k in range(n - 1):
        few_sum[0](k)
    for k in range(1, n - 1):
        for item in sums:
            for far in (0, 1):
                if k > 1 or far == 1:
                    pass_on(item, k, far)
    thin()
    cross.start()

    rows = rows_ref[...].astype(F32)
    grad, gain_grad = norm_back_parts(rows, gain_ref[...], end())
    out_ref[...] = grad + grad_ref[...]
    little[...] = little_ref[...]
    for at in range(n):
        for yy in (0, 1):
            for cc in (0, 1):
                first = (4 * at + 2 * yy + cc) * piece
                little[at, yy, cc, 0:1, 0:piece] = gain_grad[:, first : first + piece]
    hop = remote(little, little_in, hop_sems.at[0, 0], hop_sems.at[1, 0], "x")
    hop.start()

    give, forward, finish = hand_out(
        lambda yy, cc: held.at[z, yy, cc], swap, got_ref, places, swap_sems, own_sems.at[0]
    )
    few_give, few_forward, few_finish = hand_out(
        lambda yy, cc: few.at[z, yy, cc], few_swap, few_ref, places, few_swap_sems, own_sems.at[1]
    )
    for i in (0, 1):
        sums[i][2]()
        give(i)
    hop.wait()
    little[...] = little[...] + little_in[...]
    hop = remote(little.at[:, :, 1 - c], little_c, hop_sems.at[0, 1], hop_sems.at[1, 1], "c")
    hop.start()
    forward(0)
    sums[2][2]()
    give(2)
    forward(1)
    hop.wait()
    for yy in (0, 1):
        little_c[:, yy] = little_c[:, yy] + little[:, yy, c]
    hop = remote(little_c.at[:, 1 - y], little_y, hop_sems.at[0, 2], hop_sems.at[1, 2], "y")
    hop.start()
    sums[3][2]()
    give(3)
    forward(2)
    forward(3)
    pass_on(few_sum, 0, 0)
    hop.wait()
    little_y[...] = little_y[...] + little_c[:, y]
    little_sum = line_sum(lambda d: little_y.at[d], lambda d: little_box.at[d], little_sems)
    for k in range(n - 1):
        little_sum[0](k)
    for k in range(n - 1):
        for far in (0, 1):
            if k > 0 or far == 1:
                pass_on(few_sum, k, far)
    few_sum[2]()
    for i in range(4):
        few_give(i)
    for k in range(n - 1):
        for way in (0, 1):
            little_sum[1](way, k)
    little_sum[2]()
    little_out[...] = little_y[z]
    for i in range(4):
        few_forward(i)
    cross.wait()
    finish()
    few_finish()
    for item in sums + [few_sum, little_sum]:
        item[3]()


def last_call(rows, gain, grad, little, weight, common, hidden, project, sum_rows):
    n = lax.axis_size("z")
    count, width = rows.shape
    total, piece = hidden.shape[0], weight.shape[3]
    block, small, pack = weight.shape[3:], (piece, 256), little.shape[3:]
    vmem, hbm = pl.BlockSpec(memory_space=pltpu.VMEM), pl.BlockSpec(memory_space=pl.ANY)
    dma = pltpu.SemaphoreType.DMA
    return pl.pallas_call(
        last_kernel,
        in_specs=[vmem] * 4 + [hbm] * 5,
        out_specs=[vmem, vmem, hbm, hbm, hbm],
        out_shape=[
            jax.ShapeDtypeStruct((count, width), F32),
            jax.ShapeDtypeStruct(pack, F32),
            jax.ShapeDtypeStruct((2, 2, 2) + block, BF),
            jax.ShapeDtypeStruct((2, 2, 2) + small, BF),
            jax.ShapeDtypeStruct(sum_rows.shape, BF),
        ],
        scratch_shapes=[
            pltpu.VMEM((n, 2, 2) + block, BF),
            pltpu.VMEM((n + 1, 2, 2) + block, BF),
            pltpu.VMEM((n, 2, 2) + small, BF),
            pltpu.VMEM((n + 1, 2, 2) + small, BF),
            pltpu.VMEM((2, 2) + block, BF),
            pltpu.VMEM((2, 2) + small, BF),
            pltpu.VMEM((n, 2, 2) + pack, F32),
            pltpu.VMEM((n, 2, 2) + pack, F32),
            pltpu.VMEM((n, 2) + pack, F32),
            pltpu.VMEM((n,) + pack, F32),
            pltpu.VMEM((n + 1,) + pack, F32),
            pltpu.VMEM(hidden.shape, BF),
            pltpu.VMEM(common.shape, BF),
            pltpu.VMEM(project.shape, BF),
            pltpu.VMEM((2, 2, 2, count, width), BF),
            pltpu.VMEM((total, NST + HD), BF),
            pltpu.VMEM((total, 256), BF),
            pltpu.VMEM((total, 256), BF),
            pltpu.VMEM((total, 128), BF),
            pltpu.VMEM((total, 128), BF),
            pltpu.VMEM((total, 256), BF),
            dma((4,)),
            dma((4, 2, 2, n)),
            dma((2, 2, n)),
            dma((2, 2, n)),
            dma((2, 3)),
            dma((2, 7)),
            dma((2, 7)),
            dma((2, 4)),
            dma((2,)),
            dma((2, 4)),
        ]
        + sum_scratch(count, width),
        compiler_params=pltpu.CompilerParams(
            collective_id=3, has_side_effects=True, vmem_limit_bytes=61 * 1024 * 1024
        ),
        name="last",
    )(rows, gain, grad, little, weight, common, hidden, project, sum_rows)


def start_kernel(
    rows_ref, little_ref, own_ref, blocks_ref, units_ref, cot_ref,
    hidden_ref, all_ref, weight_ref, unit_ref, incoming_ref,
    block, little, hidden_sems, map_sems, kv_sems, cot_sems, local, little_sems, line_sems, across_sems,
):
    x, z, y, c = (lax.axis_index(a) for a in ("x", "z", "y", "c"))
    n = lax.axis_size("z")
    width, count = blocks_ref.shape[3], rows_ref.shape[0]
    own_maps, own_kv = own_ref.at[:, pl.ds(0, NST)], own_ref.at[:, pl.ds(NST, 2 * HD + 128)]
    greet_all()

    def map_cols(x):
        return pl.ds(pl.multiple_of(width + x * NST, 128), NST)

    kv_cols = pl.ds(width + 2 * NST, 2 * HD + 128)
    in_cols = pl.ds(0, width)

    def moves_of(blocks, place, base):
        moves = []
        for i, (dy, dc) in enumerate(((0, 1), (1, 0), (1, 1))):
            where = {"y": (1 - y) if dy else y, "c": (1 - c) if dc else c}
            move = pltpu.make_async_remote_copy(
                src_ref=blocks.at[where["c"], where["y"]],
                dst_ref=place(y, c),
                send_sem=across_sems.at[0, base + i],
                recv_sem=across_sems.at[1, base + i],
                device_id=where,
                device_id_type=pl.DeviceIdType.MESH,
            )
            move.start()
            moves.append(move)
        return moves

    map_line = line_item(
        lambda at: weight_ref.at[at, y, c, :, map_cols(x)], line_sems.at[0], own_maps
    )
    kv_line = line_item(lambda at: weight_ref.at[at, y, c, :, kv_cols], line_sems.at[6], own_kv)
    little_line = line_item(lambda at: little.at[at], line_sems.at[1])
    lines = []
    for i, (dy, dc) in enumerate(((0, 0), (0, 1), (1, 0), (1, 1))):
        yy, cc = (1 - y) if dy else y, (1 - c) if dc else c
        lines.append(
            line_item(
                lambda at, yy=yy, cc=cc: weight_ref.at[at, yy, cc, :, in_cols],
                line_sems.at[2 + i],
                blocks_ref.at[c, y] if i == 0 else None,
            )
        )

    little[z, y, c] = little_ref[...]
    hop = remote(
        little.at[z, y, c], little.at[z, y, c], little_sems.at[0, 0], little_sems.at[1, 0], "c"
    )
    hop.start()
    map_line[0](0)
    kv_line[0](0)
    hop.wait()
    hop = remote(little.at[z, y], little.at[z, y], little_sems.at[0, 1], little_sems.at[1, 1], "y")
    hop.start()
    hop.wait()
    little_line[0](0)
    lines[0][0](0)
    moves = moves_of(blocks_ref, lambda y, c: weight_ref.at[z, y, c, :, in_cols], 0)

    owns = [
        pltpu.make_async_copy(own_maps, weight_ref.at[z, y, c, :, map_cols(x)], local.at[0]),
        pltpu.make_async_copy(own_kv, weight_ref.at[z, y, c, :, kv_cols], local.at[5]),
        pltpu.make_async_copy(
            blocks_ref.at[c, y], weight_ref.at[z, y, c, :, in_cols], local.at[1]
        ),
    ]
    own_unit = pltpu.make_async_copy(units_ref.at[c, y], unit_ref.at[y, c], local.at[2])
    own_cot = pltpu.make_async_copy(cot_ref, incoming_ref.at[y, c, x], local.at[3])
    own_hidden = pltpu.make_async_copy(block, hidden_ref.at[y, c, x], local.at[4])
    for copy in owns + [own_unit, own_cot]:
        copy.start()

    def half_rows(ref, i):
        first = count // 4 // 16 * 16
        return ref.at[pl.ds(i * first, count - first if i else first)]

    cot_steps = gather_regions(
        lambda x, y, c: incoming_ref.at[y, c, x], half_rows, cot_sems, own_cot.wait, cot_ref
    )
    hidden_steps = gather_regions(
        lambda x, y, c: hidden_ref.at[y, c, x], half_rows, hidden_sems, own_hidden.wait, block
    )
    map_steps = gather_regions(
        lambda x, y, c: weight_ref.at[:, y, c, :, map_cols(x)],
        lambda ref, i: ref.at[pl.ds(i * (n // 2), n // 2)],
        map_sems,
        owns[0].wait,
    )

    def kv_copy(i, y, c, axis):
        ref = weight_ref.at[:, y, c, :, kv_cols]
        return remote(ref, ref, kv_sems.at[0, i], kv_sems.at[1, i], axis)

    cot_steps[0]()
    rows = rows_ref[...].astype(F32)
    rows = rows * factor_of(rows)
    for k in range(1, n):
        for send, arrive, finish in (little_line, map_line, kv_line):
            arrive(k - 1)
            if k < n - 1:
                send(k)

    piece = rows.shape[1] // (4 * n)
    gain = jnp.concatenate(
        [
            little[at, yy, cc, 0:1, 0:piece]
            for at in range(n)
            for yy in (0, 1)
            for cc in (0, 1)
        ],
        axis=1,
    )
    block[...] = (rows * gain).astype(BF)
    own_hidden.start()
    hidden_steps[0]()
    owns[1].wait()
    kv_copy(0, y, c, "y").start()
    kv_copy(1, y, c, "c").start()
    map_steps[0]()
    for i in range(3):
        moves[i].wait_recv()
        lines[1 + i][0](0)
    all_ref[...] = little[...]
    cot_steps[1]()

    def more(k):
        if k < n:
            for send, arrive, finish in lines:
                arrive(k - 1)
                if k < n - 1:
                    send(k)

    more(1)
    hidden_steps[1]()
    more(2)
    kv_copy(0, 1 - y, c, "y").wait_recv()
    kv_copy(2, 1 - y, c, "c").start()
    map_steps[1]()
    moves += moves_of(units_ref, lambda y, c: unit_ref.at[y, c], 3)
    for k in range(3, n):
        more(k)
    cot_steps[2]()
    hidden_steps[2]()
    map_steps[2]()
    kv_copy(1, y, 1 - c, "c").wait_recv()
    kv_copy(2, 1 - y, 1 - c, "c").wait_recv()
    kv_copy(0, y, c, "y").wait_send()
    kv_copy(1, y, c, "c").wait_send()
    kv_copy(2, 1 - y, c, "c").wait_send()
    owns[2].wait()
    own_unit.wait()
    for move in moves[3:]:
        move.wait_recv()
    for move in moves:
        move.wait_send()
    for send, arrive, finish in [map_line, kv_line, little_line] + lines:
        finish()


def start_call(rows, little, own, blocks, units, cot):
    n = lax.axis_size("z")
    count, width = rows.shape
    vmem, hbm = pl.BlockSpec(memory_space=pltpu.VMEM), pl.BlockSpec(memory_space=pl.ANY)
    dma = pltpu.SemaphoreType.DMA
    return pl.pallas_call(
        start_kernel,
        in_specs=[vmem, vmem, hbm, hbm, hbm, hbm],
        out_specs=[hbm, vmem, hbm, hbm, hbm],
        out_shape=[
            jax.ShapeDtypeStruct((2, 2, 2, count, width), BF),
            jax.ShapeDtypeStruct((n, 2, 2) + little.shape, F32),
            jax.ShapeDtypeStruct(
                (n, 2, 2, own.shape[0], blocks.shape[3] + own.shape[1] + NST), BF
            ),
            jax.ShapeDtypeStruct(units.shape, BF),
            jax.ShapeDtypeStruct((2, 2, 2, count, width), BF),
        ],
        scratch_shapes=[
            pltpu.VMEM((count, width), BF),
            pltpu.VMEM((n, 2, 2) + little.shape, F32),
            dma((2, 8)),
            dma((2, 8)),
            dma((2, 3)),
            dma((2, 8)),
            dma((6,)),
            dma((2, 2)),
            dma((7, 2, 2, n - 1)),
            dma((2, 6)),
        ],
        compiler_params=pltpu.CompilerParams(
            collective_id=0, has_side_effects=True, vmem_limit_bytes=VMEM
        ),
        name="start",
    )(rows, little, own, blocks, units, cot)


def prepare_kernel(
    query_ref, key_ref, value_ref, mamba_ref, gate_ref, up_ref, own_ref, blocks_ref, units_ref
):
    x, n = lax.axis_index("x"), lax.axis_size("z")
    inner = MH * MP
    wide = inner // PARTS

    def turned(start, width, at, count):
        rows = mamba_ref[pl.ds(pl.multiple_of(start + x * width + at, 128), count), :]
        return rows.astype(F32).T.astype(BF)

    def half(ref, start, width, at, count):
        return ref[:, pl.ds(pl.multiple_of(start + x * width + at, 128), count)]

    own_ref[:, :NST] = turned(2 * inner, NST, 0, NST)
    own_ref[:, NST : NST + HD] = half(key_ref, 0, HD, 0, HD)
    own_ref[:, NST + HD : NST + 2 * HD] = half(value_ref, 0, HD, 0, HD)
    steps = mamba_ref[2 * inner + 2 * NST :, :].astype(F32)
    steps = jnp.where(x == 0, steps[: MH // 2], steps[MH // 2 :])
    rest = jnp.zeros((128 - MH // 2, steps.shape[1]), F32)
    own_ref[:, NST + 2 * HD :] = jnp.concatenate([steps, rest], axis=0).T.astype(BF)
    for c in (0, 1):
        for y in (0, 1):
            j = 2 * c + y
            blocks_ref[c, y, :, :wide] = turned(0, inner // 2, j * wide, wide)
            blocks_ref[c, y, :, wide : 2 * wide] = turned(
                inner, inner // 2, j * wide, wide
            )
            blocks_ref[c, y, :, 2 * wide :] = half(query_ref, 0, 4 * HD, j * HD, HD)
    unit = units_ref.shape[3] // 2 // n
    for at, ref in enumerate((gate_ref, up_ref)):
        for z in range(n):
            for y in (0, 1):
                for c in (0, 1):
                    first = ((z * 2 + y) * 2 + c) * 2 * unit
                    into = pl.ds((at * n + z) * unit, unit)
                    units_ref[c, y, :, into] = half(ref, first, unit, 0, unit)


def prepare(query, key, value, mamba, gate, up):
    rows, wide = query.shape[0], MH * MP // PARTS
    vmem = pl.BlockSpec(memory_space=pltpu.VMEM)
    return pl.pallas_call(
        prepare_kernel,
        in_specs=[vmem] * 6,
        out_specs=[vmem] * 3,
        out_shape=[
            jax.ShapeDtypeStruct((rows, NST + 2 * HD + 128), BF),
            jax.ShapeDtypeStruct((2, 2, rows, 2 * wide + HD), BF),
            jax.ShapeDtypeStruct((2, 2, rows, 2 * gate.shape[1] // PARTS), BF),
        ],
        compiler_params=pltpu.CompilerParams(vmem_limit_bytes=VMEM),
        name="prepare",
    )(query, key, value, mamba.T, gate, up)


def units_kernel(own_ref, across_ref, gate_ref, up_ref):
    x, n = lax.axis_index("x"), lax.axis_size("z")
    unit = own_ref.shape[3] // 2 // n
    for at, ref in enumerate((gate_ref, up_ref)):
        for z in range(n):
            cols = pl.ds((at * n + z) * unit, unit)
            pieces = []
            for y in (0, 1):
                for c in (0, 1):
                    own, other = own_ref[c, y, :, cols], across_ref[c, y, :, cols]
                    pieces += [jnp.where(x == 0, own, other), jnp.where(x == 0, other, own)]
            ref[:, 8 * unit * z : 8 * unit * (z + 1)] = jnp.concatenate(
                [p.astype(F32) for p in pieces], axis=1
            )


def units_call(own, across):
    vmem = pl.BlockSpec(memory_space=pltpu.VMEM)
    shape = jax.ShapeDtypeStruct((own.shape[2], PARTS * own.shape[3] // 2), F32)
    return pl.pallas_call(
        units_kernel,
        in_specs=[vmem] * 2,
        out_specs=[vmem] * 2,
        out_shape=[shape, shape],
        compiler_params=pltpu.CompilerParams(vmem_limit_bytes=VMEM),
        name="units",
    )(own, across)


def finish_kernel(
    got_ref, few_ref, own_ref, across_ref, own_down, across_down,
    query_ref, key_ref, value_ref, mamba_ref, out_ref, attn_ref, down_ref,
):
    x = lax.axis_index("x")
    inner = MH * MP
    wide = inner // PARTS
    steps = []
    for xx in (0, 1):
        total = 0.0
        for c in (0, 1):
            for y in (0, 1):
                j = 4 * xx + 2 * c + y
                block = got_ref[xx, c, y].astype(F32)
                mamba_ref[j * wide : (j + 1) * wide, :] = block[:, :wide].T
                mamba_ref[inner + j * wide : inner + (j + 1) * wide, :] = block[:, wide : 2 * wide].T
                query_ref[:, j * HD : (j + 1) * HD] = block[:, 2 * wide : 2 * wide + HD]
                total = total + few_ref[xx, c, y, :, 128:].astype(F32)
        steps.append(total[:, : MH // 2])
    def pair(first, second, start, width):
        return jnp.concatenate([v[:, start : start + width].astype(F32) for v in (first, second)], axis=1)

    for xx in (0, 1):
        cols = slice(xx * HD, (xx + 1) * HD)
        key_ref[:, cols] = pair(few_ref[xx, 0, 0], few_ref[xx, 0, 1], 0, HD // 2)
        value_ref[:, cols] = pair(few_ref[xx, 1, 0], few_ref[xx, 1, 1], 0, HD // 2)
    for c in (0, 1):
        for y in (0, 1):
            first = 2 * inner + (2 * c + y) * (NST // 2)
            mamba_ref[first : first + NST // 2, :] = pair(
                few_ref[0, c, y], few_ref[1, c, y], HD // 2, NST // 4
            ).T
    rest = jnp.zeros((steps[0].shape[0], 128 - MH), F32)
    mamba_ref[2 * inner + 2 * NST :, :] = jnp.concatenate(steps + [rest], axis=1).T[:MH]

    own, across = own_ref[...], across_ref[...]
    sides = [jnp.where(x == 0, own, across), jnp.where(x == 0, across, own)]
    half, first = own.shape[1], out_ref.shape[0]
    second = first + attn_ref.shape[0]
    units = down_ref.shape[0] // 2
    for xx in (0, 1):
        side = sides[xx].astype(F32)
        cols = slice(xx * half, (xx + 1) * half)
        out_ref[:, cols] = side[:first]
        attn_ref[:, cols] = side[first:second]
        mine = own_down[...].astype(F32), across_down[...].astype(F32)
        down_ref[xx * units : (xx + 1) * units] = jnp.where(x == xx, *mine)


def finish_call(got, few, own, across, own_down, across_down, shapes):
    vmem = pl.BlockSpec(memory_space=pltpu.VMEM)
    return pl.pallas_call(
        finish_kernel,
        in_specs=[vmem] * 6,
        out_specs=[vmem] * 7,
        out_shape=[jax.ShapeDtypeStruct(v, F32) for v in shapes],
        compiler_params=pltpu.CompilerParams(vmem_limit_bytes=VMEM),
        name="finish",
    )(got, few, own, across, own_down, across_down)


def flip(value, *axes):
    count = 2 ** len(axes)
    pairs = [(i, count - 1 - i) for i in range(count)]
    axes = tuple(sorted(axes, key=MESH_AXES.index))
    return lax.ppermute(value, axes, pairs)


def ordered(own, other, axis):
    second = lax.axis_index(axis) == 1
    return jnp.where(second, other, own), jnp.where(second, own, other)


def halves_of(value, axis, dim):
    at = lax.axis_index(axis)
    kept = lax.dynamic_index_in_dim(value, at, dim, keepdims=False)
    return kept, lax.dynamic_index_in_dim(value, 1 - at, dim, keepdims=False).astype(BF)


def part_index():
    return 4 * lax.axis_index("x") + 2 * lax.axis_index("c") + lax.axis_index("y")


def half_columns(weight):
    half = weight.shape[1] // 2
    return lax.dynamic_slice_in_dim(weight, lax.axis_index("x") * half, half, 1)


def exchange_blocks(blocks, high, low):
    h, l = lax.axis_index(high), lax.axis_index(low)
    return [
        lax.dynamic_index_in_dim(blocks, 2 * (h ^ dh) + (l ^ dl), 0, keepdims=False)
        for dh in (0, 1)
        for dl in (0, 1)
    ]


def exchanged(blocks, high, low, late):
    own, for_low, for_high, for_both = blocks
    got = [flip(for_low, low), flip(for_high, high), flip(for_both, high, low)]
    by_low, by_high, by_both = after(got, late)
    near, far = ordered(own, by_low, low), ordered(by_high, by_both, low)
    first, second = ordered(near[0], far[0], high), ordered(near[1], far[1], high)
    return [[first[0], second[0]], [first[1], second[1]]]


def sum_blocks(part):
    rows = part.shape[0] // 4
    y, c = lax.axis_index("y"), lax.axis_index("c")
    return [
        lax.dynamic_slice_in_dim(part, (2 * (y ^ dy) + (c ^ dc)) * rows, rows, 0)
        for dc in (0, 1)
        for dy in (0, 1)
    ]


def whole_rows(weights):
    parts = []
    for w in weights:
        whole = lax.all_gather(w, FSDP, axis=0, tiled=True)
        rows = whole.shape[0] // PARTS
        parts.append(lax.dynamic_slice_in_dim(whole, part_index() * rows, rows, 0))
    return jnp.concatenate(parts)


def joined_rows(got, pieces):
    whole = jnp.stack([jnp.concatenate([got[0][c], got[1][c]], axis=1) for c in (0, 1)])
    outs, at = [], 0
    for count in pieces:
        outs.append(whole[:, at : at + count].reshape(2 * count, -1))
        at += count
    return jnp.concatenate(outs)


def rows_blocks(grad, pieces):
    cols, grad = grad.shape[1] // 2, grad.astype(BF)
    if lax.axis_size("z") != 4:
        parts = []
        for i, count in enumerate(pieces):
            g = grad[sum(pieces[:i]) : sum(pieces[: i + 1])]
            whole = jnp.zeros((count * PARTS, 2 * cols), BF)
            parts.append(
                lax.dynamic_update_slice_in_dim(whole, g, part_index() * g.shape[0], 0)
            )
        return parts
    x, c = lax.axis_index("x"), lax.axis_index("c")
    blocks = []
    for dx in (0, 1):
        for dc in (0, 1):
            block, at = [], 0
            for count in pieces:
                start = (at + (c ^ dc) * (count // 2), (x ^ dx) * cols)
                block.append(lax.dynamic_slice(grad, start, (count // 2, cols)))
                at += count
            blocks.append(jnp.concatenate(block))
    return blocks


def rows_stack(moved):
    if lax.axis_size("z") != 4:
        return moved
    return jnp.stack([moved[0][0], moved[0][1], moved[1][0], moved[1][1]])


def rows_sum(moved):
    if lax.axis_size("z") != 4:
        parts = []
        for whole in moved:
            part = lax.psum_scatter(whole, FSDP, scatter_dimension=0, tiled=True)
            parts.append(half_columns(lax.psum(part, "x")))
        return jnp.concatenate(parts)
    return lax.psum_scatter(moved, "z")


def after(value, earlier):
    return lax.optimization_barrier((value, earlier))[0]


def packed(first, arrays):
    lead = first.shape[0]
    flat = jnp.concatenate([a.reshape(lead, -1) for a in arrays], axis=1)
    flat = jnp.pad(flat, ((0, 0), (0, -(flat.shape[1] + 128) % 1024)))
    first = jnp.pad(first, ((0, 0), (0, 128 - first.shape[1])))
    return jnp.concatenate([first, flat], axis=1).reshape(lead, -1, 128)


def shards(
    tokens,
    cotangent,
    mixer_gain,
    query_weight,
    key_weight,
    value_weight,
    attn_out_weight,
    mamba_in_weight,
    conv_weight,
    conv_bias,
    decay_log,
    step_bias,
    skip_gain,
    mamba_gain,
    mamba_out_weight,
    ffn_gain,
    gate_weight,
    up_weight,
    down_weight,
):
    token_count, model_dim = tokens.shape[1], tokens.shape[2]
    length = 2 * token_count
    inner = MH * MP
    channels = inner + 2 * NST
    part = part_index()
    wide, heads = inner // PARTS, MH // PARTS
    rows = token_count * PARTS
    seqs = rows // length
    fsdp = lax.axis_size("z") * 4

    smalls = [ffn_gain, mamba_gain, conv_bias, conv_weight]
    little = packed(mixer_gain[None].astype(F32), [v[None].astype(F32) for v in smalls])[0]
    count = query_weight.shape[0]
    own, blocks, units = prepare(
        query_weight, key_weight, value_weight, mamba_in_weight, gate_weight, up_weight
    )
    token_rows = tokens.reshape(token_count, model_dim)
    grad_rows = cotangent.reshape(token_count, model_dim)
    hidden, gathered_little, w_in, units, incoming = start_call(
        token_rows, little, own, blocks, units, grad_rows
    )
    hidden = hidden.reshape(rows, model_dim)
    incoming = incoming.reshape(rows, model_dim)
    w_in = w_in.reshape(model_dim, -1)
    fast = lax.axis_size("z") == 4
    out_weights = [mamba_out_weight, attn_out_weight]
    out_pieces = [w.shape[0] for w in out_weights]
    if fast:
        out_blocks = half_columns(jnp.concatenate(out_weights))
        out_blocks = lax.all_gather(out_blocks, "z", axis=0, tiled=False)
        out_blocks = exchange_blocks(out_blocks, "x", "c")
    w_gateup = lax.all_gather(units.reshape(4 * count, -1), "z", axis=0, tiled=True)
    down_half = down_weight.reshape(2, -1, model_dim)
    down_half = lax.dynamic_index_in_dim(down_half, lax.axis_index("x"), 0, keepdims=False)
    ff = gate_weight.shape[1] // PARTS

    gathered_little = gathered_little.reshape(fsdp, -1)
    gain_in = gathered_little[:, : mixer_gain.size].reshape(-1)
    got, at = [], 128
    for s in smalls:
        got.append(gathered_little[:, at : at + s.size].reshape((fsdp,) + s.shape))
        at += s.size
    gain_ffn, gain_mamba, bias_full = (g.reshape(-1) for g in got[:3])
    conv_full = got[3].transpose(1, 0, 2).reshape(4, channels)
    gain_mamba = lax.dynamic_slice_in_dim(gain_mamba, part * wide, wide, 0)

    def own_heads(v):
        return lax.dynamic_slice_in_dim(v.astype(F32), part * heads, heads, 0)

    heads_rows = jnp.stack([own_heads(v) for v in (decay_log, step_bias, skip_gain)])
    heads_rows = jnp.pad(heads_rows, ((0, 5), (0, 2 * MP - heads)))
    params = [
        lax.dynamic_slice_in_dim(conv_full, part * wide, wide, 1),
        lax.dynamic_slice_in_dim(bias_full, part * wide, wide, 0)[None],
        conv_full[:, inner:],
        bias_full[None, inner:],
        heads_rows,
    ]
    tables = rope_tables(length, HD)

    projected = mm(after(hidden, out_blocks) if fast else hidden, w_in)
    scanned, gated, squares, attended = mixer_forward(seqs, length, projected, params, tables)

    if fast:
        w_out = joined_rows(exchanged(out_blocks, "x", "c", squares), out_pieces)
    else:
        w_out = whole_rows(out_weights)
    squares = plane_total(squares.reshape(-1, 128), 4)
    factor = lax.rsqrt(squares / inner + EPSILON).reshape(rows, 1)
    normal = gated * factor
    normed = (normal * gain_mamba).astype(BF)
    mixed = jnp.concatenate([normed, attended], axis=1)
    block = (2, 2, 2, token_count, model_dim)
    mixer_sum = mm(mixed, w_out).astype(BF).reshape(block)
    second, middle, w_down = middle_calls(mixer_sum, token_rows, gain_ffn[None], down_half)
    w_down = w_down.reshape(ff, model_dim)
    second = second.reshape(rows, model_dim)
    gate_up = mm(second, w_gateup)
    gate_act, up_act = gate_up[:, :ff], gate_up[:, ff:]
    sig_g = jax.nn.sigmoid(gate_act)
    active = (gate_act * sig_g * up_act).astype(BF)

    grad_active = across(incoming, w_down)
    grad_gate = grad_active * up_act * sig_g * (1.0 + gate_act * (1.0 - sig_g))
    grad_up = grad_active * gate_act * sig_g
    grad_gateup = jnp.concatenate([grad_gate.astype(BF), grad_up.astype(BF)], axis=1)
    grad_wgateup = outer_product(second, grad_gateup)
    sum_gateup = lax.psum_scatter(grad_wgateup.astype(BF).reshape(-1, 4 * count, 2 * ff), "z")
    grad_second = across(grad_gateup, w_gateup).astype(BF).reshape(block)
    grad_mixer, grad_middle, grad_gain_ffn, grad_down, *results = middle_calls(
        grad_second, middle, gain_ffn[None], w_down, grad_rows, active, incoming
    )
    sum_down = lax.psum_scatter(
        grad_down.reshape(-1, ff // lax.axis_size("z"), model_dim), "z"
    )
    results = [v.reshape(2, 2, token_count, model_dim) for v in results]
    grad_mixer = grad_mixer.reshape(rows, model_dim)
    grad_out = outer_product(mixed, grad_mixer)
    row_blocks = rows_blocks(grad_out, [wide, HD])
    grad_mixed = across(after(grad_mixer, row_blocks), w_out)
    grad_normed = grad_mixed[:, :wide]
    grad_gain_mamba = jnp.sum(grad_normed * normal, axis=0)
    scaled = grad_normed * gain_mamba
    dots = jnp.sum(scaled * normal, axis=-1).reshape(-1, 128)
    results = after(results, dots)
    half = model_dim // 2
    lefts = [halves_of(v[..., :half], "y", 0) for v in results]
    rights = [halves_of(v[..., half:], "x", 1) for v in results]
    left, right = ((a[1].astype(F32) + b[1].astype(F32)).astype(BF) for a, b in (lefts, rights))
    dots = plane_total(after(dots, (left, right)), 5)
    left, right, sum_gateup = after((left, right, sum_gateup), dots)
    gateup_blocks = sum_blocks(sum_gateup)
    row_sums = exchanged(row_blocks, "x", "c", dots) if fast else row_blocks
    row_sums = rows_stack(row_sums)
    down_across = flip(sum_down, "x")
    dots = after(dots, (gateup_blocks, left, right, row_sums, sum_down)).reshape(rows, 1) / inner

    grad_in, gxk, gxb, gmk, gmb, gheads = mixer_backward(
        seqs, length, projected, params, tables, scanned, grad_mixed, gain_mamba[None], factor, dots
    )
    sum_rows = rows_sum(row_sums)
    moved = exchanged(gateup_blocks, "c", "y", grad_in)
    moved = jnp.stack([jnp.stack(g) for g in moved])
    moved_across = flip(moved, "x")
    left, right = after((flip(left, "y"), flip(right, "x")), grad_in)
    lefts = [halves_of(v, "x", 0) for v in (lefts[0][0], lefts[1][0], left)]
    rights = [halves_of(v, "y", 0) for v in (rights[0][0], rights[1][0], right)]

    def three(values, index):
        return sum(v[index].astype(F32) for v in values)

    left, right = three(lefts, 1).astype(BF), three(rights, 1).astype(BF)
    grad_in = after(grad_in, (moved, left, right))
    grad_win = outer_product(hidden, grad_in[:, : 2 * wide + HD]).astype(BF)
    grad_win = grad_win.reshape(-1, 2, 2, count, grad_win.shape[1])
    got_left, got_right = after((flip(left, "x"), flip(right, "y")), grad_win)
    result = jnp.concatenate(
        [three(lefts, 0) + got_left.astype(F32), three(rights, 0) + got_right.astype(F32)], axis=1
    )
    output = (middle + result).astype(BF).reshape(1, token_count, model_dim)
    shard_gate, shard_up = units_call(moved, after(moved_across, grad_win))

    conv_grad = jnp.zeros((4, channels), F32)
    conv_grad = lax.dynamic_update_slice_in_dim(conv_grad, gxk, part * wide, 1)
    conv_grad = conv_grad.at[:, inner:].set(gmk)
    bias_grad = jnp.zeros((channels,), F32)
    bias_grad = lax.dynamic_update_slice_in_dim(bias_grad, gxb[0], part * wide, 0)
    bias_grad = bias_grad.at[inner:].set(gmb[0])
    gain_grad = lax.dynamic_update_slice_in_dim(
        jnp.zeros((inner,), F32), grad_gain_mamba, part * wide, 0
    )
    head_grad = lax.dynamic_update_slice_in_dim(
        jnp.zeros((3, MH), F32), gheads[:3, :heads], part * heads, 1
    )
    scattered = [grad_gain_ffn, gain_grad, bias_grad]
    little = [v.reshape(fsdp, -1) for v in scattered]
    little.append(conv_grad.reshape(4, fsdp, -1).transpose(1, 0, 2).reshape(fsdp, -1))
    little.append(jnp.broadcast_to(head_grad.reshape(1, -1), (fsdp, 3 * MH)))
    little = packed(jnp.zeros((fsdp, count), F32), little)
    little = little.reshape((-1, 2, 2) + little.shape[1:])
    tokens_grad, total, got_in, got_few, rows_across = last_call(
        token_rows, gain_in[None], grad_middle, little, grad_win, after(grad_in, (left, right)),
        hidden, w_in, sum_rows,
    )
    tokens_grad = tokens_grad.reshape(1, token_count, model_dim)
    total = total.reshape(-1)
    got, at = [total[:count]], 128
    for like in (ffn_gain, mamba_gain, conv_bias, conv_weight, head_grad):
        got.append(total[at : at + like.size].reshape(like.shape))
        at += like.size

    weights = [query_weight, key_weight, value_weight, mamba_in_weight.T]
    weights += [mamba_out_weight, attn_out_weight, down_weight]
    (
        shard_query, shard_key, shard_value, shard_mamba_in,
        shard_mamba_out, shard_attn_out, shard_down,
    ) = finish_call(
        got_in, got_few, sum_rows, rows_across, sum_down, down_across, [w.shape for w in weights]
    )

    return (
        output,
        tokens_grad,
        got[0],
        shard_query,
        shard_key,
        shard_value,
        shard_attn_out,
        shard_mamba_in.T,
        got[4],
        got[3],
        got[5][0],
        got[5][1],
        got[5][2],
        got[2],
        shard_mamba_out,
        got[1],
        shard_gate,
        shard_up,
        shard_down,
    )


def solution(mesh):
    fsdp = mesh.shape["fsdp"]
    grid = Mesh(mesh.devices.reshape(2, fsdp // 4, 2, 2), ("x", "z", "y", "c"))
    rows, flat, whole = P(FSDP, None), P(FSDP), P()
    stream = P(FSDP, "x", None)
    weights = (
        flat, rows, rows, rows, rows, rows, P(None, FSDP), flat, whole, whole, whole,
        flat, rows, flat, rows, rows, rows,
    )
    return jax.shard_map(
        shards,
        mesh=grid,
        in_specs=(stream, stream) + weights,
        out_specs=(stream, stream) + weights,
        check_vma=False,
    )
```

```python
import math

import jax
import jax.numpy as jnp
from jax import lax
from jax.experimental import pallas as pl
from jax.experimental.pallas import tpu as pltpu
from jax.sharding import Mesh
from jax.sharding import PartitionSpec as P

HQ = 8
KVH = 2
HD = 128
MH = 48
MP = 64
NST = 256
EPSILON = 1e-05
ROPE_BASE = 100000000000.0
MASKED = -1e30
BF = jnp.bfloat16
F32 = jnp.float32
MESH_AXES = ("x", "z", "y", "c")
FSDP = ("z", "y", "c")
PARTS = 8
VMEM = 48 * 1024 * 1024


def mm(left, right):
    return jnp.dot(left, right, preferred_element_type=F32)


def outer_product(left, right):
    return lax.dot_general(left, right, (((0,), (0,)), ((), ())), preferred_element_type=F32)


def across(left, right):
    return lax.dot_general(left, right, (((1,), (1,)), ((), ())), preferred_element_type=F32)


def rope_tables(length, head_size):
    half_size = head_size // 2
    frequency = jnp.exp(
        jnp.arange(half_size, dtype=F32) * (-2.0 * math.log(ROPE_BASE) / head_size)
    )
    angles = jnp.arange(length, dtype=F32)[:, None] * frequency[None, :]
    cosine, sine = jnp.cos(angles), jnp.sin(angles)
    return [jnp.concatenate(v, axis=1) for v in ([cosine, cosine], [-sine, sine])]


def silu_parts(values):
    sig = 1.0 / (1.0 + jnp.exp(-values))
    return values * sig, sig


def shifted(values, count):
    if count == 0:
        return values
    rows = values.shape[0]
    at = lax.broadcasted_iota(jnp.int32, values.shape, 0)
    kept = (at >= count) if count > 0 else (at < rows + count)
    return jnp.where(kept, pltpu.roll(values, count % rows, 0), 0.0)


def conv_silu(signal, kernel, bias):
    taps = kernel.shape[0]
    total = bias + signal * kernel[taps - 1 : taps]
    for back in range(1, taps):
        total = total + shifted(signal, back) * kernel[taps - 1 - back : taps - back]
    value, sig = silu_parts(total)
    return value, sig * (1.0 + total * (1.0 - sig))


def conv_grads(signal, kernel, grad):
    taps = kernel.shape[0]
    back = grad * kernel[taps - 1 : taps]
    rows = []
    for count in range(taps - 1, 0, -1):
        rows.append(jnp.sum(shifted(signal, count) * grad, axis=0, keepdims=True))
        back = back + shifted(grad, -count) * kernel[taps - 1 - count : taps - count]
    rows.append(jnp.sum(signal * grad, axis=0, keepdims=True))
    return back, jnp.concatenate(rows, axis=0), jnp.sum(grad, axis=0, keepdims=True)


def dot(left, right, dims=((1,), (0,)), precision=None):
    return lax.dot_general(
        left, right, (dims, ((), ())), preferred_element_type=F32, precision=precision
    )


ROWS = ((0,), (0,))
LANES = ((1,), (1,))
PRECISE = lax.Precision.HIGHEST


def step_place():
    return (MH // PARTS) * (2 * lax.axis_index("c") + lax.axis_index("y"))


def scan_parts(x_ref, m_refs, s_ref, xk_ref, xb_ref, mk_ref, mb_ref, h_ref):
    length = x_ref.shape[0]
    xin = x_ref[...].astype(BF).astype(F32)
    maps = jnp.concatenate([ref[...].astype(BF).astype(F32) for ref in m_refs], axis=1)
    xs, xslope = conv_silu(xin, xk_ref[...], xb_ref[...])
    mv, mslope = conv_silu(maps, mk_ref[...], mb_ref[...])
    mv = mv.astype(BF)
    bees, cees = mv[:, :NST], mv[:, NST:]
    raw = pltpu.roll(s_ref[...].astype(BF).astype(F32), 2 * MP - step_place(), 1) + h_ref[1:2]
    dt = jnp.maximum(raw, 0.0) + jnp.log1p(jnp.exp(-jnp.abs(raw)))
    rate = -jnp.exp(h_ref[0:1])
    t = lax.broadcasted_iota(jnp.int32, (length, length), 0)
    s = lax.broadcasted_iota(jnp.int32, (length, length), 1)
    lower = (t >= s).astype(F32)
    cum = dot(lower, dt * rate, precision=PRECISE)
    coupling = dot(cees, bees, LANES)
    return xin, maps, xs, xslope, mslope, bees, cees, raw, dt, rate, lower, cum, coupling


def lane_pair(values, first):
    lane = lax.broadcasted_iota(jnp.int32, (values.shape[0], 2 * MP), 1)
    return jnp.where(lane < MP, values[:, first : first + 1], values[:, first + 1 : first + 2])


def decay_of(cum, cumt, lower, head):
    gap = cum[:, head : head + 1] - cumt[head : head + 1, :]
    return jnp.exp(jnp.where(lower > 0.0, gap, MASKED))


def rotated(ref, cos_ref, sin_ref):
    value = ref[...].astype(BF).astype(F32)
    return (value * cos_ref[...] + pltpu.roll(value, HD // 2, 1) * sin_ref[...]).astype(BF)


def causal_scores(rq, rk):
    length = rq.shape[0]
    t = lax.broadcasted_iota(jnp.int32, (length, length), 0)
    s = lax.broadcasted_iota(jnp.int32, (length, length), 1)
    scores = jnp.where(t >= s, dot(rq, rk, LANES) * HD ** (-0.5), MASKED)
    highest = jnp.max(scores, axis=1, keepdims=True)
    weights = jnp.exp(scores - highest)
    return weights, jnp.sum(weights, axis=1, keepdims=True)


def mixer_kernel(
    x_ref, m0_ref, m1_ref, m2_ref, m3_ref, s_ref, z_ref, q_ref, k_ref, v_ref, xk_ref, xb_ref, mk_ref, mb_ref, h_ref,
    cos_ref, sin_ref, scan_ref, gated_ref, square_ref, att_ref,
):
    xin, maps, xs, xslope, mslope, bees, cees, raw, dt, rate, lower, cum, coupling = scan_parts(
        x_ref, (m0_ref, m1_ref, m2_ref, m3_ref), s_ref, xk_ref, xb_ref, mk_ref, mb_ref, h_ref
    )
    cumt = cum.T
    lane = lax.broadcasted_iota(jnp.int32, (xs.shape[0], 2 * MP), 1)
    squares = jnp.zeros((xs.shape[0], 1), F32)
    for pair in range(xs.shape[1] // (2 * MP)):
        cols = slice(2 * MP * pair, 2 * MP * (pair + 1))
        xp = xs[:, cols]
        xr = (xp * lane_pair(dt, 2 * pair)).astype(BF)
        ys = []
        for head in (2 * pair, 2 * pair + 1):
            mixing = (coupling * decay_of(cum, cumt, lower, head)).astype(BF)
            ys.append(dot(mixing, xr))
        y = jnp.where(lane < MP, ys[0], ys[1]) + lane_pair(h_ref[2:3], 2 * pair) * xp
        y = y.astype(BF)
        scan_ref[:, cols] = y
        gated = y.astype(F32) * silu_parts(z_ref[:, cols])[0]
        gated_ref[:, cols] = gated
        squares = squares + jnp.sum(gated * gated, axis=1, keepdims=True)
    square_ref[...] = squares
    weights, total = causal_scores(
        rotated(q_ref, cos_ref, sin_ref), rotated(k_ref, cos_ref, sin_ref)
    )
    att_ref[...] = dot((weights / total).astype(BF), v_ref[...].astype(BF)).astype(BF)


def mixer_back_kernel(
    x_ref, m0_ref, m1_ref, m2_ref, m3_ref, s_ref, z_ref, q_ref, k_ref, v_ref, xk_ref, xb_ref, mk_ref, mb_ref, h_ref,
    cos_ref, sin_ref, scan_ref, gn_ref, gain_ref, factor_ref, dots_ref, ga_ref,
    gin_ref,
    gxk_ref, gxb_ref, gmk_ref, gmb_ref, gh_ref,
):
    xin, maps, xs, xslope, mslope, bees, cees, raw, dt, rate, lower, cum, coupling = scan_parts(
        x_ref, (m0_ref, m1_ref, m2_ref, m3_ref), s_ref, xk_ref, xb_ref, mk_ref, mb_ref, h_ref
    )
    length, width = xs.shape
    cumt = cum.T
    lane = lax.broadcasted_iota(jnp.int32, (length, 2 * MP), 1)
    factor, dots = factor_ref[...], dots_ref[...]
    gcoup = jnp.zeros((length, length), F32)
    gcum = jnp.zeros((length, 2 * MP), F32)
    gdt = jnp.zeros((length, 2 * MP), F32)
    gskip = jnp.zeros((1, 2 * MP), F32)
    gus = []
    for pair in range(width // (2 * MP)):
        cols = slice(2 * MP * pair, 2 * MP * (pair + 1))
        gate, scanned = z_ref[:, cols], scan_ref[:, cols].astype(F32)
        silu_z, sig_z = silu_parts(gate)
        normal = scanned * silu_z * factor
        ggated = factor * (gn_ref[:, cols] * gain_ref[:, cols] - normal * dots)
        gin_ref[:, cols] = (ggated * scanned * sig_z * (1.0 + gate * (1.0 - sig_z))).astype(BF)
        gy = (ggated * silu_z).astype(BF)
        gyf = gy.astype(F32)
        xp, dtp = xs[:, cols], lane_pair(dt, 2 * pair)
        xr = (xp * dtp).astype(BF)
        ys, gxrs = [], []
        for own, head in enumerate((2 * pair, 2 * pair + 1)):
            mine = (lane < MP) if own == 0 else (lane >= MP)
            decay = decay_of(cum, cumt, lower, head)
            mixing = (coupling * decay).astype(BF)
            ys.append(dot(mixing, xr))
            gxrs.append(dot(mixing, gy, ROWS))
            gcoup = gcoup + dot(jnp.where(mine, gy, jnp.zeros_like(gy)), xr, LANES) * decay
        y = jnp.where(lane < MP, ys[0], ys[1])
        gxr = jnp.where(lane < MP, gxrs[0], gxrs[1])
        flow, drive, direct = gyf * y - xr.astype(F32) * gxr, gxr * xp, gyf * xp
        for own, head in enumerate((2 * pair, 2 * pair + 1)):
            mine = (lane < MP) if own == 0 else (lane >= MP)

            def share(v):
                return jnp.sum(jnp.where(mine, v, 0.0), axis=1, keepdims=True)

            gcum = jnp.where(lane == head, share(flow), gcum)
            gdt = jnp.where(lane == head, share(drive), gdt)
            gskip = jnp.where(
                lane[:1] == head, jnp.sum(share(direct), axis=0, keepdims=True), gskip
            )
        gus.append((gxr * dtp + lane_pair(h_ref[2:3], 2 * pair) * gyf) * xslope[:, cols])
    gu = jnp.concatenate(gus, axis=1)
    gx, gxk, gxb = conv_grads(xin, xk_ref[...], gu)
    gin_ref[:, width : 2 * width] = gx.astype(BF)
    gflow = dot(lower, gcum, ROWS, precision=PRECISE)
    gdt = gdt + gflow * rate
    graw = gdt / (1.0 + jnp.exp(-raw))
    graw = jnp.where(lane < width // MP, graw, 0.0)
    common = 2 * width + HD
    gin_ref[:, common + 2 * NST + 2 * HD :] = pltpu.roll(graw, step_place(), 1).astype(BF)
    gdecay = jnp.sum(gflow * dt, axis=0, keepdims=True) * rate
    gcb = gcoup.astype(BF)
    gmaps = jnp.concatenate([dot(gcb, cees, ROWS), dot(gcb, bees)], axis=1) * mslope
    gm, gmk, gmb = conv_grads(maps, mk_ref[...], gmaps)
    gin_ref[:, common : common + 2 * NST] = gm.astype(BF)
    gh = jnp.concatenate([gdecay, jnp.sum(graw, axis=0, keepdims=True), gskip], axis=0)

    @pl.when(pl.program_id(0) == 0)
    def _():
        for ref in (gxk_ref, gxb_ref, gmk_ref, gmb_ref, gh_ref):
            ref[...] = jnp.zeros_like(ref)

    gxk_ref[...] += gxk
    gxb_ref[...] += gxb
    gmk_ref[...] += gmk
    gmb_ref[...] += gmb
    gh_ref[0:3] += gh

    rq, rk = rotated(q_ref, cos_ref, sin_ref), rotated(k_ref, cos_ref, sin_ref)
    weights, total = causal_scores(rq, rk)
    probs = weights / total
    gatt = ga_ref[...].astype(BF)
    kv = common + 2 * NST
    gin_ref[:, kv + HD : kv + 2 * HD] = dot(probs.astype(BF), gatt, ROWS).astype(BF)
    gp = dot(gatt, v_ref[...].astype(BF), LANES)
    gsc = (probs * (gp - jnp.sum(probs * gp, axis=1, keepdims=True))).astype(BF)
    for at, grad in ((2 * width, dot(gsc, rk)), (kv, dot(gsc, rq, ROWS))):
        grad = grad * HD ** (-0.5)
        back = grad * cos_ref[...] - pltpu.roll(grad, HD // 2, 1) * sin_ref[...]
        gin_ref[:, at : at + HD] = back.astype(BF)


def column_block(length, width, at):
    return pl.BlockSpec((length, width), lambda i: (i, at // width))


def mixer_specs(length, wide):
    maps = 2 * wide + HD
    return (
        [column_block(length, wide, wide)]
        + [column_block(length, NST // 2, maps + at) for at in range(0, 2 * NST, NST // 2)]
        + [
            column_block(length, 2 * MP, maps + 2 * NST + 2 * HD),
            column_block(length, wide, 0),
            column_block(length, HD, 2 * wide),
            column_block(length, HD, maps + 2 * NST),
            column_block(length, HD, maps + 2 * NST + HD),
        ]
    )


def whole_specs(arrays):
    return [pl.BlockSpec(a.shape, lambda i: (0, 0)) for a in arrays]


def mixer_forward(seqs, length, projected, params, tables):
    wide = params[0].shape[1]
    outs = [(wide, BF), (wide, F32), (1, F32), (HD, BF)]
    return pl.pallas_call(
        mixer_kernel,
        grid=(seqs,),
        in_specs=mixer_specs(length, wide) + whole_specs(params + tables),
        out_specs=[column_block(length, w, 0) for w, _ in outs],
        out_shape=[jax.ShapeDtypeStruct((seqs * length, w), d) for w, d in outs],
        compiler_params=pltpu.CompilerParams(vmem_limit_bytes=VMEM),
        name="mixer",
    )(*[projected] * 10, *params, *tables)


def mixer_backward(seqs, length, projected, params, tables, scanned, grad_mixed, gain, factor, dots):
    wide = params[0].shape[1]
    outs = [projected.shape[1]]
    sums = [(4, wide), (1, wide), (4, 2 * NST), (1, 2 * NST), (8, 2 * MP)]
    row_specs = [column_block(length, wide, 0), column_block(length, wide, 0)]
    tail_specs = [column_block(length, 1, 0), column_block(length, 1, 0), column_block(length, HD, wide)]
    return pl.pallas_call(
        mixer_back_kernel,
        grid=(seqs,),
        in_specs=mixer_specs(length, wide) + whole_specs(params + tables)
        + row_specs + whole_specs([gain]) + tail_specs,
        out_specs=[column_block(length, w, 0) for w in outs]
        + [pl.BlockSpec(s, lambda i: (0, 0)) for s in sums],
        out_shape=[jax.ShapeDtypeStruct((seqs * length, w), BF) for w in outs]
        + [jax.ShapeDtypeStruct(s, F32) for s in sums],
        compiler_params=pltpu.CompilerParams(vmem_limit_bytes=VMEM),
        name="mixer_back",
    )(
        *[projected] * 10, *params, *tables, scanned, grad_mixed, gain, factor, dots, grad_mixed,
    )


def remote(src, dst, send, recv, axis):
    other = 1 - lax.axis_index(axis)
    return pltpu.make_async_remote_copy(
        src_ref=src,
        dst_ref=dst,
        send_sem=send,
        recv_sem=recv,
        device_id={axis: other},
        device_id_type=pl.DeviceIdType.MESH,
    )


def greet(axes):
    barrier = pltpu.get_barrier_semaphore()
    for axis in axes:
        other = 1 - lax.axis_index(axis)
        pl.semaphore_signal(
            barrier, inc=1, device_id={axis: other}, device_id_type=pl.DeviceIdType.MESH
        )
    pl.semaphore_wait(barrier, len(axes))


def line_item(region, sems, sources=None):
    z, n = lax.axis_index("z"), lax.axis_size("z")

    def copy(way, k, at, src):
        return pltpu.make_async_remote_copy(
            src_ref=src,
            dst_ref=region(at),
            send_sem=sems.at[0, way, k],
            recv_sem=sems.at[1, way, k],
            device_id={"z": z + 1 - 2 * way},
            device_id_type=pl.DeviceIdType.MESH,
        )

    def send(k):
        src = sources if k == 0 and sources is not None else None

        @pl.when((z + 1 < n) & (z - k >= 0))
        def _():
            copy(0, k, z - k, region(z - k) if src is None else src).start()

        @pl.when((z >= 1) & (z + k < n))
        def _():
            copy(1, k, z + k, region(z + k) if src is None else src).start()

    def arrive(k):
        @pl.when(z - 1 - k >= 0)
        def _():
            copy(0, k, z - 1 - k, region(z - 1 - k)).wait_recv()

        @pl.when(z + 1 + k < n)
        def _():
            copy(1, k, z + 1 + k, region(z + 1 + k)).wait_recv()

    def finish():
        for k in range(n - 1):
            src = sources if k == 0 and sources is not None else None

            @pl.when((z + 1 < n) & (z - k >= 0))
            def _(k=k, src=src):
                copy(0, k, z - k, region(z - k) if src is None else src).wait_send()

            @pl.when((z >= 1) & (z + k < n))
            def _(k=k, src=src):
                copy(1, k, z + k, region(z + k) if src is None else src).wait_send()

    return send, arrive, finish


def gather_regions(region, half, sems, own_ready, own=None):
    x, y, c = (lax.axis_index(a) for a in ("x", "y", "c"))
    sent = []

    def send(i, ref, axis, src=None):
        src = ref if src is None else src
        copy = remote(src, ref, sems.at[0, i], sems.at[1, i], axis)
        copy.start()
        sent.append(copy)

    def got(i, ref, axis):
        remote(ref, ref, sems.at[0, i], sems.at[1, i], axis).wait_recv()

    def begin():
        if own is None:
            own_ready()
        for i, axis in enumerate(("x", "y", "c")):
            send(i, region(x, y, c), axis, own)

    def forward():
        got(0, region(1 - x, y, c), "x")
        send(3, half(region(1 - x, y, c), 0), "y")
        send(4, region(1 - x, y, c), "c")
        got(1, region(x, 1 - y, c), "y")
        send(5, half(region(x, 1 - y, c), 1), "x")
        send(6, region(x, 1 - y, c), "c")

    def end():
        got(3, half(region(1 - x, 1 - y, c), 0), "y")
        got(5, half(region(1 - x, 1 - y, c), 1), "x")
        send(7, region(1 - x, 1 - y, c), "c")
        got(2, region(x, y, 1 - c), "c")
        got(4, region(1 - x, y, 1 - c), "c")
        got(6, region(x, 1 - y, 1 - c), "c")
        got(7, region(1 - x, 1 - y, 1 - c), "c")
        for copy in sent:
            copy.wait_send()
        if own is not None:
            own_ready()

    return begin, forward, end


def greet_all():
    barrier = pltpu.get_barrier_semaphore()
    x, z, y, c = (lax.axis_index(a) for a in ("x", "z", "y", "c"))
    n = lax.axis_size("z")

    def tell(where):
        pl.semaphore_signal(
            barrier, inc=1, device_id=where, device_id_type=pl.DeviceIdType.MESH
        )

    for where in ({"x": 1 - x}, {"y": 1 - y}, {"c": 1 - c}, {"y": 1 - y, "c": 1 - c}):
        tell(where)

    @pl.when(z >= 1)
    def _():
        tell({"z": z - 1})

    @pl.when(z + 1 < n)
    def _():
        tell({"z": z + 1})

    pl.semaphore_wait(barrier, 4 + jnp.minimum(z, 1) + jnp.minimum(n - 1 - z, 1))


def sum_scratch(count, width):
    half = width // 2
    return [
        pltpu.VMEM((2, 2, 2, count, half), BF),
        pltpu.VMEM((2, 2, count, half), BF),
        pltpu.VMEM((2, 2, count, half), BF),
        pltpu.VMEM((2, count, half), BF),
        pltpu.VMEM((2, count, half), BF),
        pltpu.SemaphoreType.DMA((2, 6)),
    ]


def reduce_plane(part, scratch, firsts=("y", "x")):
    core, wide_in, wide_out, thin_in, thin_out, sems = scratch
    half = part.shape[4] // 2
    x, y, c = (lax.axis_index(a) for a in ("x", "y", "c"))
    seconds = ["x" if axis == "y" else "y" for axis in firsts]
    cols = [slice(0, half), slice(half, 2 * half)]

    def chip(i, yy, xx):
        return part[yy, c, xx, :, cols[i]].astype(F32) + core[i, yy, xx].astype(F32)

    def kept(i, index):
        mine = chip(i, y, index) if firsts[i] == "y" else chip(i, index, x)
        return mine + wide_in[i, index].astype(F32)

    copies = [
        remote(part.at[:, 1 - c, :, :, cols[i]], core.at[i], sems.at[0, i], sems.at[1, i], "c")
        for i in (0, 1)
    ]
    wides = [
        remote(wide_out.at[i], wide_in.at[i], sems.at[0, 2 + i], sems.at[1, 2 + i], firsts[i])
        for i in (0, 1)
    ]
    thins = [
        remote(thin_out.at[i], thin_in.at[i], sems.at[0, 4 + i], sems.at[1, 4 + i], seconds[i])
        for i in (0, 1)
    ]

    def begin():
        for copy in copies:
            copy.start()

    def wide(which=(0, 1)):
        for i in which:
            copies[i].wait()
            for k in (0, 1):
                away = chip(i, 1 - y, k) if firsts[i] == "y" else chip(i, k, 1 - x)
                wide_out[i, k] = away.astype(BF)
            wides[i].start()

    def thin():
        for i in (0, 1):
            wides[i].wait()
            thin_out[i] = kept(i, 1 - x if firsts[i] == "y" else 1 - y).astype(BF)
            thins[i].start()

    def end():
        outs = []
        for i in (0, 1):
            thins[i].wait()
            outs.append(kept(i, x if firsts[i] == "y" else y) + thin_in[i].astype(F32))
        return jnp.concatenate(outs, axis=1)

    return begin, wide, thin, end


def gathered(block, out, sems, local):
    x, y, c = (lax.axis_index(a) for a in ("x", "y", "c"))
    half = block.shape[0] // 2
    own = pltpu.make_async_copy(block, out.at[y, c, x], local)
    own.start()
    steps = gather_regions(
        lambda x, y, c: out.at[y, c, x],
        lambda ref, i: ref.at[pl.ds(i * half, half)],
        sems,
        own.wait,
        block,
    )
    return steps


def factor_of(values):
    return lax.rsqrt(jnp.mean(values * values, axis=1, keepdims=True) + EPSILON)


def norm_back_parts(values, scaling, grad):
    factor = factor_of(values)
    normal = values * factor
    scaled = grad * scaling
    inner = jnp.mean(scaled * normal, axis=1, keepdims=True)
    return factor * (scaled - normal * inner), jnp.sum(grad * normal, axis=0, keepdims=True)


def fill_part(part, left_ref, right_ref, dims, cc):
    count = part.shape[3]
    for yy in (0, 1):
        for xx in (0, 1):
            first = pl.multiple_of((4 * yy + 2 * cc + xx) * count, 16)
            product = dot(left_ref[pl.ds(first, count), :], right_ref[...], dims)
            part[yy, cc, xx] = product.astype(BF)


def middle_kernel(
    left_ref, right_ref, rows_ref, gain_ref, down_ref, out_ref, middle_ref, whole_ref,
    block, sems, local, down_sems, part, *scratch,
):
    z, n, c = lax.axis_index("z"), lax.axis_size("z"), lax.axis_index("c")
    greet_all()
    begin, wide, thin, end = reduce_plane(part, scratch)
    own = pltpu.make_async_copy(down_ref, whole_ref.at[z], local.at[1])
    own.start()
    send, arrive, finish = line_item(lambda at: whole_ref.at[at], down_sems, down_ref)
    send(0)
    fill_part(part, left_ref, right_ref, ((1,), (0,)), 1 - c)
    begin()
    fill_part(part, left_ref, right_ref, ((1,), (0,)), c)

    def more(k):
        if k < n:
            arrive(k - 1)
        if k < n - 1:
            send(k)

    wide()
    more(1)
    thin()
    middle = rows_ref[...].astype(F32) + end()
    middle_ref[...] = middle
    block[...] = (middle * factor_of(middle) * gain_ref[...]).astype(BF)
    first, *steps = gathered(block, out_ref, sems, local.at[0])
    first()
    more(2)
    for step in steps:
        step()
    for k in range(3, n):
        more(k)
    own.wait()
    finish()


def middle_back_kernel(
    left_ref, right_ref, rows_ref, gain_ref, cot_ref, active_ref, down_ref, incoming_ref,
    out_ref, grad_ref, gain_grad_ref, down_grad_ref, kept_ref, got_ref,
    block, sems, local, part, incoming, down_grad, result, more_sems, *scratch,
):
    c = lax.axis_index("c")
    greet(("x", "y", "c"))
    load = pltpu.make_async_copy(incoming_ref, incoming, more_sems.at[0])
    load.start()
    begin, wide, thin, end = reduce_plane(part, scratch)
    fill_part(part, left_ref, right_ref, LANES, 1 - c)
    begin()
    fill_part(part, left_ref, right_ref, LANES, c)
    wide()
    copies = []
    count = active_ref.shape[0] // 4
    for side in (1, 0):
        for yy in (0, 1):
            rows = pl.multiple_of((2 * yy + ((1 - c) if side else c)) * count, 16)
            into = result.at[side, yy]
            into[...] = dot(active_ref[pl.ds(rows, count), :], down_ref[...]).astype(BF)
            if side:
                copy = remote(into, got_ref.at[yy], more_sems.at[1 + yy], more_sems.at[9 + yy], "c")
            else:
                copy = pltpu.make_async_copy(into, kept_ref.at[yy], more_sems.at[3 + yy])
            copy.start()
            copies.append(copy)
    load.wait()
    units = active_ref.shape[1] // 4
    for i in range(4):
        rows = pl.ds(i * units, units)
        down_grad[rows, :] = dot(active_ref[:, rows], incoming[...], ROWS).astype(BF)
        copies.append(
            pltpu.make_async_copy(down_grad.at[rows], down_grad_ref.at[rows], more_sems.at[5 + i])
        )
        copies[4 + i].start()
    thin()
    grad, gain_grad_ref[...] = norm_back_parts(rows_ref[...], gain_ref[...], end())
    grad = grad + cot_ref[...].astype(F32)
    grad_ref[...] = grad
    block[...] = grad.astype(BF)
    for step in gathered(block, out_ref, sems, local.at[0]):
        step()
    for copy in copies:
        copy.wait()


def middle_calls(left, right, rows, gain, down, cot=None, active=None, incoming=None):
    n = lax.axis_size("z")
    count, width = rows.shape
    vmem, hbm = pl.BlockSpec(memory_space=pltpu.VMEM), pl.BlockSpec(memory_space=pl.ANY)
    dma = pltpu.SemaphoreType.DMA
    out = [jax.ShapeDtypeStruct((2, 2, 2, count, width), BF), jax.ShapeDtypeStruct((count, width), F32)]
    scratch = [pltpu.VMEM((count, width), BF), dma((2, 8)), dma((2,))]
    if cot is None:
        inputs, specs = [left, right, rows, gain, down], [vmem] * 4 + [hbm]
        out += [jax.ShapeDtypeStruct((n,) + down.shape, BF)]
        out_specs = [hbm, vmem, hbm]
        scratch += [dma((2, 2, n)), pltpu.VMEM((2, 2, 2, count, width), BF)]
    else:
        inputs = [left, right, rows, gain, cot, active, down, incoming]
        specs = [vmem] * 7 + [hbm]
        scratch += [pltpu.VMEM((2, 2, 2, count, width), BF)]
        half = (2, incoming.shape[0] // 4, width)
        out += [jax.ShapeDtypeStruct((1, width), F32), jax.ShapeDtypeStruct(down.shape, BF)]
        out += [jax.ShapeDtypeStruct(half, BF)] * 2
        out_specs = [hbm, vmem, vmem, hbm, hbm, hbm]
        scratch += [pltpu.VMEM(v, BF) for v in (incoming.shape, down.shape, (2,) + half)]
        scratch += [dma((11,))]
    return pl.pallas_call(
        middle_kernel if cot is None else middle_back_kernel,
        in_specs=specs,
        out_specs=out_specs,
        out_shape=out,
        scratch_shapes=scratch + sum_scratch(count, width),
        compiler_params=pltpu.CompilerParams(
            collective_id=1 if cot is None else 2, has_side_effects=True, vmem_limit_bytes=60 * 1024 * 1024
        ),
        name="middle" if cot is None else "middle_back",
    )(*inputs)


def total_kernel(value_ref, out_ref, got, sems):
    greet(("c", "y", "x"))
    out_ref[...] = value_ref[...]
    for i, axis in enumerate(("c", "y", "x")):
        hop = remote(out_ref, got.at[i], sems.at[0, i], sems.at[1, i], axis)
        hop.start()
        hop.wait()
        out_ref[...] = out_ref[...] + got[i]


def plane_total(value, identity):
    vmem = pl.BlockSpec(memory_space=pltpu.VMEM)
    return pl.pallas_call(
        total_kernel,
        in_specs=[vmem],
        out_specs=vmem,
        out_shape=jax.ShapeDtypeStruct(value.shape, F32),
        scratch_shapes=[pltpu.VMEM((3,) + value.shape, F32), pltpu.SemaphoreType.DMA((2, 3))],
        compiler_params=pltpu.CompilerParams(collective_id=identity, has_side_effects=True),
        name="total",
    )(value)


def line_sum(own, inbox, sems):
    z, n = lax.axis_index("z"), lax.axis_size("z")

    def copy(way, k):
        d = k if way else n - 1 - k
        slot = jnp.where(d == z - 1, n, d) if way else d
        return pltpu.make_async_remote_copy(
            src_ref=own(d),
            dst_ref=inbox(slot),
            send_sem=sems.at[0, way, k],
            recv_sem=sems.at[1, way, k],
            device_id={"z": z + 1 - 2 * way},
            device_id_type=pl.DeviceIdType.MESH,
        )

    def add(way, k, d, slot):
        pltpu.make_async_remote_copy(
            src_ref=own(d),
            dst_ref=inbox(slot),
            send_sem=sems.at[0, way, k],
            recv_sem=sems.at[1, way, k],
            device_id={"z": z},
            device_id_type=pl.DeviceIdType.MESH,
        ).wait_recv()
        held = own(d)
        held[...] = (held[...].astype(F32) + inbox(slot)[...].astype(F32)).astype(held.dtype)

    def kick(k):
        @pl.when(z == 0)
        def _():
            copy(0, k).start()

        @pl.when(z == n - 1)
        def _():
            copy(1, k).start()

    def pass_on(way, k):
        d = k if way else n - 1 - k

        @pl.when((z > 0) & (z < n - 1) & (d < z if way else d > z))
        def _():
            add(way, k, d, d)
            copy(way, k).start()

    def end():
        @pl.when(z > 0)
        def _():
            add(0, n - 1 - z, z, z)

        @pl.when(z < n - 1)
        def _():
            add(1, z, z, n)

    def finish():
        for k in range(n - 1):
            for way in (0, 1):
                d = k if way else n - 1 - k

                @pl.when(d < z if way else d > z)
                def _(way=way):
                    copy(way, k).wait_send()

    return kick, pass_on, end, finish


def column_sums(grad_ref, grad, first, boxes, sems):
    by_c, for_y, by_y, for_x, by_x, out = boxes
    x, y, c = (lax.axis_index(a) for a in ("x", "y", "c"))

    def cols(side):
        maps = pl.ds(pl.multiple_of(first + side * NST, 128), NST)
        kv = pl.ds(pl.multiple_of(first + 2 * NST + side * HD, 128), HD)
        return (maps, pl.ds(0, NST)), (kv, pl.ds(NST, HD))

    def own():
        return jnp.concatenate([grad[:, src] for src, _ in cols(c)], axis=1).astype(F32)

    across = [
        remote(grad_ref.at[:, src], by_c.at[:, dst], sems.at[0, i], sems.at[1, i], "c")
        for i, (src, dst) in enumerate(cols(1 - c))
    ]
    over_y = remote(for_y, by_y, sems.at[0, 2], sems.at[1, 2], "y")
    over_x = remote(for_x, by_x, sems.at[0, 3], sems.at[1, 3], "x")

    def begin():
        for copy in across:
            copy.start()

    def halves(value, side):
        maps, kv = value[:, :NST], value[:, NST:]
        maps = jnp.where(side == 0, maps[:, : NST // 2], maps[:, NST // 2 :])
        kv = jnp.where(side == 0, kv[:, : HD // 2], kv[:, HD // 2 :])
        return maps, kv

    def second():
        for copy in across:
            copy.wait()
        maps, kv = halves(own() + by_c[...].astype(F32), 1 - y)
        for_y[...] = jnp.concatenate([maps, kv, kv], axis=1).astype(BF)
        over_y.start()

    def summed():
        got = by_y[...].astype(F32)
        maps, kv = halves(own() + by_c[...].astype(F32), y)
        return maps + got[:, : NST // 2], kv + got[:, NST // 2 : NST // 2 + HD // 2]

    def third():
        over_y.wait()
        maps, kv = summed()
        away = jnp.where(x == 0, maps[:, NST // 4 :], maps[:, : NST // 4])
        for_x[...] = jnp.concatenate([away, away], axis=1).astype(BF)
        over_x.start()

    def end():
        over_x.wait()
        maps, kv = summed()
        maps = jnp.where(x == 0, maps[:, : NST // 4], maps[:, NST // 4 :])
        maps = maps + by_x[...].astype(F32)[:, : NST // 4]
        out[:, 0:128] = jnp.concatenate([kv, maps], axis=1).astype(BF)
        out[:, 128:256] = grad[:, first + 2 * NST + 2 * HD :]

    return begin, second, third, end


def hand_out(held, swap, got, places, sems, own_sems):
    x, y, c = (lax.axis_index(a) for a in ("x", "y", "c"))
    moves, kept = [], []

    def give(i):
        yy, cc = places[i]
        if i == 3:
            swap[c, y] = held(yy, cc)[...]
            return
        move = pltpu.make_async_remote_copy(
            src_ref=held(yy, cc),
            dst_ref=swap.at[c, y],
            send_sem=sems.at[0, i],
            recv_sem=sems.at[1, i],
            device_id={"y": yy, "c": cc},
            device_id_type=pl.DeviceIdType.MESH,
        )
        move.start()
        moves.append(move)

    def forward(i):
        yy, cc = places[i]
        if i < 3:
            moves[i].wait_recv()
        keep = pltpu.make_async_copy(swap.at[cc, yy], got.at[x, cc, yy], own_sems.at[i])
        move = remote(swap.at[cc, yy], got.at[x, cc, yy], sems.at[0, 3 + i], sems.at[1, 3 + i], "x")
        for copy in (keep, move):
            copy.start()
            kept.append(copy)

    def finish():
        for copy in kept:
            copy.wait()
        for move in moves:
            move.wait_send()

    return give, forward, finish


def last_kernel(
    rows_ref, gain_ref, grad_ref, little_ref, weight_ref, common_ref, hidden_ref, project_ref,
    rows_in, out_ref, little_out, got_ref, few_ref, rows_out,
    held, inbox, few, few_box, swap, few_swap, little, little_in, little_c, little_y, little_box,
    hidden, common, project, part, col_c, col_y_out, col_y_in, col_x_out, col_x_in, slices,
    local, weight_sems, few_sems, little_sems, hop_sems, swap_sems, few_swap_sems, own_sems,
    cross_sems, col_sems, *scratch,
):
    x, z, y, c = (lax.axis_index(a) for a in ("x", "z", "y", "c"))
    n = lax.axis_size("z")
    greet_all()
    pairs = ((weight_ref, held), (common_ref, common), (project_ref, project), (hidden_ref, hidden))
    loads = [pltpu.make_async_copy(*pair, local.at[i]) for i, pair in enumerate(pairs)]
    for load in loads:
        load.start()
    begin, wide, thin, end = reduce_plane(part, scratch)
    boxes = (col_c, col_y_out, col_y_in, col_x_out, col_x_in, slices)
    col_begin, col_second, col_third, col_end = column_sums(
        common_ref, common, common_ref.shape[1] // 2, boxes, col_sems
    )
    col_begin()
    count = rows_ref.shape[0]

    def product_of(cc, yy):
        for xx in (0, 1):
            first = pl.multiple_of((4 * yy + 2 * cc + xx) * count, 16)
            block = common[pl.ds(first, count), :]
            part[yy, cc, xx] = dot(block, project[...], LANES).astype(BF)

    order = ((1, 1), (1, 0), (0, 1), (0, 0))
    sums, places = [], []
    for i, (dy, dc) in enumerate(order):
        yy, cc = (1 - y) if dy else y, (1 - c) if dc else c
        places.append((yy, cc))
        sums.append(
            line_sum(
                lambda d, yy=yy, cc=cc: held.at[d, yy, cc],
                lambda d, yy=yy, cc=cc: inbox.at[d, yy, cc],
                weight_sems.at[i],
            )
        )
    few_sum = line_sum(lambda d: few.at[d], lambda d: few_box.at[d], few_sems)
    cross = remote(rows_in, rows_out, cross_sems.at[0], cross_sems.at[1], "x")
    loads[0].wait()
    for k in range(n - 1):
        for item in sums:
            item[0](k)

    def pass_on(item, k, far):
        @pl.when(z < n // 2)
        def _():
            item[1](far, k)

        @pl.when(z >= n // 2)
        def _():
            item[1](1 - far, k)

    loads[1].wait()
    col_second()
    loads[2].wait()
    product_of(1 - c, 0)
    pass_on(sums[0], 0, 0)
    product_of(1 - c, 1)
    begin()
    pass_on(sums[1], 0, 0)
    pass_on(sums[0], 0, 1)
    product_of(c, 0)
    pass_on(sums[2], 0, 0)
    pass_on(sums[1], 0, 1)
    product_of(c, 1)
    pass_on(sums[3], 0, 0)
    pass_on(sums[2], 0, 1)
    wide()
    pass_on(sums[3], 0, 1)
    col_third()
    if n > 2:
        for i in (0, 1, 2, 3):
            pass_on(sums[i], 1, 0)
    col_end()
    loads[3].wait()
    product = dot(slices[...], hidden[...], ROWS).T.astype(BF)
    piece = product.shape[0] // (4 * n)
    for at in range(n):
        for yy in (0, 1):
            for cc in (0, 1):
                first = (4 * at + 2 * yy + cc) * piece
                few[at, yy, cc] = product[first : first + piece]
    for k in range(n - 1):
        few_sum[0](k)
    for k in range(1, n - 1):
        for item in sums:
            for far in (0, 1):
                if k > 1 or far == 1:
                    pass_on(item, k, far)
    thin()
    cross.start()

    rows = rows_ref[...].astype(F32)
    grad, gain_grad = norm_back_parts(rows, gain_ref[...], end())
    out_ref[...] = grad + grad_ref[...]
    little[...] = little_ref[...]
    for at in range(n):
        for yy in (0, 1):
            for cc in (0, 1):
                first = (4 * at + 2 * yy + cc) * piece
                little[at, yy, cc, 0:1, 0:piece] = gain_grad[:, first : first + piece]
    hop = remote(little, little_in, hop_sems.at[0, 0], hop_sems.at[1, 0], "x")
    hop.start()

    give, forward, finish = hand_out(
        lambda yy, cc: held.at[z, yy, cc], swap, got_ref, places, swap_sems, own_sems.at[0]
    )
    few_give, few_forward, few_finish = hand_out(
        lambda yy, cc: few.at[z, yy, cc], few_swap, few_ref, places, few_swap_sems, own_sems.at[1]
    )
    for i in (0, 1):
        sums[i][2]()
        give(i)
    hop.wait()
    little[...] = little[...] + little_in[...]
    hop = remote(little.at[:, :, 1 - c], little_c, hop_sems.at[0, 1], hop_sems.at[1, 1], "c")
    hop.start()
    forward(0)
    sums[2][2]()
    give(2)
    forward(1)
    hop.wait()
    for yy in (0, 1):
        little_c[:, yy] = little_c[:, yy] + little[:, yy, c]
    hop = remote(little_c.at[:, 1 - y], little_y, hop_sems.at[0, 2], hop_sems.at[1, 2], "y")
    hop.start()
    sums[3][2]()
    give(3)
    forward(2)
    forward(3)
    pass_on(few_sum, 0, 0)
    hop.wait()
    little_y[...] = little_y[...] + little_c[:, y]
    little_sum = line_sum(lambda d: little_y.at[d], lambda d: little_box.at[d], little_sems)
    for k in range(n - 1):
        little_sum[0](k)
    for k in range(n - 1):
        for far in (0, 1):
            if k > 0 or far == 1:
                pass_on(few_sum, k, far)
    few_sum[2]()
    for i in range(4):
        few_give(i)
    for k in range(n - 1):
        for way in (0, 1):
            little_sum[1](way, k)
    little_sum[2]()
    little_out[...] = little_y[z]
    for i in range(4):
        few_forward(i)
    cross.wait()
    finish()
    few_finish()
    for item in sums + [few_sum, little_sum]:
        item[3]()


def last_call(rows, gain, grad, little, weight, common, hidden, project, sum_rows):
    n = lax.axis_size("z")
    count, width = rows.shape
    total, piece = hidden.shape[0], weight.shape[3]
    block, small, pack = weight.shape[3:], (piece, 256), little.shape[3:]
    vmem, hbm = pl.BlockSpec(memory_space=pltpu.VMEM), pl.BlockSpec(memory_space=pl.ANY)
    dma = pltpu.SemaphoreType.DMA
    return pl.pallas_call(
        last_kernel,
        in_specs=[vmem] * 4 + [hbm] * 5,
        out_specs=[vmem, vmem, hbm, hbm, hbm],
        out_shape=[
            jax.ShapeDtypeStruct((count, width), F32),
            jax.ShapeDtypeStruct(pack, F32),
            jax.ShapeDtypeStruct((2, 2, 2) + block, BF),
            jax.ShapeDtypeStruct((2, 2, 2) + small, BF),
            jax.ShapeDtypeStruct(sum_rows.shape, BF),
        ],
        scratch_shapes=[
            pltpu.VMEM((n, 2, 2) + block, BF),
            pltpu.VMEM((n + 1, 2, 2) + block, BF),
            pltpu.VMEM((n, 2, 2) + small, BF),
            pltpu.VMEM((n + 1, 2, 2) + small, BF),
            pltpu.VMEM((2, 2) + block, BF),
            pltpu.VMEM((2, 2) + small, BF),
            pltpu.VMEM((n, 2, 2) + pack, F32),
            pltpu.VMEM((n, 2, 2) + pack, F32),
            pltpu.VMEM((n, 2) + pack, F32),
            pltpu.VMEM((n,) + pack, F32),
            pltpu.VMEM((n + 1,) + pack, F32),
            pltpu.VMEM(hidden.shape, BF),
            pltpu.VMEM(common.shape, BF),
            pltpu.VMEM(project.shape, BF),
            pltpu.VMEM((2, 2, 2, count, width), BF),
            pltpu.VMEM((total, NST + HD), BF),
            pltpu.VMEM((total, 256), BF),
            pltpu.VMEM((total, 256), BF),
            pltpu.VMEM((total, 128), BF),
            pltpu.VMEM((total, 128), BF),
            pltpu.VMEM((total, 256), BF),
            dma((4,)),
            dma((4, 2, 2, n)),
            dma((2, 2, n)),
            dma((2, 2, n)),
            dma((2, 3)),
            dma((2, 7)),
            dma((2, 7)),
            dma((2, 4)),
            dma((2,)),
            dma((2, 4)),
        ]
        + sum_scratch(count, width),
        compiler_params=pltpu.CompilerParams(
            collective_id=3, has_side_effects=True, vmem_limit_bytes=61 * 1024 * 1024
        ),
        name="last",
    )(rows, gain, grad, little, weight, common, hidden, project, sum_rows)


def start_kernel(
    rows_ref, little_ref, own_ref, blocks_ref, units_ref, cot_ref,
    hidden_ref, all_ref, weight_ref, unit_ref, incoming_ref,
    block, little, hidden_sems, map_sems, kv_sems, cot_sems, local, little_sems, line_sems, across_sems,
):
    x, z, y, c = (lax.axis_index(a) for a in ("x", "z", "y", "c"))
    n = lax.axis_size("z")
    width, count = blocks_ref.shape[3], rows_ref.shape[0]
    own_maps, own_kv = own_ref.at[:, pl.ds(0, NST)], own_ref.at[:, pl.ds(NST, 2 * HD + 128)]
    greet_all()

    def map_cols(x):
        return pl.ds(pl.multiple_of(width + x * NST, 128), NST)

    kv_cols = pl.ds(width + 2 * NST, 2 * HD + 128)
    in_cols = pl.ds(0, width)

    def moves_of(blocks, place, base):
        moves = []
        for i, (dy, dc) in enumerate(((0, 1), (1, 0), (1, 1))):
            where = {"y": (1 - y) if dy else y, "c": (1 - c) if dc else c}
            move = pltpu.make_async_remote_copy(
                src_ref=blocks.at[where["c"], where["y"]],
                dst_ref=place(y, c),
                send_sem=across_sems.at[0, base + i],
                recv_sem=across_sems.at[1, base + i],
                device_id=where,
                device_id_type=pl.DeviceIdType.MESH,
            )
            move.start()
            moves.append(move)
        return moves

    map_line = line_item(
        lambda at: weight_ref.at[at, y, c, :, map_cols(x)], line_sems.at[0], own_maps
    )
    kv_line = line_item(lambda at: weight_ref.at[at, y, c, :, kv_cols], line_sems.at[6], own_kv)
    little_line = line_item(lambda at: little.at[at], line_sems.at[1])
    lines = []
    for i, (dy, dc) in enumerate(((0, 0), (0, 1), (1, 0), (1, 1))):
        yy, cc = (1 - y) if dy else y, (1 - c) if dc else c
        lines.append(
            line_item(
                lambda at, yy=yy, cc=cc: weight_ref.at[at, yy, cc, :, in_cols],
                line_sems.at[2 + i],
                blocks_ref.at[c, y] if i == 0 else None,
            )
        )

    little[z, y, c] = little_ref[...]
    hop = remote(
        little.at[z, y, c], little.at[z, y, c], little_sems.at[0, 0], little_sems.at[1, 0], "c"
    )
    hop.start()
    map_line[0](0)
    kv_line[0](0)
    hop.wait()
    hop = remote(little.at[z, y], little.at[z, y], little_sems.at[0, 1], little_sems.at[1, 1], "y")
    hop.start()
    hop.wait()
    little_line[0](0)
    lines[0][0](0)
    moves = moves_of(blocks_ref, lambda y, c: weight_ref.at[z, y, c, :, in_cols], 0)

    owns = [
        pltpu.make_async_copy(own_maps, weight_ref.at[z, y, c, :, map_cols(x)], local.at[0]),
        pltpu.make_async_copy(own_kv, weight_ref.at[z, y, c, :, kv_cols], local.at[5]),
        pltpu.make_async_copy(
            blocks_ref.at[c, y], weight_ref.at[z, y, c, :, in_cols], local.at[1]
        ),
    ]
    own_unit = pltpu.make_async_copy(units_ref.at[c, y], unit_ref.at[y, c], local.at[2])
    own_cot = pltpu.make_async_copy(cot_ref, incoming_ref.at[y, c, x], local.at[3])
    own_hidden = pltpu.make_async_copy(block, hidden_ref.at[y, c, x], local.at[4])
    for copy in owns + [own_unit, own_cot]:
        copy.start()

    def half_rows(ref, i):
        first = count // 4 // 16 * 16
        return ref.at[pl.ds(i * first, count - first if i else first)]

    cot_steps = gather_regions(
        lambda x, y, c: incoming_ref.at[y, c, x], half_rows, cot_sems, own_cot.wait, cot_ref
    )
    hidden_steps = gather_regions(
        lambda x, y, c: hidden_ref.at[y, c, x], half_rows, hidden_sems, own_hidden.wait, block
    )
    map_steps = gather_regions(
        lambda x, y, c: weight_ref.at[:, y, c, :, map_cols(x)],
        lambda ref, i: ref.at[pl.ds(i * (n // 2), n // 2)],
        map_sems,
        owns[0].wait,
    )

    def kv_copy(i, y, c, axis):
        ref = weight_ref.at[:, y, c, :, kv_cols]
        return remote(ref, ref, kv_sems.at[0, i], kv_sems.at[1, i], axis)

    cot_steps[0]()
    rows = rows_ref[...].astype(F32)
    rows = rows * factor_of(rows)
    for k in range(1, n):
        for send, arrive, finish in (little_line, map_line, kv_line):
            arrive(k - 1)
            if k < n - 1:
                send(k)

    piece = rows.shape[1] // (4 * n)
    gain = jnp.concatenate(
        [
            little[at, yy, cc, 0:1, 0:piece]
            for at in range(n)
            for yy in (0, 1)
            for cc in (0, 1)
        ],
        axis=1,
    )
    block[...] = (rows * gain).astype(BF)
    own_hidden.start()
    hidden_steps[0]()
    owns[1].wait()
    kv_copy(0, y, c, "y").start()
    kv_copy(1, y, c, "c").start()
    map_steps[0]()
    for i in range(3):
        moves[i].wait_recv()
        lines[1 + i][0](0)
    all_ref[...] = little[...]
    cot_steps[1]()

    def more(k):
        if k < n:
            for send, arrive, finish in lines:
                arrive(k - 1)
                if k < n - 1:
                    send(k)

    more(1)
    hidden_steps[1]()
    more(2)
    kv_copy(0, 1 - y, c, "y").wait_recv()
    kv_copy(2, 1 - y, c, "c").start()
    map_steps[1]()
    moves += moves_of(units_ref, lambda y, c: unit_ref.at[y, c], 3)
    for k in range(3, n):
        more(k)
    cot_steps[2]()
    hidden_steps[2]()
    map_steps[2]()
    kv_copy(1, y, 1 - c, "c").wait_recv()
    kv_copy(2, 1 - y, 1 - c, "c").wait_recv()
    kv_copy(0, y, c, "y").wait_send()
    kv_copy(1, y, c, "c").wait_send()
    kv_copy(2, 1 - y, c, "c").wait_send()
    owns[2].wait()
    own_unit.wait()
    for move in moves[3:]:
        move.wait_recv()
    for move in moves:
        move.wait_send()
    for send, arrive, finish in [map_line, kv_line, little_line] + lines:
        finish()


def start_call(rows, little, own, blocks, units, cot):
    n = lax.axis_size("z")
    count, width = rows.shape
    vmem, hbm = pl.BlockSpec(memory_space=pltpu.VMEM), pl.BlockSpec(memory_space=pl.ANY)
    dma = pltpu.SemaphoreType.DMA
    return pl.pallas_call(
        start_kernel,
        in_specs=[vmem, vmem, hbm, hbm, hbm, hbm],
        out_specs=[hbm, vmem, hbm, hbm, hbm],
        out_shape=[
            jax.ShapeDtypeStruct((2, 2, 2, count, width), BF),
            jax.ShapeDtypeStruct((n, 2, 2) + little.shape, F32),
            jax.ShapeDtypeStruct(
                (n, 2, 2, own.shape[0], blocks.shape[3] + own.shape[1] + NST), BF
            ),
            jax.ShapeDtypeStruct(units.shape, BF),
            jax.ShapeDtypeStruct((2, 2, 2, count, width), BF),
        ],
        scratch_shapes=[
            pltpu.VMEM((count, width), BF),
            pltpu.VMEM((n, 2, 2) + little.shape, F32),
            dma((2, 8)),
            dma((2, 8)),
            dma((2, 3)),
            dma((2, 8)),
            dma((6,)),
            dma((2, 2)),
            dma((7, 2, 2, n - 1)),
            dma((2, 6)),
        ],
        compiler_params=pltpu.CompilerParams(
            collective_id=0, has_side_effects=True, vmem_limit_bytes=VMEM
        ),
        name="start",
    )(rows, little, own, blocks, units, cot)


def prepare_kernel(
    query_ref, key_ref, value_ref, mamba_ref, gate_ref, up_ref, own_ref, blocks_ref, units_ref
):
    x, n = lax.axis_index("x"), lax.axis_size("z")
    inner = MH * MP
    wide = inner // PARTS

    def turned(start, width, at, count):
        rows = mamba_ref[pl.ds(pl.multiple_of(start + x * width + at, 128), count), :]
        return rows.astype(F32).T.astype(BF)

    def half(ref, start, width, at, count):
        return ref[:, pl.ds(pl.multiple_of(start + x * width + at, 128), count)]

    own_ref[:, :NST] = turned(2 * inner, NST, 0, NST)
    own_ref[:, NST : NST + HD] = half(key_ref, 0, HD, 0, HD)
    own_ref[:, NST + HD : NST + 2 * HD] = half(value_ref, 0, HD, 0, HD)
    steps = mamba_ref[2 * inner + 2 * NST :, :].astype(F32)
    steps = jnp.where(x == 0, steps[: MH // 2], steps[MH // 2 :])
    rest = jnp.zeros((128 - MH // 2, steps.shape[1]), F32)
    own_ref[:, NST + 2 * HD :] = jnp.concatenate([steps, rest], axis=0).T.astype(BF)
    for c in (0, 1):
        for y in (0, 1):
            j = 2 * c + y
            blocks_ref[c, y, :, :wide] = turned(0, inner // 2, j * wide, wide)
            blocks_ref[c, y, :, wide : 2 * wide] = turned(
                inner, inner // 2, j * wide, wide
            )
            blocks_ref[c, y, :, 2 * wide :] = half(query_ref, 0, 4 * HD, j * HD, HD)
    unit = units_ref.shape[3] // 2 // n
    for at, ref in enumerate((gate_ref, up_ref)):
        for z in range(n):
            for y in (0, 1):
                for c in (0, 1):
                    first = ((z * 2 + y) * 2 + c) * 2 * unit
                    into = pl.ds((at * n + z) * unit, unit)
                    units_ref[c, y, :, into] = half(ref, first, unit, 0, unit)


def prepare(query, key, value, mamba, gate, up):
    rows, wide = query.shape[0], MH * MP // PARTS
    vmem = pl.BlockSpec(memory_space=pltpu.VMEM)
    return pl.pallas_call(
        prepare_kernel,
        in_specs=[vmem] * 6,
        out_specs=[vmem] * 3,
        out_shape=[
            jax.ShapeDtypeStruct((rows, NST + 2 * HD + 128), BF),
            jax.ShapeDtypeStruct((2, 2, rows, 2 * wide + HD), BF),
            jax.ShapeDtypeStruct((2, 2, rows, 2 * gate.shape[1] // PARTS), BF),
        ],
        compiler_params=pltpu.CompilerParams(vmem_limit_bytes=VMEM),
        name="prepare",
    )(query, key, value, mamba.T, gate, up)


def units_kernel(own_ref, across_ref, gate_ref, up_ref):
    x, n = lax.axis_index("x"), lax.axis_size("z")
    unit = own_ref.shape[3] // 2 // n
    for at, ref in enumerate((gate_ref, up_ref)):
        for z in range(n):
            cols = pl.ds((at * n + z) * unit, unit)
            pieces = []
            for y in (0, 1):
                for c in (0, 1):
                    own, other = own_ref[c, y, :, cols], across_ref[c, y, :, cols]
                    pieces += [jnp.where(x == 0, own, other), jnp.where(x == 0, other, own)]
            ref[:, 8 * unit * z : 8 * unit * (z + 1)] = jnp.concatenate(
                [p.astype(F32) for p in pieces], axis=1
            )


def units_call(own, across):
    vmem = pl.BlockSpec(memory_space=pltpu.VMEM)
    shape = jax.ShapeDtypeStruct((own.shape[2], PARTS * own.shape[3] // 2), F32)
    return pl.pallas_call(
        units_kernel,
        in_specs=[vmem] * 2,
        out_specs=[vmem] * 2,
        out_shape=[shape, shape],
        compiler_params=pltpu.CompilerParams(vmem_limit_bytes=VMEM),
        name="units",
    )(own, across)


def finish_kernel(
    got_ref, few_ref, own_ref, across_ref, own_down, across_down,
    query_ref, key_ref, value_ref, mamba_ref, out_ref, attn_ref, down_ref,
):
    x = lax.axis_index("x")
    inner = MH * MP
    wide = inner // PARTS
    steps = []
    for xx in (0, 1):
        total = 0.0
        for c in (0, 1):
            for y in (0, 1):
                j = 4 * xx + 2 * c + y
                block = got_ref[xx, c, y].astype(F32)
                mamba_ref[j * wide : (j + 1) * wide, :] = block[:, :wide].T
                mamba_ref[inner + j * wide : inner + (j + 1) * wide, :] = block[:, wide : 2 * wide].T
                query_ref[:, j * HD : (j + 1) * HD] = block[:, 2 * wide : 2 * wide + HD]
                total = total + few_ref[xx, c, y, :, 128:].astype(F32)
        steps.append(total[:, : MH // 2])
    def pair(first, second, start, width):
        return jnp.concatenate([v[:, start : start + width].astype(F32) for v in (first, second)], axis=1)

    for xx in (0, 1):
        cols = slice(xx * HD, (xx + 1) * HD)
        key_ref[:, cols] = pair(few_ref[xx, 0, 0], few_ref[xx, 0, 1], 0, HD // 2)
        value_ref[:, cols] = pair(few_ref[xx, 1, 0], few_ref[xx, 1, 1], 0, HD // 2)
    for c in (0, 1):
        for y in (0, 1):
            first = 2 * inner + (2 * c + y) * (NST // 2)
            mamba_ref[first : first + NST // 2, :] = pair(
                few_ref[0, c, y], few_ref[1, c, y], HD // 2, NST // 4
            ).T
    rest = jnp.zeros((steps[0].shape[0], 128 - MH), F32)
    mamba_ref[2 * inner + 2 * NST :, :] = jnp.concatenate(steps + [rest], axis=1).T[:MH]

    own, across = own_ref[...], across_ref[...]
    sides = [jnp.where(x == 0, own, across), jnp.where(x == 0, across, own)]
    half, first = own.shape[1], out_ref.shape[0]
    second = first + attn_ref.shape[0]
    units = down_ref.shape[0] // 2
    for xx in (0, 1):
        side = sides[xx].astype(F32)
        cols = slice(xx * half, (xx + 1) * half)
        out_ref[:, cols] = side[:first]
        attn_ref[:, cols] = side[first:second]
        mine = own_down[...].astype(F32), across_down[...].astype(F32)
        down_ref[xx * units : (xx + 1) * units] = jnp.where(x == xx, *mine)


def finish_call(got, few, own, across, own_down, across_down, shapes):
    vmem = pl.BlockSpec(memory_space=pltpu.VMEM)
    return pl.pallas_call(
        finish_kernel,
        in_specs=[vmem] * 6,
        out_specs=[vmem] * 7,
        out_shape=[jax.ShapeDtypeStruct(v, F32) for v in shapes],
        compiler_params=pltpu.CompilerParams(vmem_limit_bytes=VMEM),
        name="finish",
    )(got, few, own, across, own_down, across_down)


def flip(value, *axes):
    count = 2 ** len(axes)
    pairs = [(i, count - 1 - i) for i in range(count)]
    axes = tuple(sorted(axes, key=MESH_AXES.index))
    return lax.ppermute(value, axes, pairs)


def ordered(own, other, axis):
    second = lax.axis_index(axis) == 1
    return jnp.where(second, other, own), jnp.where(second, own, other)


def halves_of(value, axis, dim):
    at = lax.axis_index(axis)
    kept = lax.dynamic_index_in_dim(value, at, dim, keepdims=False)
    return kept, lax.dynamic_index_in_dim(value, 1 - at, dim, keepdims=False).astype(BF)


def part_index():
    return 4 * lax.axis_index("x") + 2 * lax.axis_index("c") + lax.axis_index("y")


def half_columns(weight):
    half = weight.shape[1] // 2
    return lax.dynamic_slice_in_dim(weight, lax.axis_index("x") * half, half, 1)


def exchange_blocks(blocks, high, low):
    h, l = lax.axis_index(high), lax.axis_index(low)
    return [
        lax.dynamic_index_in_dim(blocks, 2 * (h ^ dh) + (l ^ dl), 0, keepdims=False)
        for dh in (0, 1)
        for dl in (0, 1)
    ]


def exchanged(blocks, high, low, late):
    own, for_low, for_high, for_both = blocks
    got = [flip(for_low, low), flip(for_high, high), flip(for_both, high, low)]
    by_low, by_high, by_both = after(got, late)
    near, far = ordered(own, by_low, low), ordered(by_high, by_both, low)
    first, second = ordered(near[0], far[0], high), ordered(near[1], far[1], high)
    return [[first[0], second[0]], [first[1], second[1]]]


def sum_blocks(part):
    rows = part.shape[0] // 4
    y, c = lax.axis_index("y"), lax.axis_index("c")
    return [
        lax.dynamic_slice_in_dim(part, (2 * (y ^ dy) + (c ^ dc)) * rows, rows, 0)
        for dc in (0, 1)
        for dy in (0, 1)
    ]


def whole_rows(weights):
    parts = []
    for w in weights:
        whole = lax.all_gather(w, FSDP, axis=0, tiled=True)
        rows = whole.shape[0] // PARTS
        parts.append(lax.dynamic_slice_in_dim(whole, part_index() * rows, rows, 0))
    return jnp.concatenate(parts)


def joined_rows(got, pieces):
    whole = jnp.stack([jnp.concatenate([got[0][c], got[1][c]], axis=1) for c in (0, 1)])
    outs, at = [], 0
    for count in pieces:
        outs.append(whole[:, at : at + count].reshape(2 * count, -1))
        at += count
    return jnp.concatenate(outs)


def rows_blocks(grad, pieces):
    cols, grad = grad.shape[1] // 2, grad.astype(BF)
    if lax.axis_size("z") != 4:
        parts = []
        for i, count in enumerate(pieces):
            g = grad[sum(pieces[:i]) : sum(pieces[: i + 1])]
            whole = jnp.zeros((count * PARTS, 2 * cols), BF)
            parts.append(
                lax.dynamic_update_slice_in_dim(whole, g, part_index() * g.shape[0], 0)
            )
        return parts
    x, c = lax.axis_index("x"), lax.axis_index("c")
    blocks = []
    for dx in (0, 1):
        for dc in (0, 1):
            block, at = [], 0
            for count in pieces:
                start = (at + (c ^ dc) * (count // 2), (x ^ dx) * cols)
                block.append(lax.dynamic_slice(grad, start, (count // 2, cols)))
                at += count
            blocks.append(jnp.concatenate(block))
    return blocks


def rows_stack(moved):
    if lax.axis_size("z") != 4:
        return moved
    return jnp.stack([moved[0][0], moved[0][1], moved[1][0], moved[1][1]])


def rows_sum(moved):
    if lax.axis_size("z") != 4:
        parts = []
        for whole in moved:
            part = lax.psum_scatter(whole, FSDP, scatter_dimension=0, tiled=True)
            parts.append(half_columns(lax.psum(part, "x")))
        return jnp.concatenate(parts)
    return lax.psum_scatter(moved, "z")


def after(value, earlier):
    return lax.optimization_barrier((value, earlier))[0]


def packed(first, arrays):
    lead = first.shape[0]
    flat = jnp.concatenate([a.reshape(lead, -1) for a in arrays], axis=1)
    flat = jnp.pad(flat, ((0, 0), (0, -(flat.shape[1] + 128) % 1024)))
    first = jnp.pad(first, ((0, 0), (0, 128 - first.shape[1])))
    return jnp.concatenate([first, flat], axis=1).reshape(lead, -1, 128)


def shards(
    tokens,
    cotangent,
    mixer_gain,
    query_weight,
    key_weight,
    value_weight,
    attn_out_weight,
    mamba_in_weight,
    conv_weight,
    conv_bias,
    decay_log,
    step_bias,
    skip_gain,
    mamba_gain,
    mamba_out_weight,
    ffn_gain,
    gate_weight,
    up_weight,
    down_weight,
):
    token_count, model_dim = tokens.shape[1], tokens.shape[2]
    length = 2 * token_count
    inner = MH * MP
    channels = inner + 2 * NST
    part = part_index()
    wide, heads = inner // PARTS, MH // PARTS
    rows = token_count * PARTS
    seqs = rows // length
    fsdp = lax.axis_size("z") * 4

    smalls = [ffn_gain, mamba_gain, conv_bias, conv_weight]
    little = packed(mixer_gain[None].astype(F32), [v[None].astype(F32) for v in smalls])[0]
    count = query_weight.shape[0]
    own, blocks, units = prepare(
        query_weight, key_weight, value_weight, mamba_in_weight, gate_weight, up_weight
    )
    token_rows = tokens.reshape(token_count, model_dim)
    grad_rows = cotangent.reshape(token_count, model_dim)
    hidden, gathered_little, w_in, units, incoming = start_call(
        token_rows, little, own, blocks, units, grad_rows
    )
    hidden = hidden.reshape(rows, model_dim)
    incoming = incoming.reshape(rows, model_dim)
    w_in = w_in.reshape(model_dim, -1)
    fast = lax.axis_size("z") == 4
    out_weights = [mamba_out_weight, attn_out_weight]
    out_pieces = [w.shape[0] for w in out_weights]
    if fast:
        out_blocks = half_columns(jnp.concatenate(out_weights))
        out_blocks = lax.all_gather(out_blocks, "z", axis=0, tiled=False)
        out_blocks = exchange_blocks(out_blocks, "x", "c")
    w_gateup = lax.all_gather(units.reshape(4 * count, -1), "z", axis=0, tiled=True)
    down_half = down_weight.reshape(2, -1, model_dim)
    down_half = lax.dynamic_index_in_dim(down_half, lax.axis_index("x"), 0, keepdims=False)
    ff = gate_weight.shape[1] // PARTS

    gathered_little = gathered_little.reshape(fsdp, -1)
    gain_in = gathered_little[:, : mixer_gain.size].reshape(-1)
    got, at = [], 128
    for s in smalls:
        got.append(gathered_little[:, at : at + s.size].reshape((fsdp,) + s.shape))
        at += s.size
    gain_ffn, gain_mamba, bias_full = (g.reshape(-1) for g in got[:3])
    conv_full = got[3].transpose(1, 0, 2).reshape(4, channels)
    gain_mamba = lax.dynamic_slice_in_dim(gain_mamba, part * wide, wide, 0)

    def own_heads(v):
        return lax.dynamic_slice_in_dim(v.astype(F32), part * heads, heads, 0)

    heads_rows = jnp.stack([own_heads(v) for v in (decay_log, step_bias, skip_gain)])
    heads_rows = jnp.pad(heads_rows, ((0, 5), (0, 2 * MP - heads)))
    params = [
        lax.dynamic_slice_in_dim(conv_full, part * wide, wide, 1),
        lax.dynamic_slice_in_dim(bias_full, part * wide, wide, 0)[None],
        conv_full[:, inner:],
        bias_full[None, inner:],
        heads_rows,
    ]
    tables = rope_tables(length, HD)

    projected = mm(after(hidden, out_blocks) if fast else hidden, w_in)
    scanned, gated, squares, attended = mixer_forward(seqs, length, projected, params, tables)

    if fast:
        w_out = joined_rows(exchanged(out_blocks, "x", "c", squares), out_pieces)
    else:
        w_out = whole_rows(out_weights)
    squares = plane_total(squares.reshape(-1, 128), 4)
    factor = lax.rsqrt(squares / inner + EPSILON).reshape(rows, 1)
    normal = gated * factor
    normed = (normal * gain_mamba).astype(BF)
    mixed = jnp.concatenate([normed, attended], axis=1)
    block = (2, 2, 2, token_count, model_dim)
    second, middle, w_down = middle_calls(mixed, w_out, token_rows, gain_ffn[None], down_half)
    w_down = w_down.reshape(ff, model_dim)
    second = second.reshape(rows, model_dim)
    gate_up = mm(second, w_gateup)
    gate_act, up_act = gate_up[:, :ff], gate_up[:, ff:]
    sig_g = jax.nn.sigmoid(gate_act)
    active = (gate_act * sig_g * up_act).astype(BF)

    grad_active = across(incoming, w_down)
    grad_gate = grad_active * up_act * sig_g * (1.0 + gate_act * (1.0 - sig_g))
    grad_up = grad_active * gate_act * sig_g
    grad_gateup = jnp.concatenate([grad_gate.astype(BF), grad_up.astype(BF)], axis=1)
    grad_wgateup = outer_product(second, grad_gateup)
    sum_gateup = lax.psum_scatter(grad_wgateup.astype(BF).reshape(-1, 4 * count, 2 * ff), "z")
    grad_mixer, grad_middle, grad_gain_ffn, grad_down, *results = middle_calls(
        grad_gateup, w_gateup, middle, gain_ffn[None], w_down, grad_rows, active, incoming
    )
    sum_down = lax.psum_scatter(
        grad_down.reshape(-1, ff // lax.axis_size("z"), model_dim), "z"
    )
    results = [v.reshape(2, 2, token_count, model_dim) for v in results]
    grad_mixer = grad_mixer.reshape(rows, model_dim)
    grad_out = outer_product(mixed, grad_mixer)
    row_blocks = rows_blocks(grad_out, [wide, HD])
    grad_mixed = across(after(grad_mixer, row_blocks), w_out)
    grad_normed = grad_mixed[:, :wide]
    grad_gain_mamba = jnp.sum(grad_normed * normal, axis=0)
    scaled = grad_normed * gain_mamba
    dots = jnp.sum(scaled * normal, axis=-1).reshape(-1, 128)
    results = after(results, dots)
    half = model_dim // 2
    lefts = [halves_of(v[..., :half], "y", 0) for v in results]
    rights = [halves_of(v[..., half:], "x", 1) for v in results]
    left, right = ((a[1].astype(F32) + b[1].astype(F32)).astype(BF) for a, b in (lefts, rights))
    dots = plane_total(after(dots, (left, right)), 5)
    left, right, sum_gateup = after((left, right, sum_gateup), dots)
    gateup_blocks = sum_blocks(sum_gateup)
    row_sums = exchanged(row_blocks, "x", "c", dots) if fast else row_blocks
    row_sums = rows_stack(row_sums)
    down_across = flip(sum_down, "x")
    dots = after(dots, (gateup_blocks, left, right, row_sums, sum_down)).reshape(rows, 1) / inner

    grad_in, gxk, gxb, gmk, gmb, gheads = mixer_backward(
        seqs, length, projected, params, tables, scanned, grad_mixed, gain_mamba[None], factor, dots
    )
    sum_rows = rows_sum(row_sums)
    moved = exchanged(gateup_blocks, "c", "y", grad_in)
    moved = jnp.stack([jnp.stack(g) for g in moved])
    moved_across = flip(moved, "x")
    left, right = after((flip(left, "y"), flip(right, "x")), grad_in)
    lefts = [halves_of(v, "x", 0) for v in (lefts[0][0], lefts[1][0], left)]
    rights = [halves_of(v, "y", 0) for v in (rights[0][0], rights[1][0], right)]

    def three(values, index):
        return sum(v[index].astype(F32) for v in values)

    left, right = three(lefts, 1).astype(BF), three(rights, 1).astype(BF)
    grad_in = after(grad_in, (moved, left, right))
    grad_win = outer_product(hidden, grad_in[:, : 2 * wide + HD]).astype(BF)
    grad_win = grad_win.reshape(-1, 2, 2, count, grad_win.shape[1])
    got_left, got_right = after((flip(left, "x"), flip(right, "y")), grad_win)
    result = jnp.concatenate(
        [three(lefts, 0) + got_left.astype(F32), three(rights, 0) + got_right.astype(F32)], axis=1
    )
    output = (middle + result).astype(BF).reshape(1, token_count, model_dim)
    shard_gate, shard_up = units_call(moved, after(moved_across, grad_win))

    conv_grad = jnp.zeros((4, channels), F32)
    conv_grad = lax.dynamic_update_slice_in_dim(conv_grad, gxk, part * wide, 1)
    conv_grad = conv_grad.at[:, inner:].set(gmk)
    bias_grad = jnp.zeros((channels,), F32)
    bias_grad = lax.dynamic_update_slice_in_dim(bias_grad, gxb[0], part * wide, 0)
    bias_grad = bias_grad.at[inner:].set(gmb[0])
    gain_grad = lax.dynamic_update_slice_in_dim(
        jnp.zeros((inner,), F32), grad_gain_mamba, part * wide, 0
    )
    head_grad = lax.dynamic_update_slice_in_dim(
        jnp.zeros((3, MH), F32), gheads[:3, :heads], part * heads, 1
    )
    scattered = [grad_gain_ffn, gain_grad, bias_grad]
    little = [v.reshape(fsdp, -1) for v in scattered]
    little.append(conv_grad.reshape(4, fsdp, -1).transpose(1, 0, 2).reshape(fsdp, -1))
    little.append(jnp.broadcast_to(head_grad.reshape(1, -1), (fsdp, 3 * MH)))
    little = packed(jnp.zeros((fsdp, count), F32), little)
    little = little.reshape((-1, 2, 2) + little.shape[1:])
    tokens_grad, total, got_in, got_few, rows_across = last_call(
        token_rows, gain_in[None], grad_middle, little, grad_win, after(grad_in, (left, right)),
        hidden, w_in, sum_rows,
    )
    tokens_grad = tokens_grad.reshape(1, token_count, model_dim)
    total = total.reshape(-1)
    got, at = [total[:count]], 128
    for like in (ffn_gain, mamba_gain, conv_bias, conv_weight, head_grad):
        got.append(total[at : at + like.size].reshape(like.shape))
        at += like.size

    weights = [query_weight, key_weight, value_weight, mamba_in_weight.T]
    weights += [mamba_out_weight, attn_out_weight, down_weight]
    (
        shard_query, shard_key, shard_value, shard_mamba_in,
        shard_mamba_out, shard_attn_out, shard_down,
    ) = finish_call(
        got_in, got_few, sum_rows, rows_across, sum_down, down_across, [w.shape for w in weights]
    )

    return (
        output,
        tokens_grad,
        got[0],
        shard_query,
        shard_key,
        shard_value,
        shard_attn_out,
        shard_mamba_in.T,
        got[4],
        got[3],
        got[5][0],
        got[5][1],
        got[5][2],
        got[2],
        shard_mamba_out,
        got[1],
        shard_gate,
        shard_up,
        shard_down,
    )


def solution(mesh):
    fsdp = mesh.shape["fsdp"]
    grid = Mesh(mesh.devices.reshape(2, fsdp // 4, 2, 2), ("x", "z", "y", "c"))
    rows, flat, whole = P(FSDP, None), P(FSDP), P()
    stream = P(FSDP, "x", None)
    weights = (
        flat, rows, rows, rows, rows, rows, P(None, FSDP), flat, whole, whole, whole,
        flat, rows, flat, rows, rows, rows,
    )
    return jax.shard_map(
        shards,
        mesh=grid,
        in_specs=(stream, stream) + weights,
        out_specs=(stream, stream) + weights,
        check_vma=False,
    )
```
